32 devices in a mesh: wide: 8 (over z, y), narrow: 4 (over x, core).
Axes of the slice: x: 2, y: 2, z: 4, core: 2. Of those that a mesh axis runs over, the one named last changes fastest.
Arguments:
- tokens: bfloat16 [16, 256, 2048], P('wide', 'narrow'), may hold values from -6 to 6
- caption: bfloat16 [16, 128, 4096], P('wide', None, 'narrow'), may hold values from -6 to 6
- token_mask: int32 [16, 256], P('wide', 'narrow'), may hold values 0 or 1
- cotangent: bfloat16 [16, 256, 2048], P('wide', 'narrow'), may hold values from -6 to 6
- gain_self: bfloat16 [2048], replicated, may hold values from 0.5 to 1.5
- gain_cross: bfloat16 [2048], replicated, may hold values from 0.5 to 1.5
- gain_feed: bfloat16 [2048], replicated, may hold values from 0.5 to 1.5
- text_proj: bfloat16 [4096, 2048], P('narrow'), may hold values from -0.09375 to 0.09375
- query_self: bfloat16 [2048, 2048], P(None, 'narrow'), may hold values from -0.25 to 0.25
- key_self: bfloat16 [2048, 2048], P(None, 'narrow'), may hold values from -0.125 to 0.125
- value_self: bfloat16 [2048, 2048], P(None, 'narrow'), may hold values from -0.125 to 0.125
- out_self: bfloat16 [2048, 2048], P('narrow'), may hold values from -0.625 to 0.625
- query_cross: bfloat16 [2048, 2048], P(None, 'narrow'), may hold values from -0.25 to 0.25
- key_cross: bfloat16 [2048, 2048], P(None, 'narrow'), may hold values from -0.125 to 0.125
- value_cross: bfloat16 [2048, 2048], P(None, 'narrow'), may hold values from -0.125 to 0.125
- out_cross: bfloat16 [2048, 2048], P('narrow'), may hold values from -0.625 to 0.625
- up_proj: bfloat16 [2048, 8192], P(None, 'narrow'), may hold values from -0.125 to 0.125
- down_proj: bfloat16 [8192, 2048], P('narrow'), may hold values from -0.09375 to 0.09375
Outputs:
- layer_out: bfloat16 [16, 256, 2048], P('wide', 'narrow')
- grad_tokens: bfloat16 [16, 256, 2048], P('wide', 'narrow')
- grad_caption: bfloat16 [16, 128, 4096], P('wide', None, 'narrow')
- grad_gain_self: float32 [2048], replicated
- grad_gain_cross: float32 [2048], replicated
- grad_gain_feed: float32 [2048], replicated
- grad_text: float32 [4096, 2048], P('narrow', 'wide')
- grad_query_self: float32 [2048, 2048], P('wide', 'narrow')
- grad_key_self: float32 [2048, 2048], P('wide', 'narrow')
- grad_value_self: float32 [2048, 2048], P('wide', 'narrow')
- grad_out_self: float32 [2048, 2048], P('narrow', 'wide')
- grad_query_cross: float32 [2048, 2048], P('wide', 'narrow')
- grad_key_cross: float32 [2048, 2048], P('wide', 'narrow')
- grad_value_cross: float32 [2048, 2048], P('wide', 'narrow')
- grad_out_cross: float32 [2048, 2048], P('narrow', 'wide')
- grad_up: float32 [2048, 8192], P('wide', 'narrow')
- grad_down: float32 [8192, 2048], P('narrow', 'wide')
The draws below stay inside these ranges and needn't reach their ends.
All inputs are finite; a program needn't handle non-finite values. No bound on the sum of `token_mask` on one device may be relied on, other than what follows from the above.
Results may differ from the reference program's by a relative error of at most 0.03.
The reference program's roundings to bfloat16 on the way count: a program that leaves them out, or rounds other values in their place, can miss the bound.
Values may be sent and summed in bfloat16 or wider, within the bound.
A program may use at most 640 MiB of HBM per device.

```python
import math
import jax
import jax.numpy as jnp
from jax import lax

D = 2048
HEAD = 128
HEADS = 16
FF = 8192
TDIM = 4096
IMG_LEN = 256
TXT = 128
INNER = 2048
IMAGES = 16


def place_ends(values, rng, smallest, largest):
    longest = values.shape.index(max(values.shape))
    spots = []
    for shift in (0, 1):
        where = [jax.random.randint(jax.random.fold_in(rng, axis), (), 0, length) for axis, length in enumerate(values.shape)]
        where[longest] = (where[longest] + shift) % values.shape[longest]
        spots.append(tuple(where))
    return values.at[spots[0]].set(smallest).at[spots[1]].set(largest)


def raised(entries, stream_key, source, target, shards_of, factor):
    def block_of(dim):
        return (jnp.arange(entries.shape[dim]) // (entries.shape[dim] // shards_of)).reshape((-1,) + (1,) * (entries.ndim - 1 - dim))

    near = jax.random.permutation(stream_key, shards_of)[block_of(target)]
    second = (block_of(target) + shards_of // 2) % shards_of
    return jnp.where((block_of(source) == near) | (block_of(source) == second), factor * entries, entries)


def block_scale(own_key, extent, cuts, low, high):
    def one(position, blocks):
        steps = jax.random.uniform(jax.random.fold_in(jax.random.fold_in(own_key, 6), position), (blocks,), jnp.float32, low / len(cuts), high / len(cuts))
        return jnp.repeat(jnp.exp(steps), extent[position] // blocks).reshape((-1,) + (1,) * (len(extent) - position - 1))

    factor_of = one(*cuts[0])
    for cut in cuts[1:]:
        factor_of = factor_of * one(*cut)
    return factor_of


def noise(own_key, dims, spread, limit, pieces=(), kind=jnp.bfloat16):
    values = spread * jax.random.normal(own_key, dims, jnp.float32)
    if pieces:
        values = values * block_scale(own_key, dims, pieces, -0.22, 0.18)
    return jnp.clip(values, -limit, limit).astype(kind)


def noise_with(key, extent, scale, reach, pieces, heavy, dtype=jnp.bfloat16):
    entries = scale * jax.random.normal(key, extent, jnp.float32)
    if pieces:
        entries = entries * block_scale(key, extent, pieces, -0.22, 0.18)
    return jnp.clip(raised(entries, jax.random.fold_in(key, 3), *heavy), -reach, reach).astype(dtype)


def setup_inputs(seed: int = 0) -> dict:
    splits = jax.random.split(jax.random.key(seed), 19)
    return {
        "tokens": noise(splits[0], (IMAGES, IMG_LEN, D), 1.0, 6.0, ((0, 8), (1, 4))),
        "caption": noise(splits[1], (IMAGES, TXT, TDIM), 1.0, 6.0, ((0, 8), (2, 4))),
        "token_mask": place_ends((jax.random.randint(splits[2], (IMAGES, IMG_LEN), 0, 2) < 1).astype(jnp.int32), jax.random.fold_in(splits[2], 1), 0, 1),
        "cotangent": noise_with(splits[3], (IMAGES, IMG_LEN, D), 1.0, 6.0, ((0, 8), (1, 4)), (0, 2, 8, 2.0)),
        "gain_self": jnp.clip(1.0 + 0.1 * jax.random.normal(splits[4], (D,), jnp.float32), 0.5, 1.5).astype(jnp.bfloat16),
        "gain_cross": jnp.clip(1.0 + 0.1 * jax.random.normal(splits[5], (D,), jnp.float32), 0.5, 1.5).astype(jnp.bfloat16),
        "gain_feed": jnp.clip(1.0 + 0.1 * jax.random.normal(splits[6], (D,), jnp.float32), 0.5, 1.5).astype(jnp.bfloat16),
        "text_proj": noise(splits[7], (TDIM, D), TDIM ** -0.5, 0.09375, ((0, 4),)),
        "query_self": noise(splits[8], (D, INNER), (D // 4) ** -0.5, 0.25, ((1, 4),)),
        "key_self": noise(splits[9], (D, INNER), D ** -0.5, 0.125, ((1, 4),)),
        "value_self": noise(splits[10], (D, INNER), D ** -0.5, 0.125, ((1, 4),)),
        "out_self": noise(splits[11], (INNER, D), (max(INNER // 24, 2)) ** -0.5, 0.625, ((0, 4),)),
        "query_cross": noise(splits[12], (D, INNER), (D // 4) ** -0.5, 0.25, ((1, 4),)),
        "key_cross": noise(splits[13], (D, INNER), D ** -0.5, 0.125, ((1, 4),)),
        "value_cross": noise(splits[14], (D, INNER), D ** -0.5, 0.125, ((1, 4),)),
        "out_cross": noise(splits[15], (INNER, D), (max(INNER // 24, 2)) ** -0.5, 0.625, ((0, 4),)),
        "up_proj": noise(splits[16], (D, FF), D ** -0.5, 0.125, ((1, 4),)),
        "down_proj": noise(splits[17], (FF, D), (FF // 2) ** -0.5, 0.09375, ((0, 4),)),
    }


@jax.custom_vjp
def low(v):
    return lax.optimization_barrier(v.astype(jnp.bfloat16)).astype(jnp.float32)

@jax.custom_vjp
def low_back(v):
    return v

def low_keep(v):
    return (low(v), None)

def low_pass(kept, grad):
    return (grad,)

def back_keep(v):
    return (v, None)

def back_low(kept, grad):
    return (low(grad),)
low.defvjp(low_keep, low_pass)
low_back.defvjp(back_keep, back_low)

def layer_norm(rows):
    centre = lax.optimization_barrier(jnp.mean(rows, axis=-1, keepdims=True))
    centred = rows - centre
    variance = lax.optimization_barrier(jnp.mean(centred * centred, axis=-1, keepdims=True))
    return centred * lax.rsqrt(variance + 1e-05)

def project(left, weight):
    return jnp.einsum('gld,de->gle', left, weight, precision=lax.Precision.HIGHEST)

def rounded_project(left, weight):
    return low(low_back(project(left, weight)))

def attention(query, keys, values):
    groups, query_len = (query.shape[0], query.shape[1])
    key_len = keys.shape[1]
    query_heads = query.reshape(groups, query_len, HEADS, HEAD)
    key_heads = keys.reshape(groups, key_len, HEADS, HEAD)
    value_heads = values.reshape(groups, key_len, HEADS, HEAD)
    raw_scores = jnp.einsum('gqhe,gkhe->ghqk', query_heads, key_heads, precision=lax.Precision.HIGHEST)
    scores = low_back(raw_scores * (1.0 / math.sqrt(HEAD)))
    peak = lax.optimization_barrier(jnp.max(scores, axis=-1, keepdims=True))
    powers = jnp.exp(scores - peak)
    probs = low(powers / lax.optimization_barrier(jnp.sum(powers, axis=-1, keepdims=True)))
    attended = jnp.einsum('ghqk,gkhe->gqhe', probs, value_heads, precision=lax.Precision.HIGHEST)
    return low(low_back(attended.reshape(groups, query_len, HEADS * HEAD)))

def forward(image_rows, words, gain_self, gain_cross, gain_feed, text_proj, query_self, key_self, value_self, out_self, query_cross, key_cross, value_cross, out_cross, up_proj, down_proj):
    context = rounded_project(words, text_proj)
    hidden_self = low(layer_norm(image_rows) * gain_self)
    attended_sa = attention(rounded_project(hidden_self, query_self), rounded_project(hidden_self, key_self), rounded_project(hidden_self, value_self))
    resid_mid = image_rows + low_back(project(attended_sa, out_self))
    hidden_cross = low(layer_norm(resid_mid) * gain_cross)
    attended_ca = attention(rounded_project(hidden_cross, query_cross), rounded_project(context, key_cross), rounded_project(context, value_cross))
    resid_late = resid_mid + low_back(project(attended_ca, out_cross))
    hidden_feed = low(layer_norm(resid_late) * gain_feed)
    activ = low(jax.nn.gelu(low_back(project(hidden_feed, up_proj))))
    return resid_late + low_back(project(activ, down_proj))

def reference(tokens, caption, token_mask, cotangent, gain_self, gain_cross, gain_feed, text_proj, query_self, key_self, value_self, out_self, query_cross, key_cross, value_cross, out_cross, up_proj, down_proj):
    group_size = math.gcd(IMAGES, 16)
    group_count = IMAGES // group_size
    token_blocks = tokens.astype(jnp.float32).reshape(group_count, group_size, IMG_LEN, D)
    word_blocks = caption.astype(jnp.float32).reshape(group_count, group_size, TXT, TDIM)
    mask_blocks = token_mask.reshape(group_count, group_size, IMG_LEN)
    grad_blocks = cotangent.astype(jnp.float32).reshape(group_count, group_size, IMG_LEN, D)
    weights = tuple((weight.astype(jnp.float32) for weight in (gain_self, gain_cross, gain_feed, text_proj, query_self, key_self, value_self, out_self, query_cross, key_cross, value_cross, out_cross, up_proj, down_proj)))

    def one_group(totals, block_data):
        image_rows, words, marks, grads_in = block_data
        result, pullback = jax.vjp(forward, image_rows, words, *weights)
        seeded = grads_in * marks[..., None].astype(jnp.float32)
        backs = pullback(seeded)
        updated = tuple((total + part for total, part in zip(totals, backs[2:])))
        return (updated, (result.astype(jnp.bfloat16), backs[0].astype(jnp.bfloat16), backs[1].astype(jnp.bfloat16)))
    initial = tuple((jnp.zeros(weight.shape, jnp.float32) for weight in weights))
    totals, stacked = lax.scan(one_group, initial, (token_blocks, word_blocks, mask_blocks, grad_blocks))
    layer_out = stacked[0].reshape(IMAGES, IMG_LEN, D)
    grad_tokens = stacked[1].reshape(IMAGES, IMG_LEN, D)
    grad_caption = stacked[2].reshape(IMAGES, TXT, TDIM)
    return (layer_out, grad_tokens, grad_caption, totals[0], totals[1], totals[2], totals[3], totals[4], totals[5], totals[6], totals[7], totals[8], totals[9], totals[10], totals[11], totals[12], totals[13])
```

```python
import math

import jax
import jax.numpy as jnp
from jax import lax
from jax.experimental import pallas as pl
from jax.experimental.pallas import tpu as pltpu
from jax.sharding import PartitionSpec as P

HEAD = 128
MESH = pl.DeviceIdType.MESH

def normalize(rows):
    centre = jnp.mean(rows, axis=-1, keepdims=True)
    centred = rows - centre
    variance = jnp.mean(centred * centred, axis=-1, keepdims=True)
    inv_std = lax.rsqrt(variance + 1e-05)
    return (centred * inv_std, inv_std)


def norm_back(d_normed, normed, inv_std):
    inner = d_normed - jnp.mean(d_normed, axis=-1, keepdims=True)
    inner = inner - normed * jnp.mean(d_normed * normed, axis=-1, keepdims=True)
    return inv_std * inner


def times_weight(left, right):
    return jnp.dot(left, right, preferred_element_type=jnp.float32)


def split_heads(matrix):
    return matrix.reshape(matrix.shape[0], matrix.shape[1], matrix.shape[2] // HEAD, HEAD)


def join_heads(heads):
    return heads.reshape(heads.shape[0], heads.shape[1], heads.shape[2] * HEAD)


def head_scores(query, keys):
    scores = jnp.einsum(
        "bqhe,bkhe->bhqk", split_heads(query), split_heads(keys), preferred_element_type=jnp.float32
    )
    return scores * (1.0 / math.sqrt(HEAD))


def attend(query, keys, values):
    scores = head_scores(query, keys)
    peak = jnp.max(scores, axis=-1, keepdims=True)
    powers = jnp.exp(scores - peak)
    summed = jnp.sum(powers, axis=-1, keepdims=True)
    low_probs = (powers / summed).astype(jnp.bfloat16)
    attended = jnp.einsum(
        "bhqk,bkhe->bqhe", low_probs, split_heads(values), preferred_element_type=jnp.float32
    )
    return join_heads(attended).astype(jnp.bfloat16), peak + jnp.log(summed)


def attend_back(query, keys, values, log_total, d_attended):
    probs = jnp.exp(head_scores(query, keys) - log_total)
    low_probs = probs.astype(jnp.bfloat16)
    d_heads = split_heads(d_attended)
    d_probs = jnp.einsum(
        "bqhe,bkhe->bhqk", d_heads, split_heads(values), preferred_element_type=jnp.float32
    )
    d_values = jnp.einsum("bhqk,bqhe->bkhe", low_probs, d_heads, preferred_element_type=jnp.float32)
    weighted = jnp.sum(probs * d_probs, axis=-1, keepdims=True)
    d_scores = (probs * (d_probs - weighted)).astype(jnp.bfloat16)
    scale = 1.0 / math.sqrt(HEAD)
    d_query = (
        jnp.einsum("bhqk,bkhe->bqhe", d_scores, split_heads(keys), preferred_element_type=jnp.float32)
        * scale
    )
    d_keys = (
        jnp.einsum("bhqk,bqhe->bkhe", d_scores, split_heads(query), preferred_element_type=jnp.float32)
        * scale
    )
    return tuple(join_heads(d).astype(jnp.bfloat16) for d in (d_query, d_keys, d_values))


def contract(left, right):
    return lax.dot_general(
        left, right, (((0, 1), (0, 1)), ((), ())), preferred_element_type=jnp.float32
    ).astype(jnp.bfloat16)


def against(left, right):
    return lax.dot_general(
        left, right, (((2,), (1,)), ((), ())), preferred_element_type=jnp.float32
    )


def group_rows(piece):
    return lax.all_gather(piece, "narrow", axis=1, tiled=True)


def own_rows(partial):
    return lax.psum_scatter(partial, "narrow", scatter_dimension=1, tiled=True)


def feed_back(partial):
    return own_rows(partial.astype(jnp.bfloat16)).astype(jnp.float32)


def text_total(partial):
    return lax.psum(partial, "narrow")


def wide_sum(arrays, dims, wide, order=None, z_first=3, ahead=2):
    Z = wide // 2
    units = []
    shapes = []
    for a, (arr, dim) in enumerate(zip(arrays, dims)):
        if dim == 0:
            blk = arr.shape[0] // wide
            n = arr.shape[1] // 512
            shapes.append((blk, arr.shape[1]))
        else:
            blk = arr.shape[1] // wide
            n = arr.shape[0] // 512
            shapes.append((arr.shape[0], blk))
        for c in range(n):
            units.append((a, dim, c, blk))
    if order is not None:
        units = [units[i] for i in order]
    blk = units[0][3]
    shp = [(blk, 512), (512, blk)]
    U = len(units)
    zset = set(int((k + 0.5) * U / z_first) for k in range(z_first)) if z_first else set()
    yf = [u for k, u in enumerate(units) if k not in zset]
    zf = [u for k, u in enumerate(units) if k in zset]
    cnt = {}
    def slot(key):
        cnt[key] = cnt.get(key, 0) + 1
        return cnt[key] - 1
    yslots = [slot(("y", u[1])) for u in yf]
    zslots = [slot(("z", u[1])) for u in zf]
    ny = [max(1, cnt.get(("y", d), 0)) for d in (0, 1)]
    nz = [max(1, cnt.get(("z", d), 0)) for d in (0, 1)]
    OWN = 3

    def kernel(*refs):
        ins = refs[: len(arrays)]
        outs = refs[len(arrays): 2 * len(arrays)]
        (S0, S1, R0, R1, L0, L1, O0, O1, T0, T1, ZR0, ZR1, ZL0, ZL1, YB0, YB1, F0, F1,
         ysend, yrecv, own_sem, rsend, rrecv, lsend, lrecv,
         tsem, zrsend, zrrecv, zlsend, zlrecv, ybsend, ybrecv, out_sem) = refs[2 * len(arrays):]
        S, R, L, O, T, ZR, ZL, YB, F = ((S0, S1), (R0, R1), (L0, L1), (O0, O1), (T0, T1), (ZR0, ZR1), (ZL0, ZL1), (YB0, YB1), (F0, F1))
        me = lax.axis_index("wide")
        z = me // 2
        y = me % 2
        yp = {"wide": z * 2 + (1 - y)}
        zr = {"wide": jnp.minimum(z + 1, Z - 1) * 2 + y}
        zl = {"wide": jnp.maximum(z - 1, 0) * 2 + y}
        has_r = z < Z - 1
        has_l = z > 0
        bar = pltpu.get_barrier_semaphore()
        pl.semaphore_signal(bar, inc=1, device_id=yp, device_id_type=MESH)
        @pl.when(has_r)
        def _():
            pl.semaphore_signal(bar, inc=1, device_id=zr, device_id_type=MESH)
        @pl.when(has_l)
        def _():
            pl.semaphore_signal(bar, inc=1, device_id=zl, device_id_type=MESH)
        pl.semaphore_wait(bar, 1 + has_r.astype(jnp.int32) + has_l.astype(jnp.int32))

        def block(u, w):
            a, dim, c, b = u
            start = pl.multiple_of(w * b, b)
            if dim == 0:
                return ins[a].at[pl.ds(start, b), pl.ds(c * 512, 512)]
            return ins[a].at[pl.ds(c * 512, 512), pl.ds(start, b)]

        def outblock(u):
            a, dim, c, b = u
            if dim == 0:
                return outs[a].at[:, pl.ds(c * 512, 512)]
            return outs[a].at[pl.ds(c * 512, 512), :]

        def addto(dst, src):
            rows = dst.shape[0]
            step = min(rows, 64)
            def body(i, _):
                s = pl.ds(pl.multiple_of(i * step, step), step)
                dst[s, :] = dst[s, :] + src[s, :]
                return 0
            lax.fori_loop(0, rows // step, body, 0)

        def rc(src, dst, ss, rs, dev):
            return pltpu.make_async_remote_copy(src_ref=src, dst_ref=dst, send_sem=ss, recv_sem=rs, device_id=dev, device_id_type=MESH)

        def ycopy(i, k):
            u, s = yf[i], yslots[i]
            return rc(block(u, k * 2 + (1 - y)), S[u[1]].at[s, k], ysend.at[i, k], yrecv.at[i, k], yp)
        def ocopy(i, k):
            u = yf[i]
            return pltpu.make_async_copy(block(u, k * 2 + y), O[u[1]].at[i % OWN, k], own_sem.at[i % OWN, k])
        korder = [0, Z - 1] + list(range(1, Z - 1))
        def ystart(i):
            for k in korder:
                ycopy(i, k).start()
        def ostart(i):
            for k in korder:
                ocopy(i, k).start()
        def yadd(i):
            u, s = yf[i], yslots[i]
            for k in korder:
                ycopy(i, k).wait_recv()
                ocopy(i, k).wait()
                addto(S[u[1]].at[s, k], O[u[1]].at[i % OWN, k])

        def rcopy(i, t):
            u, s = yf[i], yslots[i]
            d = Z - t + z
            return rc(S[u[1]].at[s, jnp.clip(d, 0, Z - 1)], R[u[1]].at[s, t - 1], rsend.at[i, t - 1], rrecv.at[i, t - 1], zr)
        def lcopy(i, t):
            u, s = yf[i], yslots[i]
            d = t - Z + z
            return rc(S[u[1]].at[s, jnp.clip(d, 0, Z - 1)], L[u[1]].at[s, t - 1], lsend.at[i, t - 1], lrecv.at[i, t - 1], zl)
        def chain(i, t):
            u, s = yf[i], yslots[i]
            kd = u[1]
            @pl.when(has_r & (t >= z + 1))
            def _():
                if t > 1:
                    @pl.when(has_l & (t - 1 >= z))
                    def _():
                        rcopy(i, t - 1).wait_recv()
                        addto(S[kd].at[s, jnp.clip(Z - t + z, 0, Z - 1)], R[kd].at[s, t - 2])
                rcopy(i, t).start()
            zb = Z - 1 - z
            @pl.when(has_l & (t >= zb + 1))
            def _():
                if t > 1:
                    @pl.when(has_r & (t - 1 >= zb))
                    def _():
                        lcopy(i, t - 1).wait_recv()
                        addto(S[kd].at[s, jnp.clip(t - Z + z, 0, Z - 1)], L[kd].at[s, t - 2])
                lcopy(i, t).start()
        nfin = [0]
        def emit(u, get):
            f = nfin[0]
            nfin[0] += 1
            q = f % 2
            if f >= 2:
                pu = emitted[f - 2]
                pltpu.make_async_copy(F[pu[1]].at[q], outblock(pu), out_sem.at[q]).wait()
            get(F[u[1]].at[q])
            pltpu.make_async_copy(F[u[1]].at[q], outblock(u), out_sem.at[q]).start()
            emitted.append(u)
        emitted = []
        def final(i):
            u, s = yf[i], yslots[i]
            kd = u[1]
            @pl.when(has_l)
            def _():
                rcopy(i, Z - 1).wait_recv()
                addto(S[kd].at[s, z], R[kd].at[s, Z - 2])
            @pl.when(has_r)
            def _():
                lcopy(i, Z - 1).wait_recv()
                addto(S[kd].at[s, z], L[kd].at[s, Z - 2])
            def get(dst):
                dst[...] = S[kd][s, z]
            emit(u, get)

        def tcopy(j, w):
            u, s = zf[j], zslots[j]
            return pltpu.make_async_copy(block(u, w), T[u[1]].at[s, w // 2, w % 2], tsem.at[j, w])
        def zrcopy(j, t):
            u, s = zf[j], zslots[j]
            d = Z - t + z
            return rc(T[u[1]].at[s, jnp.clip(d, 0, Z - 1)], ZR[u[1]].at[s, t - 1], zrsend.at[j, t - 1], zrrecv.at[j, t - 1], zr)
        def zlcopy(j, t):
            u, s = zf[j], zslots[j]
            d = t - Z + z
            return rc(T[u[1]].at[s, jnp.clip(d, 0, Z - 1)], ZL[u[1]].at[s, t - 1], zlsend.at[j, t - 1], zlrecv.at[j, t - 1], zl)
        def zchain(j, t):
            u, s = zf[j], zslots[j]
            kd = u[1]
            if t == 1:
                for w in range(wide):
                    tcopy(j, w).wait()
            @pl.when(has_r & (t >= z + 1))
            def _():
                if t > 1:
                    @pl.when(has_l & (t - 1 >= z))
                    def _():
                        zrcopy(j, t - 1).wait_recv()
                        for q in range(2):
                            addto(T[kd].at[s, jnp.clip(Z - t + z, 0, Z - 1), q], ZR[kd].at[s, t - 2, q])
                zrcopy(j, t).start()
            zb = Z - 1 - z
            @pl.when(has_l & (t >= zb + 1))
            def _():
                if t > 1:
                    @pl.when(has_r & (t - 1 >= zb))
                    def _():
                        zlcopy(j, t - 1).wait_recv()
                        for q in range(2):
                            addto(T[kd].at[s, jnp.clip(t - Z + z, 0, Z - 1), q], ZL[kd].at[s, t - 2, q])
                zlcopy(j, t).start()
        def ybcopy(j):
            u, s = zf[j], zslots[j]
            return rc(T[u[1]].at[s, z, 1 - y], YB[u[1]].at[s], ybsend.at[j], ybrecv.at[j], yp)
        def zfold(j):
            u, s = zf[j], zslots[j]
            kd = u[1]
            @pl.when(has_l)
            def _():
                zrcopy(j, Z - 1).wait_recv()
                for q in range(2):
                    addto(T[kd].at[s, z, q], ZR[kd].at[s, Z - 2, q])
            @pl.when(has_r)
            def _():
                zlcopy(j, Z - 1).wait_recv()
                for q in range(2):
                    addto(T[kd].at[s, z, q], ZL[kd].at[s, Z - 2, q])
            ybcopy(j).start()
        def zfinal(j):
            u, s = zf[j], zslots[j]
            kd = u[1]
            ybcopy(j).wait_recv()
            def get(dst):
                dst[...] = T[kd][s, z, y] + YB[kd][s]
            emit(u, get)

        NY, NZ = len(yf), len(zf)
        for i in range(min(ahead, NY)):
            ystart(i)
        for j in range(NZ):
            for w in range(wide):
                tcopy(j, w).start()
        for i in range(min(2, NY)):
            ostart(i)
        gap = max(2, NY // max(NZ, 1))
        zev = {}
        for j in range(NZ):
            b = j * gap
            for t in range(1, Z):
                zev.setdefault(b + 1 * (t - 1), []).append(("c", j, t))
            zev.setdefault(b + (Z - 1), []).append(("f", j, 0))
            zev.setdefault(b + (Z - 1) + 1, []).append(("e", j, 0))
        last = max([NY + Z] + [k + 1 for k in zev])
        for k in range(last):
            for ev in zev.get(k, []):
                if ev[0] == "c":
                    zchain(ev[1], ev[2])
                elif ev[0] == "f":
                    zfold(ev[1])
                else:
                    zfinal(ev[1])
            if k < NY:
                if k + ahead < NY:
                    ystart(k + ahead)
                if k + 2 < NY:
                    ostart(k + 2)
                yadd(k)
            for t in range(1, Z):
                i = k - (t - 1)
                if 0 <= i < NY:
                    chain(i, t)
            i = k - (Z - 1)
            if 0 <= i < NY:
                final(i)
        nf = nfin[0]
        for f in range(max(0, nf - 2), nf):
            u = emitted[f]
            pltpu.make_async_copy(F[u[1]].at[f % 2], outblock(u), out_sem.at[f % 2]).wait()
        for i in range(NY):
            for k in range(Z):
                ycopy(i, k).wait_send()
            for t in range(1, Z):
                @pl.when(has_r & (t >= z + 1))
                def _():
                    rcopy(i, t).wait_send()
                @pl.when(has_l & (t >= Z - z))
                def _():
                    lcopy(i, t).wait_send()
        for j in range(NZ):
            for t in range(1, Z):
                @pl.when(has_r & (t >= z + 1))
                def _():
                    zrcopy(j, t).wait_send()
                @pl.when(has_l & (t >= Z - z))
                def _():
                    zlcopy(j, t).wait_send()
            ybcopy(j).wait_send()

    bf = jnp.bfloat16
    V = pltpu.VMEM
    DS = pltpu.SemaphoreType.DMA
    sc = []
    for d in (0, 1): sc.append(V((ny[d], Z) + shp[d], bf))
    for _ in range(2):
        for d in (0, 1): sc.append(V((ny[d], Z - 1) + shp[d], bf))
    for d in (0, 1): sc.append(V((OWN, Z) + shp[d], bf))
    for d in (0, 1): sc.append(V((nz[d], Z, 2) + shp[d], bf))
    for _ in range(2):
        for d in (0, 1): sc.append(V((nz[d], Z - 1, 2) + shp[d], bf))
    for d in (0, 1): sc.append(V((nz[d],) + shp[d], bf))
    for d in (0, 1): sc.append(V((2,) + shp[d], bf))
    NY, NZ = len(yf), max(1, len(zf))
    sc += [DS((NY, Z)), DS((NY, Z)), DS((OWN, Z))] + [DS((NY, Z - 1))] * 4
    sc += [DS((NZ, wide))] + [DS((NZ, Z - 1))] * 4 + [DS((NZ,)), DS((NZ,)), DS((2,))]
    return pl.pallas_call(
        kernel,
        out_shape=[jax.ShapeDtypeStruct(s, bf) for s in shapes],
        in_specs=[pl.BlockSpec(memory_space=pl.ANY)] * len(arrays),
        out_specs=[pl.BlockSpec(memory_space=pl.ANY)] * len(arrays),
        scratch_shapes=sc,
        compiler_params=pltpu.CompilerParams(collective_id=0, has_side_effects=True, vmem_limit_bytes=63 * 1024 * 1024),
        name="wide_sum",
    )(*arrays)


def local(
    tokens,
    caption,
    token_mask,
    cotangent,
    gain_self,
    gain_cross,
    gain_feed,
    text_proj,
    query_self,
    key_self,
    value_self,
    out_self,
    query_cross,
    key_cross,
    value_cross,
    out_cross,
    up_proj,
    down_proj,
):
    gain_one = gain_self.astype(jnp.float32)
    gain_two = gain_cross.astype(jnp.float32)
    gain_three = gain_feed.astype(jnp.float32)
    low = jnp.bfloat16

    resid_in = tokens.astype(jnp.float32)
    normed_self, inv_self = normalize(resid_in)
    image_self = group_rows((normed_self * gain_one).astype(low))
    query_sa = times_weight(image_self, query_self).astype(low)
    keys_sa = times_weight(image_self, key_self).astype(low)
    values_sa = times_weight(image_self, value_self).astype(low)
    attended_sa, total_sa = attend(query_sa, keys_sa, values_sa)
    resid_mid = resid_in + own_rows(times_weight(attended_sa, out_self))
    context = text_total(times_weight(caption, text_proj)).astype(low)
    keys_ca = times_weight(context, key_cross).astype(low)
    values_ca = times_weight(context, value_cross).astype(low)
    normed_cross, inv_cross = normalize(resid_mid)
    image_cross = group_rows((normed_cross * gain_two).astype(low))
    query_ca = times_weight(image_cross, query_cross).astype(low)
    attended_ca, total_ca = attend(query_ca, keys_ca, values_ca)
    resid_late = resid_mid + own_rows(times_weight(attended_ca, out_cross))
    normed_feed, inv_feed = normalize(resid_late)
    d_result = cotangent.astype(jnp.float32) * token_mask[:, :, None].astype(jnp.float32)
    d_image = group_rows(d_result.astype(low))
    image_feed = group_rows((normed_feed * gain_three).astype(low))
    pre_act = times_weight(image_feed, up_proj)
    gelu_out, gelu_pull = jax.vjp(jax.nn.gelu, pre_act)
    activ = gelu_out.astype(low)
    resid_out = resid_late + feed_back(times_weight(activ, down_proj))
    d_pre = gelu_pull(against(d_image, down_proj))[0].astype(low)
    part_down = contract(activ, d_image)
    part_up = contract(image_feed, d_pre)
    d_hidden_feed = feed_back(against(d_pre, up_proj))
    part_gain_feed = jnp.sum(d_hidden_feed * normed_feed, axis=(0, 1))
    d_late = d_result + norm_back(d_hidden_feed * gain_three, normed_feed, inv_feed)
    d_image_cross = group_rows(d_late.astype(low))
    part_out_cross = contract(attended_ca, d_image_cross)
    d_attended_ca = against(d_image_cross, out_cross).astype(low)
    d_query_ca, d_keys_ca, d_values_ca = attend_back(
        query_ca, keys_ca, values_ca, total_ca, d_attended_ca
    )
    part_query_cross = contract(image_cross, d_query_ca)
    part_key_cross = contract(context, d_keys_ca)
    part_value_cross = contract(context, d_values_ca)
    d_hidden_cross = own_rows(against(d_query_ca, query_cross))
    d_context = text_total(against(d_keys_ca, key_cross) + against(d_values_ca, value_cross))
    d_context = d_context.astype(low)
    part_text = contract(caption, d_context)
    d_words = against(d_context, text_proj).astype(low)
    part_gain_cross = jnp.sum(d_hidden_cross * normed_cross, axis=(0, 1))
    d_mid = d_late + norm_back(d_hidden_cross * gain_two, normed_cross, inv_cross)
    d_image_self = group_rows(d_mid.astype(low))
    part_out_self = contract(attended_sa, d_image_self)
    d_attended_sa = against(d_image_self, out_self).astype(low)
    d_query_sa, d_keys_sa, d_values_sa = attend_back(
        query_sa, keys_sa, values_sa, total_sa, d_attended_sa
    )
    part_query_self = contract(image_self, d_query_sa)
    part_key_self = contract(image_self, d_keys_sa)
    part_value_self = contract(image_self, d_values_sa)
    d_hidden_self = own_rows(
        against(d_query_sa, query_self)
        + against(d_keys_sa, key_self)
        + against(d_values_sa, value_self)
    )
    part_gain_self = jnp.sum(d_hidden_self * normed_self, axis=(0, 1))
    d_input = d_mid + norm_back(d_hidden_self * gain_one, normed_self, inv_self)
    parts = (
        part_text,
        part_query_self,
        part_key_self,
        part_value_self,
        part_out_self,
        part_query_cross,
        part_key_cross,
        part_value_cross,
        part_out_cross,
        part_up,
        part_down,
    )
    dims = (1, 0, 0, 0, 1, 0, 0, 0, 1, 0, 1)
    wide = lax.axis_size("wide")
    if wide % 2 == 0 and 4 <= wide <= 8:
        summed = wide_sum(parts, dims, wide)
    else:
        summed = [
            lax.psum_scatter(part, "wide", scatter_dimension=dim, tiled=True)
            for part, dim in zip(parts, dims)
        ]
    gains = lax.psum((part_gain_self, part_gain_cross, part_gain_feed), ("wide", "narrow"))
    return (
        resid_out.astype(low),
        d_input.astype(low),
        d_words,
        *gains,
        *[part.astype(jnp.float32) for part in summed],
    )


def solution(mesh):
    in_specs = (
        P("wide", "narrow", None),
        P("wide", None, "narrow"),
        P("wide", "narrow"),
        P("wide", "narrow", None),
        P(),
        P(),
        P(),
        P("narrow", None),
        P(None, "narrow"),
        P(None, "narrow"),
        P(None, "narrow"),
        P("narrow", None),
        P(None, "narrow"),
        P(None, "narrow"),
        P(None, "narrow"),
        P("narrow", None),
        P(None, "narrow"),
        P("narrow", None),
    )
    out_specs = (
        P("wide", "narrow", None),
        P("wide", "narrow", None),
        P("wide", None, "narrow"),
        P(),
        P(),
        P(),
        P("narrow", "wide"),
        P("wide", "narrow"),
        P("wide", "narrow"),
        P("wide", "narrow"),
        P("narrow", "wide"),
        P("wide", "narrow"),
        P("wide", "narrow"),
        P("wide", "narrow"),
        P("narrow", "wide"),
        P("wide", "narrow"),
        P("narrow", "wide"),
    )
    return jax.shard_map(local, mesh=mesh, in_specs=in_specs, out_specs=out_specs, check_vma=False)
```

```python
import math

import jax
import jax.numpy as jnp
from jax import lax
from jax.experimental import pallas as pl
from jax.experimental.pallas import tpu as pltpu
from jax.sharding import PartitionSpec as P

HEAD = 128
MESH = pl.DeviceIdType.MESH

def times_weight(left, right):
    return jnp.dot(left, right, preferred_element_type=jnp.float32)


def split_heads(matrix):
    return matrix.reshape(matrix.shape[0], matrix.shape[1], matrix.shape[2] // HEAD, HEAD)


def join_heads(heads):
    return heads.reshape(heads.shape[0], heads.shape[1], heads.shape[2] * HEAD)


def head_scores(query, keys):
    scores = jnp.einsum(
        "bqhe,bkhe->bhqk", split_heads(query), split_heads(keys), preferred_element_type=jnp.float32
    )
    return scores * (1.0 / math.sqrt(HEAD))


def attend(query, keys, values):
    scores = head_scores(query, keys)
    peak = jnp.max(scores, axis=-1, keepdims=True)
    powers = jnp.exp(scores - peak)
    summed = jnp.sum(powers, axis=-1, keepdims=True)
    low_probs = (powers / summed).astype(jnp.bfloat16)
    attended = jnp.einsum(
        "bhqk,bkhe->bqhe", low_probs, split_heads(values), preferred_element_type=jnp.float32
    )
    return join_heads(attended).astype(jnp.bfloat16), peak + jnp.log(summed)


def attend_back(query, keys, values, log_total, d_attended):
    probs = jnp.exp(head_scores(query, keys) - log_total)
    low_probs = probs.astype(jnp.bfloat16)
    d_heads = split_heads(d_attended)
    d_probs = jnp.einsum(
        "bqhe,bkhe->bhqk", d_heads, split_heads(values), preferred_element_type=jnp.float32
    )
    d_values = jnp.einsum("bhqk,bqhe->bkhe", low_probs, d_heads, preferred_element_type=jnp.float32)
    weighted = jnp.sum(probs * d_probs, axis=-1, keepdims=True)
    d_scores = (probs * (d_probs - weighted)).astype(jnp.bfloat16)
    scale = 1.0 / math.sqrt(HEAD)
    d_query = (
        jnp.einsum("bhqk,bkhe->bqhe", d_scores, split_heads(keys), preferred_element_type=jnp.float32)
        * scale
    )
    d_keys = (
        jnp.einsum("bhqk,bqhe->bkhe", d_scores, split_heads(query), preferred_element_type=jnp.float32)
        * scale
    )
    return tuple(join_heads(d).astype(jnp.bfloat16) for d in (d_query, d_keys, d_values))


def contract(left, right):
    return lax.dot_general(
        left, right, (((0, 1), (0, 1)), ((), ())), preferred_element_type=jnp.float32
    ).astype(jnp.bfloat16)


def against(left, right):
    return lax.dot_general(
        left, right, (((2,), (1,)), ((), ())), preferred_element_type=jnp.float32
    )


def group_rows(piece):
    return lax.all_gather(piece, "narrow", axis=1, tiled=True)


def own_rows(partial):
    return lax.psum_scatter(partial, "narrow", scatter_dimension=1, tiled=True)


def feed_back(partial):
    return own_rows(partial.astype(jnp.bfloat16)).astype(jnp.float32)


def text_total(partial):
    own = lax.psum_scatter(partial, "narrow", scatter_dimension=1, tiled=True)
    return lax.all_gather(own.astype(jnp.bfloat16), "narrow", axis=1, tiled=True)


VM = pl.BlockSpec(memory_space=pltpu.VMEM)
HB = pl.BlockSpec(memory_space=pl.ANY)
SLAB = 16


def norm_rows(rows):
    centre = jnp.mean(rows, axis=-1, keepdims=True)
    centred = rows - centre
    variance = jnp.mean(centred * centred, axis=-1, keepdims=True)
    inv_std = lax.rsqrt(variance + 1e-05)
    return centred * inv_std, inv_std


def each_slab(count, step):
    def body(i, carry):
        step(pl.ds(pl.multiple_of(i * SLAB, SLAB), SLAB))
        return carry

    lax.fori_loop(0, count // SLAB, body, 0)


class Narrow:
    def __init__(self):
        self.me = lax.axis_index("narrow")
        self.x = self.me // 2
        self.c = self.me % 2
        self.core_at = self.x * 2 + 1 - self.c
        self.chip_at = (1 - self.x) * 2 + self.c
        self.far_at = (1 - self.x) * 2 + 1 - self.c
        self.core = {"narrow": self.core_at}
        self.chip = {"narrow": self.chip_at}

    def meet(self):
        barrier = pltpu.get_barrier_semaphore()
        for peer in (self.core, self.chip):
            pl.semaphore_signal(barrier, inc=1, device_id=peer, device_id_type=MESH)
        pl.semaphore_wait(barrier, 2)


def send(src, dst, sems, index, peer):
    return pltpu.make_async_remote_copy(
        src_ref=src,
        dst_ref=dst,
        send_sem=sems.at[(0,) + index],
        recv_sem=sems.at[(1,) + index],
        device_id=peer,
        device_id_type=MESH,
    )


class Gather:
    def __init__(self, net, held, full, sems, local_sems):
        self.net, self.held, self.full, self.sems, self.local = net, held, full, sems, local_sems
        self.own = held.shape[1]

    def place(self, b, who):
        return self.full.at[b, pl.ds(pl.multiple_of(who * self.own, self.own), self.own), :]

    def to_core(self, b):
        return send(self.held.at[b], self.place(b, self.net.me), self.sems, (b, 0), self.net.core)

    def to_chip(self, b):
        return send(self.held.at[b], self.place(b, self.net.me), self.sems, (b, 1), self.net.chip)

    def onward(self, b):
        block = self.place(b, self.net.chip_at)
        return send(block, block, self.sems, (b, 2), self.net.core)

    def keep(self, b):
        return pltpu.make_async_copy(self.held.at[b], self.place(b, self.net.me), self.local.at[b])

    def start(self, b):
        self.to_chip(b).start()
        self.to_core(b).start()
        self.keep(b).start()

    def forward(self, b):
        self.to_chip(b).wait_recv()
        self.onward(b).start()

    def finish(self, b):
        self.to_core(b).wait_recv()
        self.onward(b).wait_recv()
        self.to_core(b).wait_send()
        self.to_chip(b).wait_send()
        self.onward(b).wait_send()
        self.keep(b).wait()


class Scatter:
    def __init__(self, net, part, landed, outgoing, arrived, sems):
        self.net, self.part, self.landed = net, part, landed
        self.outgoing, self.arrived, self.sems = outgoing, arrived, sems
        self.own = part.shape[1] // 4

    def rows(self, b, who):
        return self.part.at[b, pl.ds(pl.multiple_of(who * self.own, self.own), self.own), :]

    def core_copy(self, b, k):
        who = self.net.far_at if k == 0 else self.net.core_at
        return send(self.rows(b, who), self.landed.at[b, k], self.sems, (b, k), self.net.core)

    def chip_copy(self, b):
        return send(self.outgoing.at[b], self.arrived.at[b], self.sems, (b, 2), self.net.chip)

    def start(self, b):
        self.core_copy(b, 0).start()
        self.core_copy(b, 1).start()

    def cross(self, b):
        self.core_copy(b, 0).wait_recv()
        mine = self.rows(b, self.net.chip_at)

        def step(s):
            total = mine[s, :] + self.landed[b, 0, s, :]
            self.outgoing[b, s, :] = total.astype(self.outgoing.dtype)

        each_slab(self.own, step)
        self.chip_copy(b).start()

    def ready(self, b):
        self.core_copy(b, 1).wait_recv()
        self.chip_copy(b).wait_recv()

    def total(self, b, s):
        near = self.rows(b, self.net.me)[s, :] + self.landed[b, 1, s, :]
        return near + self.arrived[b, s, :].astype(jnp.float32)

    def finish(self, b):
        self.core_copy(b, 0).wait_send()
        self.core_copy(b, 1).wait_send()
        self.chip_copy(b).wait_send()


def scatter_scratch(images, own, width):
    return [
        pltpu.VMEM((images, 4 * own, width), jnp.float32),
        pltpu.VMEM((images, 2, own, width), jnp.float32),
        pltpu.VMEM((images, own, width), jnp.bfloat16),
        pltpu.VMEM((images, own, width), jnp.bfloat16),
        pltpu.SemaphoreType.DMA((2, images, 3)),
    ]


def gather_scratch(images, own, width):
    return [
        pltpu.VMEM((images, own, width), jnp.bfloat16),
        pltpu.SemaphoreType.DMA((2, images, 3)),
        pltpu.SemaphoreType.DMA((images,)),
    ]


def partial_rows(part, b, lefts, rights, transposed, tile=512):
    width = part.shape[2]

    def body(i, carry):
        cols = pl.ds(pl.multiple_of(i * tile, tile), tile)
        total = None
        for left, right in zip(lefts, rights):
            if transposed:
                term = lax.dot_general(
                    left[b], right[cols, :], (((1,), (1,)), ((), ())),
                    preferred_element_type=jnp.float32,
                )
            else:
                term = jnp.dot(left[b], right[:, cols], preferred_element_type=jnp.float32)
            total = term if total is None else total + term
        part[b, :, cols] = total
        return carry

    lax.fori_loop(0, width // tile, body, 0)


def params(number, limit):
    return pltpu.CompilerParams(
        collective_id=number, has_side_effects=True, vmem_limit_bytes=limit * 1024 * 1024
    )


def open_rows(tokens, gain, number):
    images, own, width = tokens.shape

    def kernel(rows, gain_ref, full, held, sems, local):
        net = Narrow()
        net.meet()
        gather = Gather(net, held, full, sems, local)
        for b in range(images):
            def step(s, b=b):
                normed, _ = norm_rows(rows[b, s, :].astype(jnp.float32))
                held[b, s, :] = (normed * gain_ref[...]).astype(jnp.bfloat16)
            each_slab(own, step)
            gather.start(b)
        for b in range(images):
            gather.forward(b)
        for b in range(images):
            gather.finish(b)

    return pl.pallas_call(
        kernel,
        out_shape=jax.ShapeDtypeStruct((images, 4 * own, width), jnp.bfloat16),
        in_specs=[VM, VM],
        out_specs=HB,
        scratch_shapes=gather_scratch(images, own, width),
        compiler_params=params(number, 16),
        name="open_rows",
    )(tokens, gain)


def forward_rows(lefts, rights, resid, gain, number):
    images, own, width = resid.shape
    count = len(lefts)

    def kernel(*refs):
        left_refs, right_refs = refs[:count], refs[count : 2 * count]
        resid_ref, gain_ref, out, full = refs[2 * count : 2 * count + 4]
        rest = refs[2 * count + 4 :]
        net = Narrow()
        scatter = Scatter(net, *rest[:5])
        held, sems, local = rest[5:]
        gather = Gather(net, held, full, sems, local)
        net.meet()
        for b in range(images):
            partial_rows(scatter.part, b, left_refs, right_refs, False)
            scatter.start(b)
        for b in range(images):
            scatter.cross(b)
        for b in range(images):
            scatter.ready(b)

            def step(s, b=b):
                rows = resid_ref[b, s, :].astype(jnp.float32) + scatter.total(b, s)
                out[b, s, :] = rows
                normed, _ = norm_rows(rows)
                held[b, s, :] = (normed * gain_ref[...]).astype(jnp.bfloat16)

            each_slab(own, step)
            gather.start(b)
        for b in range(images):
            gather.forward(b)
        for b in range(images):
            scatter.finish(b)
            gather.finish(b)

    return pl.pallas_call(
        kernel,
        out_shape=[
            jax.ShapeDtypeStruct((images, own, width), jnp.float32),
            jax.ShapeDtypeStruct((images, 4 * own, width), jnp.bfloat16),
        ],
        in_specs=[VM] * (2 * count + 2),
        out_specs=[VM, HB],
        scratch_shapes=scatter_scratch(images, own, width) + gather_scratch(images, own, width),
        compiler_params=params(number, 40),
        name="forward_rows",
    )(*lefts, *rights, resid, gain)


def backward_rows(lefts, rights, above, rows_in, gain, number, masks=None, gathered=True):
    images, own, width = rows_in.shape
    count = len(lefts)
    extra = [] if masks is None else [masks]

    def kernel(*refs):
        left_refs, right_refs = refs[:count], refs[count : 2 * count]
        above_ref, rows_ref, gain_ref = refs[2 * count : 2 * count + 3]
        refs = refs[2 * count + 3 :]
        mask_ref = None
        if masks is not None:
            mask_ref, refs = refs[0], refs[1:]
        out, gain_out = refs[:2]
        refs = refs[2:]
        if gathered:
            full, refs = refs[0], refs[1:]
        net = Narrow()
        scatter = Scatter(net, *refs[:5])
        if gathered:
            held, sems, local = refs[5:]
            gather = Gather(net, held, full, sems, local)
        net.meet()
        for b in range(images):
            partial_rows(scatter.part, b, left_refs, right_refs, True)
            scatter.start(b)
        gain_out[...] = jnp.zeros_like(gain_out)
        for b in range(images):
            scatter.cross(b)
        for b in range(images):
            scatter.ready(b)

            def step(s, b=b):
                d_hidden = scatter.total(b, s)
                normed, inv_std = norm_rows(rows_ref[b, s, :].astype(jnp.float32))
                gain_out[...] += jnp.sum(d_hidden * normed, axis=0, keepdims=True)
                top = above_ref[b, s, :].astype(jnp.float32)
                if mask_ref is not None:
                    top = top * mask_ref[b, s, :]
                scaled = d_hidden * gain_ref[...]
                inner = scaled - jnp.mean(scaled, axis=-1, keepdims=True)
                inner = inner - normed * jnp.mean(scaled * normed, axis=-1, keepdims=True)
                d_rows = top + inv_std * inner
                out[b, s, :] = d_rows.astype(out.dtype)
                if gathered:
                    held[b, s, :] = d_rows.astype(jnp.bfloat16)

            each_slab(own, step)
            if gathered:
                gather.start(b)
        if gathered:
            for b in range(images):
                gather.forward(b)
        for b in range(images):
            scatter.finish(b)
            if gathered:
                gather.finish(b)

    out_shape = [
        jax.ShapeDtypeStruct((images, own, width), jnp.float32 if gathered else jnp.bfloat16),
        jax.ShapeDtypeStruct((1, width), jnp.float32),
    ]
    out_specs = [VM, VM]
    scratch = scatter_scratch(images, own, width)
    if gathered:
        out_shape.append(jax.ShapeDtypeStruct((images, 4 * own, width), jnp.bfloat16))
        out_specs.append(HB)
        scratch += gather_scratch(images, own, width)
    return pl.pallas_call(
        kernel,
        out_shape=out_shape,
        in_specs=[VM] * (2 * count + 3 + len(extra)),
        out_specs=out_specs,
        scratch_shapes=scratch,
        compiler_params=params(number, 48),
        name="backward_rows",
    )(*lefts, *rights, above, rows_in, gain, *extra)


def wide_sum(arrays, dims, wide, order=None, z_first=3, ahead=2):
    Z = wide // 2
    units = []
    shapes = []
    for a, (arr, dim) in enumerate(zip(arrays, dims)):
        if dim == 0:
            blk = arr.shape[0] // wide
            n = arr.shape[1] // 512
            shapes.append((blk, arr.shape[1]))
        else:
            blk = arr.shape[1] // wide
            n = arr.shape[0] // 512
            shapes.append((arr.shape[0], blk))
        for c in range(n):
            units.append((a, dim, c, blk))
    if order is not None:
        units = [units[i] for i in order]
    blk = units[0][3]
    shp = [(blk, 512), (512, blk)]
    U = len(units)
    zset = set(int((k + 0.5) * U / z_first) for k in range(z_first)) if z_first else set()
    yf = [u for k, u in enumerate(units) if k not in zset]
    zf = [u for k, u in enumerate(units) if k in zset]
    cnt = {}
    def slot(key):
        cnt[key] = cnt.get(key, 0) + 1
        return cnt[key] - 1
    yslots = [slot(("y", u[1])) for u in yf]
    zslots = [slot(("z", u[1])) for u in zf]
    ny = [max(1, cnt.get(("y", d), 0)) for d in (0, 1)]
    nz = [max(1, cnt.get(("z", d), 0)) for d in (0, 1)]
    OWN = 3

    def kernel(*refs):
        ins = refs[: len(arrays)]
        outs = refs[len(arrays): 2 * len(arrays)]
        (S0, S1, R0, R1, L0, L1, O0, O1, T0, T1, ZR0, ZR1, ZL0, ZL1, YB0, YB1, F0, F1,
         ysend, yrecv, own_sem, rsend, rrecv, lsend, lrecv,
         tsem, zrsend, zrrecv, zlsend, zlrecv, ybsend, ybrecv, out_sem) = refs[2 * len(arrays):]
        S, R, L, O, T, ZR, ZL, YB, F = ((S0, S1), (R0, R1), (L0, L1), (O0, O1), (T0, T1), (ZR0, ZR1), (ZL0, ZL1), (YB0, YB1), (F0, F1))
        me = lax.axis_index("wide")
        z = me // 2
        y = me % 2
        yp = {"wide": z * 2 + (1 - y)}
        zr = {"wide": jnp.minimum(z + 1, Z - 1) * 2 + y}
        zl = {"wide": jnp.maximum(z - 1, 0) * 2 + y}
        has_r = z < Z - 1
        has_l = z > 0
        bar = pltpu.get_barrier_semaphore()
        pl.semaphore_signal(bar, inc=1, device_id=yp, device_id_type=MESH)
        @pl.when(has_r)
        def _():
            pl.semaphore_signal(bar, inc=1, device_id=zr, device_id_type=MESH)
        @pl.when(has_l)
        def _():
            pl.semaphore_signal(bar, inc=1, device_id=zl, device_id_type=MESH)
        pl.semaphore_wait(bar, 1 + has_r.astype(jnp.int32) + has_l.astype(jnp.int32))

        def block(u, w):
            a, dim, c, b = u
            start = pl.multiple_of(w * b, b)
            if dim == 0:
                return ins[a].at[pl.ds(start, b), pl.ds(c * 512, 512)]
            return ins[a].at[pl.ds(c * 512, 512), pl.ds(start, b)]

        def outblock(u):
            a, dim, c, b = u
            if dim == 0:
                return outs[a].at[:, pl.ds(c * 512, 512)]
            return outs[a].at[pl.ds(c * 512, 512), :]

        def addto(dst, src):
            rows = dst.shape[0]
            step = min(rows, 64)
            def body(i, _):
                s = pl.ds(pl.multiple_of(i * step, step), step)
                dst[s, :] = dst[s, :] + src[s, :]
                return 0
            lax.fori_loop(0, rows // step, body, 0)

        def rc(src, dst, ss, rs, dev):
            return pltpu.make_async_remote_copy(src_ref=src, dst_ref=dst, send_sem=ss, recv_sem=rs, device_id=dev, device_id_type=MESH)

        def ycopy(i, k):
            u, s = yf[i], yslots[i]
            return rc(block(u, k * 2 + (1 - y)), S[u[1]].at[s, k], ysend.at[i, k], yrecv.at[i, k], yp)
        def ocopy(i, k):
            u = yf[i]
            return pltpu.make_async_copy(block(u, k * 2 + y), O[u[1]].at[i % OWN, k], own_sem.at[i % OWN, k])
        korder = [0, Z - 1] + list(range(1, Z - 1))
        def ystart(i):
            for k in korder:
                ycopy(i, k).start()
        def ostart(i):
            for k in korder:
                ocopy(i, k).start()
        def yadd(i):
            u, s = yf[i], yslots[i]
            for k in korder:
                ycopy(i, k).wait_recv()
                ocopy(i, k).wait()
                addto(S[u[1]].at[s, k], O[u[1]].at[i % OWN, k])

        def rcopy(i, t):
            u, s = yf[i], yslots[i]
            d = Z - t + z
            return rc(S[u[1]].at[s, jnp.clip(d, 0, Z - 1)], R[u[1]].at[s, t - 1], rsend.at[i, t - 1], rrecv.at[i, t - 1], zr)
        def lcopy(i, t):
            u, s = yf[i], yslots[i]
            d = t - Z + z
            return rc(S[u[1]].at[s, jnp.clip(d, 0, Z - 1)], L[u[1]].at[s, t - 1], lsend.at[i, t - 1], lrecv.at[i, t - 1], zl)
        def chain(i, t):
            u, s = yf[i], yslots[i]
            kd = u[1]
            @pl.when(has_r & (t >= z + 1))
            def _():
                if t > 1:
                    @pl.when(has_l & (t - 1 >= z))
                    def _():
                        rcopy(i, t - 1).wait_recv()
                        addto(S[kd].at[s, jnp.clip(Z - t + z, 0, Z - 1)], R[kd].at[s, t - 2])
                rcopy(i, t).start()
            zb = Z - 1 - z
            @pl.when(has_l & (t >= zb + 1))
            def _():
                if t > 1:
                    @pl.when(has_r & (t - 1 >= zb))
                    def _():
                        lcopy(i, t - 1).wait_recv()
                        addto(S[kd].at[s, jnp.clip(t - Z + z, 0, Z - 1)], L[kd].at[s, t - 2])
                lcopy(i, t).start()
        nfin = [0]
        def emit(u, get):
            f = nfin[0]
            nfin[0] += 1
            q = f % 2
            if f >= 2:
                pu = emitted[f - 2]
                pltpu.make_async_copy(F[pu[1]].at[q], outblock(pu), out_sem.at[q]).wait()
            get(F[u[1]].at[q])
            pltpu.make_async_copy(F[u[1]].at[q], outblock(u), out_sem.at[q]).start()
            emitted.append(u)
        emitted = []
        def final(i):
            u, s = yf[i], yslots[i]
            kd = u[1]
            @pl.when(has_l)
            def _():
                rcopy(i, Z - 1).wait_recv()
                addto(S[kd].at[s, z], R[kd].at[s, Z - 2])
            @pl.when(has_r)
            def _():
                lcopy(i, Z - 1).wait_recv()
                addto(S[kd].at[s, z], L[kd].at[s, Z - 2])
            def get(dst):
                dst[...] = S[kd][s, z]
            emit(u, get)

        def tcopy(j, w):
            u, s = zf[j], zslots[j]
            return pltpu.make_async_copy(block(u, w), T[u[1]].at[s, w // 2, w % 2], tsem.at[j, w])
        def zrcopy(j, t):
            u, s = zf[j], zslots[j]
            d = Z - t + z
            return rc(T[u[1]].at[s, jnp.clip(d, 0, Z - 1)], ZR[u[1]].at[s, t - 1], zrsend.at[j, t - 1], zrrecv.at[j, t - 1], zr)
        def zlcopy(j, t):
            u, s = zf[j], zslots[j]
            d = t - Z + z
            return rc(T[u[1]].at[s, jnp.clip(d, 0, Z - 1)], ZL[u[1]].at[s, t - 1], zlsend.at[j, t - 1], zlrecv.at[j, t - 1], zl)
        def zchain(j, t):
            u, s = zf[j], zslots[j]
            kd = u[1]
            if t == 1:
                for w in range(wide):
                    tcopy(j, w).wait()
            @pl.when(has_r & (t >= z + 1))
            def _():
                if t > 1:
                    @pl.when(has_l & (t - 1 >= z))
                    def _():
                        zrcopy(j, t - 1).wait_recv()
                        for q in range(2):
                            addto(T[kd].at[s, jnp.clip(Z - t + z, 0, Z - 1), q], ZR[kd].at[s, t - 2, q])
                zrcopy(j, t).start()
            zb = Z - 1 - z
            @pl.when(has_l & (t >= zb + 1))
            def _():
                if t > 1:
                    @pl.when(has_r & (t - 1 >= zb))
                    def _():
                        zlcopy(j, t - 1).wait_recv()
                        for q in range(2):
                            addto(T[kd].at[s, jnp.clip(t - Z + z, 0, Z - 1), q], ZL[kd].at[s, t - 2, q])
                zlcopy(j, t).start()
        def ybcopy(j):
            u, s = zf[j], zslots[j]
            return rc(T[u[1]].at[s, z, 1 - y], YB[u[1]].at[s], ybsend.at[j], ybrecv.at[j], yp)
        def zfold(j):
            u, s = zf[j], zslots[j]
            kd = u[1]
            @pl.when(has_l)
            def _():
                zrcopy(j, Z - 1).wait_recv()
                for q in range(2):
                    addto(T[kd].at[s, z, q], ZR[kd].at[s, Z - 2, q])
            @pl.when(has_r)
            def _():
                zlcopy(j, Z - 1).wait_recv()
                for q in range(2):
                    addto(T[kd].at[s, z, q], ZL[kd].at[s, Z - 2, q])
            ybcopy(j).start()
        def zfinal(j):
            u, s = zf[j], zslots[j]
            kd = u[1]
            ybcopy(j).wait_recv()
            def get(dst):
                dst[...] = T[kd][s, z, y] + YB[kd][s]
            emit(u, get)

        NY, NZ = len(yf), len(zf)
        for i in range(min(ahead, NY)):
            ystart(i)
        for j in range(NZ):
            for w in range(wide):
                tcopy(j, w).start()
        for i in range(min(2, NY)):
            ostart(i)
        gap = max(2, NY // max(NZ, 1))
        zev = {}
        for j in range(NZ):
            b = j * gap
            for t in range(1, Z):
                zev.setdefault(b + 1 * (t - 1), []).append(("c", j, t))
            zev.setdefault(b + (Z - 1), []).append(("f", j, 0))
            zev.setdefault(b + (Z - 1) + 1, []).append(("e", j, 0))
        last = max([NY + Z] + [k + 1 for k in zev])
        for k in range(last):
            for ev in zev.get(k, []):
                if ev[0] == "c":
                    zchain(ev[1], ev[2])
                elif ev[0] == "f":
                    zfold(ev[1])
                else:
                    zfinal(ev[1])
            if k < NY:
                if k + ahead < NY:
                    ystart(k + ahead)
                if k + 2 < NY:
                    ostart(k + 2)
                yadd(k)
            for t in range(1, Z):
                i = k - (t - 1)
                if 0 <= i < NY:
                    chain(i, t)
            i = k - (Z - 1)
            if 0 <= i < NY:
                final(i)
        nf = nfin[0]
        for f in range(max(0, nf - 2), nf):
            u = emitted[f]
            pltpu.make_async_copy(F[u[1]].at[f % 2], outblock(u), out_sem.at[f % 2]).wait()
        for i in range(NY):
            for k in range(Z):
                ycopy(i, k).wait_send()
            for t in range(1, Z):
                @pl.when(has_r & (t >= z + 1))
                def _():
                    rcopy(i, t).wait_send()
                @pl.when(has_l & (t >= Z - z))
                def _():
                    lcopy(i, t).wait_send()
        for j in range(NZ):
            for t in range(1, Z):
                @pl.when(has_r & (t >= z + 1))
                def _():
                    zrcopy(j, t).wait_send()
                @pl.when(has_l & (t >= Z - z))
                def _():
                    zlcopy(j, t).wait_send()
            ybcopy(j).wait_send()

    bf = jnp.bfloat16
    V = pltpu.VMEM
    DS = pltpu.SemaphoreType.DMA
    sc = []
    for d in (0, 1): sc.append(V((ny[d], Z) + shp[d], bf))
    for _ in range(2):
        for d in (0, 1): sc.append(V((ny[d], Z - 1) + shp[d], bf))
    for d in (0, 1): sc.append(V((OWN, Z) + shp[d], bf))
    for d in (0, 1): sc.append(V((nz[d], Z, 2) + shp[d], bf))
    for _ in range(2):
        for d in (0, 1): sc.append(V((nz[d], Z - 1, 2) + shp[d], bf))
    for d in (0, 1): sc.append(V((nz[d],) + shp[d], bf))
    for d in (0, 1): sc.append(V((2,) + shp[d], bf))
    NY, NZ = len(yf), max(1, len(zf))
    sc += [DS((NY, Z)), DS((NY, Z)), DS((OWN, Z))] + [DS((NY, Z - 1))] * 4
    sc += [DS((NZ, wide))] + [DS((NZ, Z - 1))] * 4 + [DS((NZ,)), DS((NZ,)), DS((2,))]
    return pl.pallas_call(
        kernel,
        out_shape=[jax.ShapeDtypeStruct(s, bf) for s in shapes],
        in_specs=[pl.BlockSpec(memory_space=pl.ANY)] * len(arrays),
        out_specs=[pl.BlockSpec(memory_space=pl.ANY)] * len(arrays),
        scratch_shapes=sc,
        compiler_params=pltpu.CompilerParams(collective_id=0, has_side_effects=True, vmem_limit_bytes=63 * 1024 * 1024),
        name="wide_sum",
    )(*arrays)


def local(
    tokens,
    caption,
    token_mask,
    cotangent,
    gain_self,
    gain_cross,
    gain_feed,
    text_proj,
    query_self,
    key_self,
    value_self,
    out_self,
    query_cross,
    key_cross,
    value_cross,
    out_cross,
    up_proj,
    down_proj,
):
    gain_one = gain_self.astype(jnp.float32)[None]
    gain_two = gain_cross.astype(jnp.float32)[None]
    gain_three = gain_feed.astype(jnp.float32)[None]
    low = jnp.bfloat16

    image_self = open_rows(tokens, gain_one, 1)
    query_sa = times_weight(image_self, query_self).astype(low)
    keys_sa = times_weight(image_self, key_self).astype(low)
    values_sa = times_weight(image_self, value_self).astype(low)
    attended_sa, total_sa = attend(query_sa, keys_sa, values_sa)
    resid_mid, image_cross = forward_rows([attended_sa], [out_self], tokens, gain_two, 2)
    context = text_total(times_weight(caption, text_proj)).astype(low)
    keys_ca = times_weight(context, key_cross).astype(low)
    values_ca = times_weight(context, value_cross).astype(low)
    query_ca = times_weight(image_cross, query_cross).astype(low)
    attended_ca, total_ca = attend(query_ca, keys_ca, values_ca)
    resid_late, image_feed = forward_rows([attended_ca], [out_cross], resid_mid, gain_three, 3)
    marks = token_mask[:, :, None].astype(jnp.float32)
    d_image = group_rows((cotangent.astype(jnp.float32) * marks).astype(low))
    pre_act = times_weight(image_feed, up_proj)
    gelu_out, gelu_pull = jax.vjp(jax.nn.gelu, pre_act)
    activ = gelu_out.astype(low)
    resid_out = resid_late + feed_back(times_weight(activ, down_proj))
    d_pre = gelu_pull(against(d_image, down_proj))[0].astype(low)
    part_down = contract(activ, d_image)
    part_up = contract(image_feed, d_pre)
    d_late, part_gain_feed, d_image_cross = backward_rows(
        [d_pre], [up_proj], cotangent, resid_late, gain_three, 4, masks=marks
    )
    part_out_cross = contract(attended_ca, d_image_cross)
    d_attended_ca = against(d_image_cross, out_cross).astype(low)
    d_query_ca, d_keys_ca, d_values_ca = attend_back(
        query_ca, keys_ca, values_ca, total_ca, d_attended_ca
    )
    part_query_cross = contract(image_cross, d_query_ca)
    part_key_cross = contract(context, d_keys_ca)
    part_value_cross = contract(context, d_values_ca)
    d_mid, part_gain_cross, d_image_self = backward_rows(
        [d_query_ca], [query_cross], d_late, resid_mid, gain_two, 5
    )
    d_context = text_total(against(d_keys_ca, key_cross) + against(d_values_ca, value_cross))
    d_context = d_context.astype(low)
    part_text = contract(caption, d_context)
    d_words = against(d_context, text_proj).astype(low)
    part_out_self = contract(attended_sa, d_image_self)
    d_attended_sa = against(d_image_self, out_self).astype(low)
    d_query_sa, d_keys_sa, d_values_sa = attend_back(
        query_sa, keys_sa, values_sa, total_sa, d_attended_sa
    )
    part_query_self = contract(image_self, d_query_sa)
    part_key_self = contract(image_self, d_keys_sa)
    part_value_self = contract(image_self, d_values_sa)
    d_input, part_gain_self = backward_rows(
        [d_query_sa, d_keys_sa, d_values_sa],
        [query_self, key_self, value_self],
        d_mid,
        tokens,
        gain_one,
        6,
        gathered=False,
    )
    parts = (
        part_text,
        part_query_self,
        part_key_self,
        part_value_self,
        part_out_self,
        part_query_cross,
        part_key_cross,
        part_value_cross,
        part_out_cross,
        part_up,
        part_down,
    )
    dims = (1, 0, 0, 0, 1, 0, 0, 0, 1, 0, 1)
    wide = lax.axis_size("wide")
    if wide % 2 == 0 and 4 <= wide <= 8:
        summed = wide_sum(parts, dims, wide)
    else:
        summed = [
            lax.psum_scatter(part, "wide", scatter_dimension=dim, tiled=True)
            for part, dim in zip(parts, dims)
        ]
    gains = lax.psum((part_gain_self[0], part_gain_cross[0], part_gain_feed[0]), ("wide", "narrow"))
    return (
        resid_out.astype(low),
        d_input,
        d_words,
        *gains,
        *[part.astype(jnp.float32) for part in summed],
    )


def solution(mesh):
    in_specs = (
        P("wide", "narrow", None),
        P("wide", None, "narrow"),
        P("wide", "narrow"),
        P("wide", "narrow", None),
        P(),
        P(),
        P(),
        P("narrow", None),
        P(None, "narrow"),
        P(None, "narrow"),
        P(None, "narrow"),
        P("narrow", None),
        P(None, "narrow"),
        P(None, "narrow"),
        P(None, "narrow"),
        P("narrow", None),
        P(None, "narrow"),
        P("narrow", None),
    )
    out_specs = (
        P("wide", "narrow", None),
        P("wide", "narrow", None),
        P("wide", None, "narrow"),
        P(),
        P(),
        P(),
        P("narrow", "wide"),
        P("wide", "narrow"),
        P("wide", "narrow"),
        P("wide", "narrow"),
        P("narrow", "wide"),
        P("wide", "narrow"),
        P("wide", "narrow"),
        P("wide", "narrow"),
        P("narrow", "wide"),
        P("wide", "narrow"),
        P("narrow", "wide"),
    )
    return jax.shard_map(local, mesh=mesh, in_specs=in_specs, out_specs=out_specs, check_vma=False)
```

```python
import math
import types

import jax
import jax.numpy as jnp
from jax import lax
from jax.experimental import pallas as pl
from jax.experimental.pallas import tpu as pltpu
from jax.sharding import PartitionSpec as P

HEAD = 128
MESH = pl.DeviceIdType.MESH
WIDE, NARROW = "wide", "narrow"
LOW, F32 = jnp.bfloat16, jnp.float32
LAST, FIRST = (((1,), (1,)), ((), ())), (((0,), (0,)), ((), ()))

def normalize(rows):
    centre = jnp.mean(rows, axis=-1, keepdims=True)
    centred = rows - centre
    variance = jnp.mean(centred * centred, axis=-1, keepdims=True)
    inv_std = lax.rsqrt(variance + 1e-05)
    return (centred * inv_std, inv_std)


def norm_back(d_normed, normed, inv_std):
    inner = d_normed - jnp.mean(d_normed, axis=-1, keepdims=True)
    inner = inner - normed * jnp.mean(d_normed * normed, axis=-1, keepdims=True)
    return inv_std * inner


def times_weight(left, right):
    return jnp.dot(left, right, preferred_element_type=jnp.float32)


def split_heads(matrix):
    return matrix.reshape(matrix.shape[0], matrix.shape[1], matrix.shape[2] // HEAD, HEAD)


def join_heads(heads):
    return heads.reshape(heads.shape[0], heads.shape[1], heads.shape[2] * HEAD)


def head_scores(query, keys):
    scores = jnp.einsum(
        "bqhe,bkhe->bhqk", split_heads(query), split_heads(keys), preferred_element_type=jnp.float32
    )
    return scores * (1.0 / math.sqrt(HEAD))


def attend(query, keys, values):
    scores = head_scores(query, keys)
    peak = jnp.max(scores, axis=-1, keepdims=True)
    powers = jnp.exp(scores - peak)
    summed = jnp.sum(powers, axis=-1, keepdims=True)
    low_probs = (powers / summed).astype(jnp.bfloat16)
    attended = jnp.einsum(
        "bhqk,bkhe->bqhe", low_probs, split_heads(values), preferred_element_type=jnp.float32
    )
    return join_heads(attended).astype(jnp.bfloat16), peak + jnp.log(summed)


def attend_back(query, keys, values, log_total, d_attended):
    probs = jnp.exp(head_scores(query, keys) - log_total)
    low_probs = probs.astype(jnp.bfloat16)
    d_heads = split_heads(d_attended)
    d_probs = jnp.einsum(
        "bqhe,bkhe->bhqk", d_heads, split_heads(values), preferred_element_type=jnp.float32
    )
    d_values = jnp.einsum("bhqk,bqhe->bkhe", low_probs, d_heads, preferred_element_type=jnp.float32)
    weighted = jnp.sum(probs * d_probs, axis=-1, keepdims=True)
    d_scores = (probs * (d_probs - weighted)).astype(jnp.bfloat16)
    scale = 1.0 / math.sqrt(HEAD)
    d_query = (
        jnp.einsum("bhqk,bkhe->bqhe", d_scores, split_heads(keys), preferred_element_type=jnp.float32)
        * scale
    )
    d_keys = (
        jnp.einsum("bhqk,bqhe->bkhe", d_scores, split_heads(query), preferred_element_type=jnp.float32)
        * scale
    )
    return tuple(join_heads(d).astype(jnp.bfloat16) for d in (d_query, d_keys, d_values))


def contract(left, right):
    return lax.dot_general(
        left, right, (((0, 1), (0, 1)), ((), ())), preferred_element_type=jnp.float32
    ).astype(jnp.bfloat16)


def against(left, right):
    return lax.dot_general(
        left, right, (((2,), (1,)), ((), ())), preferred_element_type=jnp.float32
    )


def group_rows(piece):
    return lax.all_gather(piece, NARROW, axis=1, tiled=True)


def own_rows(partial):
    return lax.psum_scatter(partial, NARROW, scatter_dimension=1, tiled=True)


def feed_back(partial):
    return own_rows(partial.astype(jnp.bfloat16)).astype(jnp.float32)


def text_total(partial):
    return lax.psum(partial, NARROW)


def by_collectives(
    tokens,
    caption,
    token_mask,
    cotangent,
    gain_self,
    gain_cross,
    gain_feed,
    text_proj,
    query_self,
    key_self,
    value_self,
    out_self,
    query_cross,
    key_cross,
    value_cross,
    out_cross,
    up_proj,
    down_proj,
):
    gain_one = gain_self.astype(jnp.float32)
    gain_two = gain_cross.astype(jnp.float32)
    gain_three = gain_feed.astype(jnp.float32)
    low = jnp.bfloat16

    resid_in = tokens.astype(jnp.float32)
    normed_self, inv_self = normalize(resid_in)
    image_self = group_rows((normed_self * gain_one).astype(low))
    query_sa = times_weight(image_self, query_self).astype(low)
    keys_sa = times_weight(image_self, key_self).astype(low)
    values_sa = times_weight(image_self, value_self).astype(low)
    attended_sa, total_sa = attend(query_sa, keys_sa, values_sa)
    resid_mid = resid_in + own_rows(times_weight(attended_sa, out_self))
    context = text_total(times_weight(caption, text_proj)).astype(low)
    keys_ca = times_weight(context, key_cross).astype(low)
    values_ca = times_weight(context, value_cross).astype(low)
    normed_cross, inv_cross = normalize(resid_mid)
    image_cross = group_rows((normed_cross * gain_two).astype(low))
    query_ca = times_weight(image_cross, query_cross).astype(low)
    attended_ca, total_ca = attend(query_ca, keys_ca, values_ca)
    resid_late = resid_mid + own_rows(times_weight(attended_ca, out_cross))
    normed_feed, inv_feed = normalize(resid_late)
    d_result = cotangent.astype(jnp.float32) * token_mask[:, :, None].astype(jnp.float32)
    d_image = group_rows(d_result.astype(low))
    image_feed = group_rows((normed_feed * gain_three).astype(low))
    pre_act = times_weight(image_feed, up_proj)
    gelu_out, gelu_pull = jax.vjp(jax.nn.gelu, pre_act)
    activ = gelu_out.astype(low)
    resid_out = resid_late + feed_back(times_weight(activ, down_proj))
    d_pre = gelu_pull(against(d_image, down_proj))[0].astype(low)
    part_down = contract(activ, d_image)
    part_up = contract(image_feed, d_pre)
    d_hidden_feed = feed_back(against(d_pre, up_proj))
    part_gain_feed = jnp.sum(d_hidden_feed * normed_feed, axis=(0, 1))
    d_late = d_result + norm_back(d_hidden_feed * gain_three, normed_feed, inv_feed)
    d_image_cross = group_rows(d_late.astype(low))
    part_out_cross = contract(attended_ca, d_image_cross)
    d_attended_ca = against(d_image_cross, out_cross).astype(low)
    d_query_ca, d_keys_ca, d_values_ca = attend_back(
        query_ca, keys_ca, values_ca, total_ca, d_attended_ca
    )
    part_query_cross = contract(image_cross, d_query_ca)
    part_key_cross = contract(context, d_keys_ca)
    part_value_cross = contract(context, d_values_ca)
    d_hidden_cross = own_rows(against(d_query_ca, query_cross))
    d_context = text_total(against(d_keys_ca, key_cross) + against(d_values_ca, value_cross))
    d_context = d_context.astype(low)
    part_text = contract(caption, d_context)
    d_words = against(d_context, text_proj).astype(low)
    part_gain_cross = jnp.sum(d_hidden_cross * normed_cross, axis=(0, 1))
    d_mid = d_late + norm_back(d_hidden_cross * gain_two, normed_cross, inv_cross)
    d_image_self = group_rows(d_mid.astype(low))
    part_out_self = contract(attended_sa, d_image_self)
    d_attended_sa = against(d_image_self, out_self).astype(low)
    d_query_sa, d_keys_sa, d_values_sa = attend_back(
        query_sa, keys_sa, values_sa, total_sa, d_attended_sa
    )
    part_query_self = contract(image_self, d_query_sa)
    part_key_self = contract(image_self, d_keys_sa)
    part_value_self = contract(image_self, d_values_sa)
    d_hidden_self = own_rows(
        against(d_query_sa, query_self)
        + against(d_keys_sa, key_self)
        + against(d_values_sa, value_self)
    )
    part_gain_self = jnp.sum(d_hidden_self * normed_self, axis=(0, 1))
    d_input = d_mid + norm_back(d_hidden_self * gain_one, normed_self, inv_self)
    parts = (
        part_text,
        part_query_self,
        part_key_self,
        part_value_self,
        part_out_self,
        part_query_cross,
        part_key_cross,
        part_value_cross,
        part_out_cross,
        part_up,
        part_down,
    )
    dims = (1, 0, 0, 0, 1, 0, 0, 0, 1, 0, 1)
    summed = [
        lax.psum_scatter(part, WIDE, scatter_dimension=dim, tiled=True)
        for part, dim in zip(parts, dims)
    ]
    gains = lax.psum((part_gain_self, part_gain_cross, part_gain_feed), (WIDE, NARROW))
    return (
        resid_out.astype(low),
        d_input.astype(low),
        d_words,
        *gains,
        *[part.astype(jnp.float32) for part in summed],
    )


RING = 6
HELD = 7


def send(src, dst, sems, index, peer):
    return pltpu.make_async_remote_copy(
        src_ref=src,
        dst_ref=dst,
        send_sem=sems.at[(0,) + index],
        recv_sem=sems.at[(1,) + index],
        device_id=peer,
        device_id_type=MESH,
    )


def greet(barrier, peer):
    pl.semaphore_signal(barrier, inc=1, device_id=peer, device_id_type=MESH)


def each_slab(count, step, slab=16):
    def body(i, carry):
        step(pl.ds(pl.multiple_of(i * slab, slab), slab))
        return carry

    lax.fori_loop(0, count // slab, body, 0)


class Wide:
    def __init__(self, pairs, units, refs):
        (self.mine, self.theirs, self.fromy, self.right, self.left, self.stage,
         self.aslot, self.bslot, self.ysem, self.rsem, self.lsem, self.asem, self.bsem,
         self.osem, self.rfree, self.lfree) = refs
        self.pairs, self.units = pairs, units
        me = lax.axis_index(WIDE)
        self.z, self.y = me // 2, me % 2
        self.has_right, self.has_left = self.z < pairs - 1, self.z > 0
        self.peer = {WIDE: self.z * 2 + 1 - self.y}
        self.next = {WIDE: jnp.minimum(self.z + 1, pairs - 1) * 2 + self.y}
        self.last = {WIDE: jnp.maximum(self.z - 1, 0) * 2 + self.y}
        self.summed = [i for i, unit in enumerate(units) if not unit.trade]
        group = -1
        for i, unit in enumerate(units):
            if i == 0 or unit.rows is not units[i - 1].rows:
                group += 1
            unit.group = group
        self.blk, self.cols = self.mine.shape[2], self.mine.shape[3]

    def meet(self, barrier):
        greet(barrier, self.peer)

        @pl.when(self.has_right)
        def _():
            greet(barrier, self.next)

        @pl.when(self.has_left)
        def _():
            greet(barrier, self.last)

        return 1 + self.has_right.astype(jnp.int32) + self.has_left.astype(jnp.int32)

    def trade(self, i):
        unit = self.units[i]
        return send(unit.columns, unit.nb_columns, unit.sems, (i,), self.peer)

    def loads(self, i):
        unit = self.units[i]
        s, rows = unit.group % 2, unit.count
        copies = []
        if i == 0 or self.units[i - 1].group != unit.group:
            for k in range(self.pairs):
                for part in (0, 1):
                    if part == 0 or not unit.trade:
                        at = (k * 2 + (self.y if part == 0 else 1 - self.y)) * self.blk
                        src = unit.rows.at[:, pl.ds(pl.multiple_of(at, self.blk), self.blk)]
                    else:
                        src = unit.nb_rows.at[:, pl.ds(k * self.blk, self.blk)]
                    copies.append(
                        pltpu.make_async_copy(
                            src, self.aslot.at[s, part, k, pl.ds(0, rows)], self.asem.at[s, part, k]
                        )
                    )
        q = i % 2
        copies.append(
            pltpu.make_async_copy(
                unit.columns, self.bslot.at[q, 0, pl.ds(0, rows)], self.bsem.at[q, 0]
            )
        )
        if unit.trade:
            copies.append(
                pltpu.make_async_copy(
                    unit.nb_columns, self.bslot.at[q, 1, pl.ds(0, rows)], self.bsem.at[q, 1]
                )
            )
        return copies

    def load(self, i):
        unit = self.units[i]
        if unit.trade:
            self.trade(i).wait_recv()
            if unit.halves is not None and (i == 0 or self.units[i - 1].group != unit.group):
                unit.halves.arrive()
        for copy in self.loads(i):
            copy.start()

    def y_copy(self, i, k):
        n = self.summed.index(i)
        return send(self.theirs.at[n % 2, k], self.fromy.at[n, k], self.ysem, (n, k), self.peer)

    def compute(self, i):
        unit = self.units[i]
        s, q, g, rows = unit.group % 2, i % 2, i % HELD, unit.count
        for copy in self.loads(i):
            copy.wait()
        if i >= HELD:
            self.sent(i - HELD)
        if not unit.trade:
            n = self.summed.index(i)
            if n >= 2:
                for k in range(self.pairs):
                    self.y_copy(self.summed[n - 2], k).wait_send()

            def far(k, carry):
                self.theirs[n % 2, k] = lax.dot_general(
                    self.aslot[s, 1, k, :rows], self.bslot[q, 0, :rows], FIRST,
                    preferred_element_type=F32,
                ).astype(LOW)
                return carry

            lax.fori_loop(0, self.pairs, far, 0)
            for k in range(self.pairs):
                self.y_copy(i, k).start()

        def near(k, carry):
            total = lax.dot_general(
                self.aslot[s, 0, k, :rows], self.bslot[q, 0, :rows], FIRST,
                preferred_element_type=F32,
            )
            if unit.trade:
                total = total + lax.dot_general(
                    self.aslot[s, 1, k, :rows], self.bslot[q, 1, :rows], FIRST,
                    preferred_element_type=F32,
                )
            self.mine[g, k] = total.astype(LOW)
            return carry

        lax.fori_loop(0, self.pairs, near, 0)

    def add(self, dst, src):
        def step(s):
            dst[s, :] = dst[s, :] + src[s, :]

        each_slab(self.blk, step, 64)

    def y_add(self, i):
        n = self.summed.index(i)
        for k in range(self.pairs):
            self.y_copy(i, k).wait_recv()
            self.add(self.mine.at[i % HELD, k], self.fromy.at[n, k])

    def r_copy(self, i, t):
        d = jnp.clip(self.pairs - t + self.z, 0, self.pairs - 1)
        return send(self.mine.at[i % HELD, d], self.right.at[i % RING, t - 1], self.rsem, (i, t - 1), self.next)

    def l_copy(self, i, t):
        d = jnp.clip(t - self.pairs + self.z, 0, self.pairs - 1)
        return send(self.mine.at[i % HELD, d], self.left.at[i % RING, t - 1], self.lsem, (i, t - 1), self.last)

    def sends_right(self, t):
        return self.has_right & (t >= self.z + 1)

    def sends_left(self, t):
        return self.has_left & (t >= self.pairs - self.z)

    def step(self, i, t):
        g, r = i % HELD, i % RING
        if t == 1 and i >= RING:

            @pl.when(self.has_right)
            def _():
                pl.semaphore_wait(self.rfree, 1)

            @pl.when(self.has_left)
            def _():
                pl.semaphore_wait(self.lfree, 1)

        @pl.when(self.sends_right(t))
        def _():
            if t > 1:

                @pl.when(self.has_left & (t - 1 >= self.z))
                def _():
                    self.r_copy(i, t - 1).wait_recv()
                    d = jnp.clip(self.pairs - t + self.z, 0, self.pairs - 1)
                    self.add(self.mine.at[g, d], self.right.at[r, t - 2])

            self.r_copy(i, t).start()

        @pl.when(self.sends_left(t))
        def _():
            if t > 1:

                @pl.when(self.has_right & (t - 1 >= self.pairs - 1 - self.z))
                def _():
                    self.l_copy(i, t - 1).wait_recv()
                    d = jnp.clip(t - self.pairs + self.z, 0, self.pairs - 1)
                    self.add(self.mine.at[g, d], self.left.at[r, t - 2])

            self.l_copy(i, t).start()

    def out_copy(self, i):
        return pltpu.make_async_copy(self.stage.at[i % 2], self.units[i].out, self.osem.at[i % 2])

    def final(self, i):
        g, r, t = i % HELD, i % RING, self.pairs - 1

        @pl.when(self.has_left)
        def _():
            self.r_copy(i, t).wait_recv()
            self.add(self.mine.at[g, self.z], self.right.at[r, t - 1])

        @pl.when(self.has_right)
        def _():
            self.l_copy(i, t).wait_recv()
            self.add(self.mine.at[g, self.z], self.left.at[r, t - 1])

        if i + RING < len(self.units):

            @pl.when(self.has_left)
            def _():
                pl.semaphore_signal(self.rfree, inc=1, device_id=self.last, device_id_type=MESH)

            @pl.when(self.has_right)
            def _():
                pl.semaphore_signal(self.lfree, inc=1, device_id=self.next, device_id_type=MESH)

        if i >= 2:
            self.out_copy(i - 2).wait()

        def step(s):
            self.stage[i % 2, s, :] = self.mine[g, self.z, s, :]

        each_slab(self.blk, step, 64)
        self.out_copy(i).start()

    def sent(self, i):
        for t in range(1, self.pairs):

            @pl.when(self.sends_right(t))
            def _():
                self.r_copy(i, t).wait_send()

            @pl.when(self.sends_left(t))
            def _():
                self.l_copy(i, t).wait_send()

    def lead(self, i):
        return 1 if self.units[i].trade else 2

    def ask(self, i):
        if i < len(self.units) and self.units[i].trade:
            self.trade(i).start()

    def tick(self, k):
        count, pairs = len(self.units), self.pairs
        due = [i for i in range(count) if max(j - self.lead(j) for j in range(i + 1)) == k]
        for i in due[:1]:
            self.load(i)
        if k >= 0:
            self.ask(k + 4)
        for t in range(pairs - 1, 1, -1):
            if 0 <= k - (t - 1) < count:
                self.step(k - (t - 1), t)
        if 0 <= k < count:
            if not self.units[k].trade:
                self.y_add(k)
            self.step(k, 1)
        if 0 <= k - (pairs - 1) < count:
            self.final(k - (pairs - 1))
        for n, i in enumerate(due):
            if n > 0:
                self.load(i)
            self.compute(i)

    def drain(self):
        count = len(self.units)
        for i in range(max(0, count - 2), count):
            self.out_copy(i).wait()
        for i in range(max(0, count - HELD), count):
            self.sent(i)
        for i in self.summed[-2:]:
            for k in range(self.pairs):
                self.y_copy(i, k).wait_send()
        for i, unit in enumerate(self.units):
            if unit.trade:
                self.trade(i).wait_send()


VM = pl.BlockSpec(memory_space=pltpu.VMEM)
HB = pl.BlockSpec(memory_space=pl.ANY)


def norm_rows(rows):
    centre = jnp.mean(rows, axis=-1, keepdims=True)
    centred = rows - centre
    variance = jnp.mean(centred * centred, axis=-1, keepdims=True)
    inv_std = lax.rsqrt(variance + 1e-05)
    return centred * inv_std, inv_std


class Narrow:
    def __init__(self):
        self.me = lax.axis_index(NARROW)
        x, c = self.me // 2, self.me % 2
        self.core_at = x * 2 + 1 - c
        self.chip_at = (1 - x) * 2 + c
        self.far_at = (1 - x) * 2 + 1 - c
        self.core = {NARROW: self.core_at}
        self.chip = {NARROW: self.chip_at}

    def meet(self, barrier):
        greet(barrier, self.core)
        greet(barrier, self.chip)
        return 2


class Gather:
    def __init__(self, net, full, own, sems):
        self.net, self.full, self.own, self.sems = net, full, own, sems

    def place(self, b, who):
        at = (b * 4 + who) * self.own
        return self.full.at[pl.ds(pl.multiple_of(at, self.own), self.own), :]

    def mine(self, b):
        return self.place(b, self.net.me)

    def to_core(self, b):
        return send(self.mine(b), self.mine(b), self.sems, (b, 0), self.net.core)

    def to_chip(self, b):
        return send(self.mine(b), self.mine(b), self.sems, (b, 1), self.net.chip)

    def onward(self, b):
        block = self.place(b, self.net.chip_at)
        return send(block, block, self.sems, (b, 2), self.net.core)

    def start(self, b):
        self.to_chip(b).start()
        self.to_core(b).start()

    def forward(self, b):
        self.to_chip(b).wait_recv()
        self.onward(b).start()

    def finish(self, b):
        self.to_core(b).wait_recv()
        self.onward(b).wait_recv()
        self.to_core(b).wait_send()
        self.to_chip(b).wait_send()
        self.onward(b).wait_send()


class Scatter:
    def __init__(self, net, part, landed, outgoing, arrived, sems):
        self.net, self.part, self.landed = net, part, landed
        self.outgoing, self.arrived, self.sems = outgoing, arrived, sems
        self.own = part.shape[1] // 4

    def rows(self, b, who):
        return self.part.at[b, pl.ds(pl.multiple_of(who * self.own, self.own), self.own), :]

    def core_copy(self, b, k):
        who = self.net.far_at if k == 0 else self.net.core_at
        return send(self.rows(b, who), self.landed.at[b, k], self.sems, (b, k), self.net.core)

    def chip_copy(self, b):
        return send(self.outgoing.at[b], self.arrived.at[b], self.sems, (b, 2), self.net.chip)

    def start(self, b):
        self.core_copy(b, 0).start()
        self.core_copy(b, 1).start()

    def cross(self, b):
        self.core_copy(b, 0).wait_recv()
        mine = self.rows(b, self.net.chip_at)

        def step(s):
            total = mine[s, :] + self.landed[b, 0, s, :]
            self.outgoing[b, s, :] = total.astype(self.outgoing.dtype)

        each_slab(self.own, step)
        self.chip_copy(b).start()

    def ready(self, b):
        self.core_copy(b, 1).wait_recv()
        self.chip_copy(b).wait_recv()

    def total(self, b, s):
        near = self.rows(b, self.net.me)[s, :] + self.landed[b, 1, s, :]
        return near + self.arrived[b, s, :].astype(F32)

    def finish(self, b):
        self.core_copy(b, 0).wait_send()
        self.core_copy(b, 1).wait_send()
        self.chip_copy(b).wait_send()


class Halves:
    def __init__(self, full, there, pairs, sems, index):
        me = lax.axis_index(WIDE)
        y = me % 2
        blk = full.shape[1] // (2 * pairs)
        peer = {WIDE: me + 1 - 2 * y}
        self.copies = [
            send(
                full.at[:, pl.ds(pl.multiple_of((2 * k + 1 - y) * blk, blk), blk)],
                there.at[:, pl.ds(k * blk, blk)], sems, (index, k), peer,
            )
            for k in range(pairs)
        ]

    def start(self):
        for copy in self.copies:
            copy.start()

    def arrive(self):
        for copy in self.copies:
            copy.wait_recv()

    def leave(self):
        for copy in self.copies:
            copy.wait_send()


def scatter_scratch(images, own, width):
    return [
        pltpu.VMEM((images, 4 * own, width), F32),
        pltpu.VMEM((images, 2, own, width), F32),
        pltpu.VMEM((images, own, width), LOW),
        pltpu.VMEM((images, own, width), LOW),
        pltpu.SemaphoreType.DMA((2, images, 3)),
    ]


def params(number, limit):
    return pltpu.CompilerParams(
        collective_id=number, has_side_effects=True, vmem_limit_bytes=limit * 1024 * 1024
    )


class Copies:
    def __init__(self, sems):
        self.sems, self.used, self.open = sems, 0, []

    def start(self, src, dst):
        copy = pltpu.make_async_copy(src, dst, self.sems.at[self.used])
        self.used += 1
        copy.start()
        return copy

    def later(self, src, dst):
        self.open.append(self.start(src, dst))

    def close(self):
        for copy in self.open:
            copy.wait()


def columns_of(width, step, tile=512):
    def body(j, carry):
        step(pl.ds(pl.multiple_of(j * tile, tile), tile))
        return carry

    lax.fori_loop(0, width // tile, body, 0)


def dot(left, right, dims=(((1,), (0,)), ((), ()))):
    return lax.dot_general(left, right, dims, preferred_element_type=F32)


def softmax_parts(q, k):
    scores = dot(q, k, LAST) * (1.0 / math.sqrt(HEAD))
    powers = jnp.exp(scores - jnp.max(scores, axis=-1, keepdims=True))
    return powers / jnp.sum(powers, axis=-1, keepdims=True)


def head_columns(j):
    return pl.ds(pl.multiple_of(j * HEAD, HEAD), HEAD)


def heads_forward(b, images, query, keys, values, out):
    many, some = query.shape[0] // images, keys.shape[0] // images
    asked, told = pl.ds(b * many, many), pl.ds(b * some, some)

    def body(j, carry):
        cols = head_columns(j)
        probs = softmax_parts(query[asked, cols], keys[told, cols])
        out[asked, cols] = dot(probs.astype(LOW), values[told, cols]).astype(LOW)
        return carry

    lax.fori_loop(0, query.shape[1] // HEAD, body, 0)


def heads_back(images, query, keys, values, d_att):
    heads = query.shape[1] // HEAD
    many, some = query.shape[0] // images, keys.shape[0] // images
    scale = 1.0 / math.sqrt(HEAD)

    def body(j, carry):
        b = j // heads
        cols = head_columns(j % heads)
        asked = pl.ds(pl.multiple_of(b * many, many), many)
        told = pl.ds(pl.multiple_of(b * some, some), some)
        q, k, v, d = query[asked, cols], keys[told, cols], values[told, cols], d_att[asked, cols]
        probs = softmax_parts(q, k)
        d_probs = dot(d, v, LAST)
        weighted = jnp.sum(probs * d_probs, axis=-1, keepdims=True)
        d_scores = (probs * (d_probs - weighted)).astype(LOW)
        values[told, cols] = dot(probs.astype(LOW), d, FIRST).astype(LOW)
        keys[told, cols] = (dot(d_scores, q, FIRST) * scale).astype(LOW)
        query[asked, cols] = (dot(d_scores, k) * scale).astype(LOW)
        return carry

    lax.fori_loop(0, images * heads, body, 0)


def gelu(u):
    turn = jnp.tanh(math.sqrt(2.0 / math.pi) * (u + 0.044715 * (u * u * u)))
    return 0.5 * u * (1.0 + turn)


def gelu_slope(u):
    c = math.sqrt(2.0 / math.pi)
    turn = jnp.tanh(c * (u + 0.044715 * (u * u * u)))
    return 0.5 * (1.0 + turn) + 0.5 * u * (1.0 - turn * turn) * (c * (1.0 + 0.134145 * (u * u)))


def flat(array):
    return array.reshape(array.shape[0] * array.shape[1], array.shape[2])


def forward_all(pairs, number, given):
    t = given
    images, own, width = t.tokens.shape
    length, words = 4 * own, t.caption.shape[1]
    inner, ff, states = t.query_self.shape[1], t.up_proj.shape[1], t.caption.shape[2]
    rows, word_rows, word_own = images * length, images * words, words // 4
    chunks, text_chunks = ff // inner, states // inner
    half = width // 2
    vars_in = dict(
        tokens=t.tokens, caption=flat(t.caption), cotangent=t.cotangent, text_proj=t.text_proj,
        query_self=t.query_self, key_self=t.key_self, value_self=t.value_self, out_self=t.out_self,
        query_cross=t.query_cross, key_cross=t.key_cross, value_cross=t.value_cross,
        out_cross=t.out_cross, up_proj=t.up_proj, down_proj=t.down_proj,
    )
    sds = jax.ShapeDtypeStruct
    outs = dict(
        image_self=sds((rows, width), LOW), image_cross=sds((rows, width), LOW),
        image_feed=sds((rows, width), LOW), d_image=sds((rows, width), LOW),
        context=sds((word_rows, width), LOW),
        query_sa=sds((rows, inner), LOW), keys_sa=sds((rows, inner), LOW), values_sa=sds((rows, inner), LOW),
        query_ca=sds((rows, inner), LOW), keys_ca=sds((word_rows, inner), LOW), values_ca=sds((word_rows, inner), LOW),
        attended_sa=sds((rows, inner), LOW), attended_ca=sds((rows, inner), LOW),
        resid_mid=sds((images, own, width), F32), resid_late=sds((images, own, width), F32),
        activ=sds((rows, ff), LOW), d_pre=sds((rows, ff), LOW),
        nb_self=sds((rows, half), LOW), nb_cross=sds((rows, half), LOW), nb_low=sds((rows, half), LOW),
        nb_context=sds((word_rows, half), LOW),
    )

    def kernel(*refs):
        h = types.SimpleNamespace(**dict(zip(vars_in, refs)))
        refs = refs[len(vars_in):]
        marks, gain_self, gain_cross, gain_feed = refs[:4]
        refs = refs[4:]
        o = types.SimpleNamespace(**dict(zip(outs, refs)))
        refs = refs[len(outs):]
        scatter_refs, text_refs = refs[:5], refs[5:10]
        (full_s, full_c, full_f, full_d, full_x, gsem_s, gsem_c, gsem_f, gsem_d, gsem_x,
         wn, wt, tok, cot, cap, sq, sk, sv, xq, xk, xv, att_s, att_c, mid, late, act, dpre,
         fsem, osem, hsem) = refs[10:]
        net = Narrow()
        fetch, store = Copies(fsem), Copies(osem)
        barrier = pltpu.get_barrier_semaphore()
        me = lax.axis_index(WIDE)
        greet(barrier, {WIDE: me + 1 - 2 * (me % 2)})
        others = net.meet(barrier) + 1

        def whole(j, ref):
            return fetch.start(ref, wn.at[j])

        def band(j, ref, c):
            return fetch.start(ref.at[pl.ds(c * inner, inner)], wt.at[j])

        need_tok = fetch.start(h.tokens, tok)
        need_cap = fetch.start(h.caption, cap)
        need_proj = [band(c, h.text_proj, c) for c in range(text_chunks)]
        need_cot = fetch.start(h.cotangent, cot)
        need_qkv = [whole(j, ref) for j, ref in enumerate((h.query_self, h.key_self, h.value_self))]
        need_out_self = fetch.start(h.out_self, wt.at[2])
        need_kv = [whole(4, h.key_cross), whole(5, h.value_cross)]
        need_query_cross = whole(3, h.query_cross)
        need_out_cross = fetch.start(h.out_cross, wt.at[3])
        need_up = {3: fetch.start(h.up_proj.at[:, pl.ds(3 * inner, inner)], wn.at[6])}
        gather_s = Gather(net, full_s, own, gsem_s)
        gather_c = Gather(net, full_c, own, gsem_c)
        gather_f = Gather(net, full_f, own, gsem_f)
        gather_d = Gather(net, full_d, own, gsem_d)
        gather_x = Gather(net, full_x, word_own, gsem_x)
        scatter, text = Scatter(net, *scatter_refs), Scatter(net, *text_refs)
        part = scatter.part

        def of(b, n=length):
            return pl.ds(b * n, n)

        need_tok.wait()
        pl.semaphore_wait(barrier, others)
        for b in range(images):
            mine = gather_s.mine(b)

            def step(s, b=b, mine=mine):
                normed, _ = norm_rows(tok[b, s, :].astype(F32))
                mine[s, :] = (normed * gain_self[...].astype(F32)[None]).astype(LOW)

            each_slab(own, step)
            gather_s.start(b)
        need_cap.wait()
        for need in need_proj:
            need.wait()
        for b in range(images):

            def step(cols, b=b):
                total = None
                for c in range(text_chunks):
                    term = dot(cap[of(b, words), pl.ds(c * inner, inner)], wt[c, :, cols])
                    total = term if total is None else total + term
                text.part[b, :, cols] = total

            columns_of(width, step)
            text.start(b)
        need_cot.wait()
        for b in range(images):
            mine = gather_d.mine(b)

            def step(s, b=b, mine=mine):
                mine[s, :] = (cot[b, s, :].astype(F32) * marks[b, s, :]).astype(LOW)

            each_slab(own, step)

        def project(b, source, weights, targets, n=length):
            for j, target in zip(weights, targets):
                target[of(b, n), :] = dot(source[of(b, n), :], wn[j]).astype(LOW)

        def back_out(b, attended, j):
            def step(cols):
                part[b, :, cols] = dot(attended[of(b), :], wt[j, :, cols])

            columns_of(width, step)
            scatter.start(b)

        need_down = {c: band(c, h.down_proj, c) for c in range(text_chunks)}
        gather_s.forward(0)
        text.cross(0)
        text.cross(1)
        gather_d.start(0)
        for b in range(images):
            gather_s.finish(b)
            if b == 0:
                for need in need_qkv:
                    need.wait()
            project(b, full_s, (0, 1, 2), (sq, sk, sv))
            if b + 1 < images:
                gather_s.forward(b + 1)
            heads_forward(b, images, sq, sk, sv, att_s)
            if b == 0:
                need_out_self.wait()
            back_out(b, att_s, 2)
            if b == 0:
                scatter.cross(b)
        store.later(full_s, o.image_self)
        for ref, out in ((sq, o.query_sa), (sk, o.keys_sa), (sv, o.values_sa), (att_s, o.attended_sa)):
            store.later(ref, out)
        for c in range(3):
            need_up[c] = fetch.start(h.up_proj.at[:, pl.ds(c * inner, inner)], wn.at[c])
        need_down[2] = band(2, h.down_proj, 2)
        for b in range(images):
            text.ready(b)
            mine = gather_x.mine(b)

            def step(s, b=b, mine=mine):
                mine[s, :] = text.total(b, s).astype(LOW)

            each_slab(word_own, step)
        scatter.cross(1)
        for b in range(images):
            gather_x.start(b)
        halves_self = Halves(full_s, o.nb_self, pairs, hsem, 0)
        halves_self.start()

        def rows_out(b, source, target, gain, gather):
            scatter.ready(b)
            mine = gather.mine(b)

            def step(s):
                kept = source[b, s, :].astype(F32) + scatter.total(b, s)
                target[b, s, :] = kept
                normed, _ = norm_rows(kept)
                mine[s, :] = (normed * gain[...].astype(F32)[None]).astype(LOW)

            each_slab(own, step)
            gather.start(b)

        rows_out(0, tok, mid, gain_cross, gather_c)
        gather_d.start(1)
        for b in range(images):
            gather_x.forward(b)
        rows_out(1, tok, mid, gain_cross, gather_c)
        store.later(mid, o.resid_mid)
        for need in need_kv:
            need.wait()
        for b in range(images):
            gather_x.finish(b)
            project(b, full_x, (4, 5), (xk, xv), words)
            text.finish(b)
        halves_context = Halves(full_x, o.nb_context, pairs, hsem, 1)
        halves_context.start()
        store.later(full_x, o.context)
        store.later(xk, o.keys_ca)
        store.later(xv, o.values_ca)
        need_query_cross.wait()
        gather_c.forward(0)
        for b in range(images):
            gather_d.forward(b)
        for b in range(images):
            gather_c.finish(b)
            project(b, full_c, (3,), (xq,))
            if b + 1 < images:
                gather_c.forward(b + 1)
            heads_forward(b, images, xq, xk, xv, att_c)
            scatter.finish(b)
            if b == 0:
                need_out_cross.wait()
            back_out(b, att_c, 3)
            if b == 0:
                scatter.cross(b)
        store.later(full_c, o.image_cross)
        store.later(xq, o.query_ca)
        store.later(att_c, o.attended_ca)
        need_down[3] = band(3, h.down_proj, 3)
        for b in range(images):
            gather_d.finish(b)
        halves_low = Halves(full_d, o.nb_low, pairs, hsem, 2)
        halves_low.start()
        scatter.cross(1)
        store.later(full_d, o.d_image)
        rows_out(0, mid, late, gain_feed, gather_f)
        rows_out(1, mid, late, gain_feed, gather_f)
        store.later(late, o.resid_late)
        halves_cross = Halves(full_c, o.nb_cross, pairs, hsem, 3)
        halves_cross.start()
        gather_f.forward(0)
        for b in range(images):
            gather_f.finish(b)
            scatter.finish(b)
            for c in range(chunks):
                if b == 0:
                    need_up[c].wait()
                cols = pl.ds(c * inner, inner)
                part[b, :, cols] = dot(full_f[of(b), :], wn[6 if c == 3 else c])
                if b == 0 and c == 1:
                    gather_f.forward(1)

                def step(s, b=b, cols=cols):
                    act[pl.ds(pl.multiple_of(b * length + s.start, 16), 16), cols] = gelu(part[b, s, cols]).astype(LOW)

                each_slab(length, step)
        store.later(act, o.activ)
        store.later(full_f, o.image_feed)
        for c in range(chunks):
            need_down[c].wait()
            cols = pl.ds(c * inner, inner)
            for b in range(images):
                slope = dot(full_d[of(b), :], wt[c], LAST)
                dpre[of(b), cols] = (gelu_slope(part[b, :, cols]) * slope).astype(LOW)
            store.later(dpre.at[:, cols], o.d_pre.at[:, cols])
        for halves in (halves_self, halves_context, halves_low, halves_cross):
            halves.arrive()
            halves.leave()
        store.close()

    V, DS = pltpu.VMEM, pltpu.SemaphoreType.DMA
    gsem = DS((2, images, 3))
    scratch = scatter_scratch(images, own, width) + scatter_scratch(images, word_own, width)
    scratch += [V((rows, width), LOW)] * 4 + [V((word_rows, width), LOW)] + [gsem] * 5
    scratch += [
        V((7, width, inner), LOW), V((4, inner, width), LOW),
        V((images, own, width), LOW), V((images, own, width), LOW), V((word_rows, states), LOW),
        V((rows, inner), LOW), V((rows, inner), LOW), V((rows, inner), LOW),
        V((rows, inner), LOW), V((word_rows, inner), LOW), V((word_rows, inner), LOW),
        V((rows, inner), LOW), V((rows, inner), LOW),
        V((images, own, width), F32), V((images, own, width), F32), V((rows, ff), LOW), V((rows, ff), LOW),
        DS((40,)), DS((40,)), DS((2, 4, pairs)),
    ]
    result = pl.pallas_call(
        kernel,
        out_shape=list(outs.values()),
        in_specs=[HB] * len(vars_in) + [VM] * 4,
        out_specs=[HB] * len(outs),
        scratch_shapes=scratch,
        compiler_params=params(number, 62),
        name="forward_all",
    )(*vars_in.values(), t.marks, *t.gains)
    return types.SimpleNamespace(**dict(zip(outs, result)))


def backward_all(pairs, number, given, kept):
    t = given
    images, own, width = t.tokens.shape
    length, words = 4 * own, t.caption.shape[1]
    inner, ff, states = t.query_self.shape[1], t.up_proj.shape[1], t.caption.shape[2]
    rows, word_rows, word_own = images * length, images * words, words // 4
    chunks, text_chunks = ff // inner, states // inner
    half, blk = width // 2, width // (2 * pairs)
    count = 2 * chunks + text_chunks + 8
    vars_in = dict(
        vars(kept),
        tokens=t.tokens, caption=flat(t.caption), cotangent=t.cotangent, text_proj=t.text_proj,
        query_self=t.query_self, key_self=t.key_self, value_self=t.value_self, out_self=t.out_self,
        query_cross=t.query_cross, key_cross=t.key_cross, value_cross=t.value_cross,
        out_cross=t.out_cross, up_proj=t.up_proj, down_proj=t.down_proj,
    )

    def kernel(*refs):
        h = types.SimpleNamespace(**dict(zip(vars_in, refs)))
        refs = refs[len(vars_in):]
        marks, gain_self, gain_cross, gain_feed = refs[:4]
        grads_out, words_out, tokens_out, layer_out, gain_out, nb_cols, nb_feed = refs[4:11]
        refs = refs[11:]
        scatter_refs = refs[:5]
        (full_c, full_s, full_x, gsem_c, gsem_s, gsem_x, text_sem,
         big, d_att, wa, wb, xq, xk, xv, sq, sk, sv, cot, late, mid, tok, low_rows, word_grad,
         fsem, osem, nbsem, hsem, gacc, gland, gsems) = refs[5:35]
        net = Narrow()
        units = []

        def unit(trade, rows_ref, nb_rows, columns, size, halves=None):
            i = len(units)
            units.append(types.SimpleNamespace(
                trade=trade, rows=rows_ref, nb_rows=nb_rows, columns=columns, count=size, halves=halves,
                nb_columns=nb_cols.at[i, pl.ds(0, size)], sems=nbsem, out=grads_out.at[i],
            ))

        def chunk(ref, c):
            return ref.at[:, pl.ds(c * inner, inner)]

        halves_feed = Halves(h.image_feed, nb_feed, pairs, hsem, 0)
        for c in range(chunks):
            unit(True, h.d_image, h.nb_low, chunk(h.activ, c), rows)
        for c in range(chunks):
            unit(True, h.image_feed, nb_feed, chunk(h.d_pre, c), rows, halves_feed)
        unit(False, full_c, None, h.attended_ca, rows)
        unit(True, h.image_cross, h.nb_cross, xq, rows)
        unit(True, h.context, h.nb_context, xk, word_rows)
        unit(True, h.context, h.nb_context, xv, word_rows)
        for c in range(text_chunks):
            unit(False, full_x, None, chunk(h.caption, c), word_rows)
        unit(False, full_s, None, h.attended_sa, rows)
        unit(True, h.image_self, h.nb_self, sq, rows)
        unit(True, h.image_self, h.nb_self, sk, rows)
        unit(True, h.image_self, h.nb_self, sv, rows)
        wide = Wide(pairs, units, refs[35:])
        fetch, store = Copies(fsem), Copies(osem)

        def of(b, n=length):
            return pl.ds(b * n, n)

        barrier = pltpu.get_barrier_semaphore()
        far = {WIDE: (wide.z + 2) % pairs * 2 + wide.y}
        near = {WIDE: (wide.z + 1 - 2 * (wide.z % 2)) * 2 + wide.y}
        greet(barrier, far)
        others = wide.meet(barrier) + net.meet(barrier) + 1

        def up_chunk(c):
            return fetch.start(chunk(h.up_proj, c), wa.at[c % 2])

        need_up = {c: up_chunk(c) for c in range(2)}
        need_pre = fetch.start(h.d_pre, big)
        need_cot = fetch.start(h.cotangent, cot)
        need_late = fetch.start(h.resid_late, late)
        need_out = fetch.start(h.out_cross, wb)
        need_ca = [fetch.start(a, b) for a, b in ((h.query_ca, xq), (h.keys_ca, xk), (h.values_ca, xv))]
        need_mid = fetch.start(h.resid_mid, mid)
        need_sa = [fetch.start(a, b) for a, b in ((h.query_sa, sq), (h.keys_sa, sk), (h.values_sa, sv))]
        need_tok = fetch.start(h.tokens, tok)
        pl.semaphore_wait(barrier, others)
        wide.ask(0)
        wide.ask(1)
        scatter = Scatter(net, *scatter_refs)
        part = scatter.part
        gather_c, gather_s = Gather(net, full_c, own, gsem_c), Gather(net, full_s, own, gsem_s)
        gather_x = Gather(net, full_x, word_own, gsem_x)

        need_pre.wait()
        for c in range(chunks):
            need_up[c].wait()
            for b in range(images):

                def step(cols, b=b, c=c):
                    term = dot(big[of(b), pl.ds(c * inner, inner)], wa[c % 2, cols, :], LAST)
                    part[b, :, cols] = term if c == 0 else part[b, :, cols] + term

                columns_of(width, step)
                if c == chunks - 1:
                    scatter.start(b)
            if c + 2 < chunks:
                need_up[c + 2] = up_chunk(c + 2)
        need_query = fetch.start(h.query_cross, wa.at[0])
        need_key = fetch.start(h.key_cross, wa.at[1])
        halves_feed.start()
        gacc[...] = jnp.zeros_like(gacc)

        def back_rows(b, above, mask, source, gain, slot, keep, mine):
            scatter.ready(b)

            def step(s):
                d_hidden = scatter.total(b, s)
                normed, inv_std = norm_rows(source[b, s, :].astype(F32))
                gacc[slot : slot + 1, :] += jnp.sum(d_hidden * normed, axis=0, keepdims=True)
                top = above[b, s, :].astype(F32)
                if mask is not None:
                    top = top * mask[b, s, :]
                scaled = d_hidden * gain[...].astype(F32)[None]
                inside = scaled - jnp.mean(scaled, axis=-1, keepdims=True)
                inside = inside - normed * jnp.mean(scaled * normed, axis=-1, keepdims=True)
                d_rows = top + inv_std * inside
                if keep is not None:
                    keep[b, s, :] = d_rows
                mine[s, :] = d_rows.astype(LOW)

            each_slab(own, step)

        def multiply(b, target, lefts, rights, n=length):
            def step(cols):
                total = None
                for left, j in zip(lefts, rights):
                    term = dot(left[of(b, n), :], wa[j, cols, :], LAST)
                    total = term if total is None else total + term
                target[b, :, cols] = total

            columns_of(width, step)

        def out_back(b, full):
            d_att[of(b), :] = dot(full[of(b), :], wb[...], LAST).astype(LOW)

        wide.tick(-1)
        for b in range(images):
            scatter.cross(b)
        wide.tick(0)
        need_cot.wait()
        need_late.wait()
        for b in range(images):
            back_rows(b, cot, marks, late, gain_feed, 2, late, gather_c.mine(b))
            gather_c.start(b)
        wide.ask(2)
        wide.ask(3)
        for b in range(images):
            gather_c.forward(b)
        wide.tick(1)
        need_out.wait()
        for b in range(images):
            scatter.finish(b)
            gather_c.finish(b)
            out_back(b, full_c)
        need_out = fetch.start(h.out_self, wb)
        for need in need_ca:
            need.wait()
        heads_back(images, xq, xk, xv, d_att)
        wide.tick(2)
        need_query.wait()
        for b in range(images):
            multiply(b, part, [xq], [0])
            scatter.start(b)
        need_value = fetch.start(h.value_cross, wa.at[0])
        for b in range(images):
            scatter.cross(b)
        need_mid.wait()
        for b in range(images):
            back_rows(b, late, None, mid, gain_cross, 1, mid, gather_s.mine(b))
            gather_s.start(b)
        wide.tick(3)
        need_again = fetch.start(h.resid_late, late)
        for b in range(images):
            gather_s.forward(b)
        for b in range(images):
            scatter.finish(b)
            gather_s.finish(b)
        text = Scatter(
            net, part.at[:, pl.ds(0, words)], scatter.landed.at[:, :, pl.ds(0, word_own)],
            scatter.outgoing.at[:, pl.ds(0, word_own)], scatter.arrived.at[:, pl.ds(0, word_own)], text_sem,
        )
        need_key.wait()
        need_value.wait()
        for b in range(images):
            multiply(b, text.part, [xk, xv], [1, 0], words)
            text.start(b)
        need_qkv = [fetch.start(h.query_self, wa.at[0]), fetch.start(h.key_self, wa.at[1])]
        need_out.wait()
        for b in range(images):
            out_back(b, full_s)
        need_text = fetch.start(h.text_proj.at[pl.ds(0, inner)], wb)
        wide.tick(4)
        for b in range(images):
            text.cross(b)
        for need in need_sa:
            need.wait()
        heads_back(images, sq, sk, sv, d_att)
        for b in range(images):
            text.ready(b)
            mine = gather_x.mine(b)

            def step(s, b=b, mine=mine):
                mine[s, :] = text.total(b, s).astype(LOW)

            each_slab(word_own, step)
            gather_x.start(b)
        for b in range(images):
            gather_x.forward(b)
        wide.tick(5)
        for b in range(images):
            text.finish(b)
            gather_x.finish(b)
        for c in range(text_chunks):
            need_text.wait()
            word_grad[:, pl.ds(c * inner, inner)] = dot(full_x[...], wb[...], LAST).astype(LOW)
            if c + 1 < text_chunks:
                need_text = fetch.start(h.text_proj.at[pl.ds((c + 1) * inner, inner)], wb)
        store.later(word_grad, words_out)
        need_down = fetch.start(h.down_proj.at[pl.ds(0, inner)], wb)
        for need in need_qkv:
            need.wait()
        for b in range(images):
            multiply(b, part, [sq, sk], [0, 1])
        need_value = fetch.start(h.value_self, wa.at[0])
        need_act = fetch.start(h.activ, big)
        need_value.wait()
        for b in range(images):

            def step(cols, b=b):
                part[b, :, cols] += dot(sv[of(b), :], wa[0, cols, :], LAST)

            columns_of(width, step)
            scatter.start(b)
        wide.tick(6)
        for b in range(images):
            scatter.cross(b)
        need_tok.wait()
        for b in range(images):
            back_rows(b, mid, None, tok, gain_self, 0, None, low_rows.at[b])
        store.later(low_rows, tokens_out)
        for b in range(images):
            scatter.finish(b)
        wide.tick(7)
        for j, peer in enumerate((net.core, net.chip, wide.peer, near, far)):
            trip = send(gacc, gland.at[j], gsems, (j,), peer)
            trip.start()
            trip.wait()
            gacc[...] = gacc[...] + gland[j]
        store.later(gacc, gain_out)
        wide.tick(8)
        need_act.wait()
        for c in range(chunks):
            need_down.wait()
            for b in range(images):

                def step(cols, b=b, c=c):
                    term = dot(big[of(b), pl.ds(c * inner, inner)], wb[:, cols])
                    part[b, :, cols] = term if c == 0 else part[b, :, cols] + term

                columns_of(width, step)
            if c + 1 < chunks:
                need_down = fetch.start(h.down_proj.at[pl.ds((c + 1) * inner, inner)], wb)
        for b in range(images):
            scatter.start(b)
        wide.tick(9)
        for b in range(images):
            scatter.cross(b)
        wide.tick(10)
        need_again.wait()
        for b in range(images):
            scatter.ready(b)

            def step(s, b=b):
                tok[b, s, :] = (late[b, s, :] + scatter.total(b, s)).astype(LOW)

            each_slab(own, step)
            scatter.finish(b)
        store.later(tok, layer_out)
        for k in range(11, count + pairs - 1):
            wide.tick(k)
        wide.drain()
        halves_feed.leave()
        store.close()

    V, DS = pltpu.VMEM, pltpu.SemaphoreType.DMA
    gsem = DS((2, images, 3))
    sums = 2 + text_chunks
    scratch = scatter_scratch(images, own, width)
    scratch += [V((rows, width), LOW), V((rows, width), LOW), V((word_rows, width), LOW)] + [gsem] * 4
    scratch += [
        V((rows, ff), LOW), V((rows, inner), LOW), V((2, width, inner), LOW), V((inner, width), LOW),
        V((rows, inner), LOW), V((word_rows, inner), LOW), V((word_rows, inner), LOW),
        V((rows, inner), LOW), V((rows, inner), LOW), V((rows, inner), LOW),
        V((images, own, width), LOW), V((images, own, width), F32), V((images, own, width), F32),
        V((images, own, width), LOW), V((images, own, width), LOW), V((word_rows, states), LOW),
        DS((40,)), DS((8,)), DS((2, count)), DS((2, 1, pairs)), V((8, width), F32), V((5, 8, width), F32), DS((2, 5)),
    ]
    scratch += [
        V((HELD, pairs, blk, inner), LOW), V((2, pairs, blk, inner), LOW), V((sums, pairs, blk, inner), LOW),
        V((RING, pairs - 1, blk, inner), LOW), V((RING, pairs - 1, blk, inner), LOW), V((2, blk, inner), LOW),
        V((2, 2, pairs, rows, blk), LOW), V((2, 2, rows, inner), LOW),
        DS((2, sums, pairs)), DS((2, count, pairs - 1)), DS((2, count, pairs - 1)),
        DS((2, 2, pairs)), DS((2, 2)), DS((2,)),
        pltpu.SemaphoreType.REGULAR, pltpu.SemaphoreType.REGULAR,
    ]
    sds = jax.ShapeDtypeStruct
    result = pl.pallas_call(
        kernel,
        out_shape=[
            sds((count, blk, inner), LOW), sds((word_rows, states), LOW), sds((images, own, width), LOW),
            sds((images, own, width), LOW), sds((8, width), F32), sds((count, rows, inner), LOW), sds((rows, half), LOW),
        ],
        in_specs=[HB] * len(vars_in) + [VM] * 4,
        out_specs=[HB] * 7,
        scratch_shapes=scratch,
        compiler_params=params(number, 62),
        name="backward_all",
    )(*vars_in.values(), t.marks, *t.gains)
    return result[:5]


def spread(blocks, places, shapes, whole, gains):
    count, blk, inner = blocks.shape
    more = len(whole)

    def kernel(*refs):
        blocks_ref, whole_in, gains_ref, refs = refs[0], refs[1 : 1 + more], refs[1 + more], refs[2 + more :]
        outs, whole_out, refs = refs[: len(shapes)], refs[len(shapes) : len(shapes) + more], refs[len(shapes) + more :]
        gains_out, refs = refs[:3], refs[3:]
        for j, row in enumerate(gains_out):
            row[...] = gains_ref[j, :]
        held, flat_stage, turned_stage, isem, osem, wsem = refs
        ins = [pltpu.make_async_copy(blocks_ref.at[i], held.at[i], isem.at[i]) for i in range(count)]
        for copy in ins:
            copy.start()
        done, plain, turns = [], 0, 0
        for j in range(more):
            done.append(pltpu.make_async_copy(whole_in[j], whole_out[j], wsem.at[j]))
            done[-1].start()
        for i, (which, row, col, turned) in enumerate(places):
            ins[i].wait()
            if turned:
                stage = turned_stage.at[turns]
                turns += 1
                for j in range(0, inner, 128):
                    stage[pl.ds(j, 128), :] = held[i, :, pl.ds(j, 128)].astype(F32).T
                place = outs[which].at[pl.ds(row, inner), pl.ds(col, blk)]
            else:
                stage = flat_stage.at[plain]
                plain += 1
                stage[...] = held[i].astype(F32)
                place = outs[which].at[pl.ds(row, blk), pl.ds(col, inner)]
            done.append(pltpu.make_async_copy(stage, place, osem.at[i]))
            done[-1].start()
        for copy in done:
            copy.wait()

    turns = sum(1 for place in places if place[3])
    V, DS = pltpu.VMEM, pltpu.SemaphoreType.DMA
    return pl.pallas_call(
        kernel,
        out_shape=[jax.ShapeDtypeStruct(shape, F32) for shape in shapes]
        + [jax.ShapeDtypeStruct(array.shape, array.dtype) for array in whole]
        + [jax.ShapeDtypeStruct(gains.shape[1:], F32)] * 3,
        in_specs=[HB] * (1 + more) + [VM],
        out_specs=[HB] * (len(shapes) + more) + [VM] * 3,
        scratch_shapes=[
            V((count, blk, inner), LOW), V((count - turns, blk, inner), F32), V((turns, inner, blk), F32),
            DS((count,)), DS((count,)), DS((more,)),
        ],
        compiler_params=pltpu.CompilerParams(vmem_limit_bytes=62 * 1024 * 1024),
        name="spread",
    )(blocks, *whole, gains)


def by_kernels(
    tokens, caption, token_mask, cotangent, gain_self, gain_cross, gain_feed, text_proj,
    query_self, key_self, value_self, out_self, query_cross, key_cross, value_cross, out_cross, up_proj, down_proj,
):
    given = types.SimpleNamespace(
        tokens=tokens, caption=caption, cotangent=cotangent, text_proj=text_proj,
        query_self=query_self, key_self=key_self, value_self=value_self, out_self=out_self,
        query_cross=query_cross, key_cross=key_cross, value_cross=value_cross, out_cross=out_cross,
        up_proj=up_proj, down_proj=down_proj, marks=token_mask[:, :, None].astype(F32),
        gains=[gain_self, gain_cross, gain_feed],
    )
    pairs = lax.axis_size(WIDE) // 2
    kept = forward_all(pairs, 1, given)
    grads, d_words, d_tokens, layer_out, gains = backward_all(pairs, 2, given, kept)
    inner = query_self.shape[1]
    blk = query_self.shape[0] // (2 * pairs)
    ff, text = up_proj.shape[1] // inner, caption.shape[2] // inner
    places = [(10, c * inner, 0, True) for c in range(ff)]
    places += [(9, 0, c * inner, False) for c in range(ff)]
    places += [(8, 0, 0, True), (5, 0, 0, False), (6, 0, 0, False), (7, 0, 0, False)]
    places += [(0, c * inner, 0, True) for c in range(text)]
    places += [(4, 0, 0, True), (1, 0, 0, False), (2, 0, 0, False), (3, 0, 0, False)]
    shapes = [(text * inner, blk)] + [(blk, inner)] * 3 + [(inner, blk)] + [(blk, inner)] * 3 + [(inner, blk)]
    shapes += [(blk, ff * inner), (ff * inner, blk)]
    out = spread(grads, places, shapes, [layer_out, d_tokens, d_words], gains)
    sums, (layer_out, d_tokens, d_words, *gains) = out[: len(shapes)], out[len(shapes) :]
    return (layer_out, d_tokens, d_words.reshape(caption.shape), *gains, *sums)


def local(
    tokens,
    caption,
    token_mask,
    cotangent,
    gain_self,
    gain_cross,
    gain_feed,
    text_proj,
    query_self,
    key_self,
    value_self,
    out_self,
    query_cross,
    key_cross,
    value_cross,
    out_cross,
    up_proj,
    down_proj,
):
    given = (tokens, caption, token_mask, cotangent, gain_self, gain_cross, gain_feed, text_proj, query_self, key_self, value_self, out_self, query_cross, key_cross, value_cross, out_cross, up_proj, down_proj)
    if lax.axis_size(WIDE) != 8 or lax.axis_size(NARROW) != 4:
        return by_collectives(*given)
    return by_kernels(*given)


def solution(mesh):
    in_specs = (
        P(WIDE, NARROW, None),
        P(WIDE, None, NARROW),
        P(WIDE, NARROW),
        P(WIDE, NARROW, None),
        P(),
        P(),
        P(),
        P(NARROW, None),
        P(None, NARROW),
        P(None, NARROW),
        P(None, NARROW),
        P(NARROW, None),
        P(None, NARROW),
        P(None, NARROW),
        P(None, NARROW),
        P(NARROW, None),
        P(None, NARROW),
        P(NARROW, None),
    )
    out_specs = (
        P(WIDE, NARROW, None),
        P(WIDE, NARROW, None),
        P(WIDE, None, NARROW),
        P(),
        P(),
        P(),
        P(NARROW, WIDE),
        P(WIDE, NARROW),
        P(WIDE, NARROW),
        P(WIDE, NARROW),
        P(NARROW, WIDE),
        P(WIDE, NARROW),
        P(WIDE, NARROW),
        P(WIDE, NARROW),
        P(NARROW, WIDE),
        P(WIDE, NARROW),
        P(NARROW, WIDE),
    )
    return jax.shard_map(local, mesh=mesh, in_specs=in_specs, out_specs=out_specs, check_vma=False)
```

```python
import math
import types

import jax
import jax.numpy as jnp
from jax import lax
from jax.experimental import pallas as pl
from jax.experimental.pallas import tpu as pltpu
from jax.sharding import PartitionSpec as P

HEAD = 128
MESH = pl.DeviceIdType.MESH
WIDE, NARROW = "wide", "narrow"
LOW, F32 = jnp.bfloat16, jnp.float32
LAST, FIRST = (((1,), (1,)), ((), ())), (((0,), (0,)), ((), ()))

def normalize(rows):
    centre = jnp.mean(rows, axis=-1, keepdims=True)
    centred = rows - centre
    variance = jnp.mean(centred * centred, axis=-1, keepdims=True)
    inv_std = lax.rsqrt(variance + 1e-05)
    return (centred * inv_std, inv_std)


def norm_back(d_normed, normed, inv_std):
    inner = d_normed - jnp.mean(d_normed, axis=-1, keepdims=True)
    inner = inner - normed * jnp.mean(d_normed * normed, axis=-1, keepdims=True)
    return inv_std * inner


def times_weight(left, right):
    return jnp.dot(left, right, preferred_element_type=jnp.float32)


def split_heads(matrix):
    return matrix.reshape(matrix.shape[0], matrix.shape[1], matrix.shape[2] // HEAD, HEAD)


def join_heads(heads):
    return heads.reshape(heads.shape[0], heads.shape[1], heads.shape[2] * HEAD)


def head_scores(query, keys):
    scores = jnp.einsum(
        "bqhe,bkhe->bhqk", split_heads(query), split_heads(keys), preferred_element_type=jnp.float32
    )
    return scores * (1.0 / math.sqrt(HEAD))


def attend(query, keys, values):
    scores = head_scores(query, keys)
    peak = jnp.max(scores, axis=-1, keepdims=True)
    powers = jnp.exp(scores - peak)
    summed = jnp.sum(powers, axis=-1, keepdims=True)
    low_probs = (powers / summed).astype(jnp.bfloat16)
    attended = jnp.einsum(
        "bhqk,bkhe->bqhe", low_probs, split_heads(values), preferred_element_type=jnp.float32
    )
    return join_heads(attended).astype(jnp.bfloat16), peak + jnp.log(summed)


def attend_back(query, keys, values, log_total, d_attended):
    probs = jnp.exp(head_scores(query, keys) - log_total)
    low_probs = probs.astype(jnp.bfloat16)
    d_heads = split_heads(d_attended)
    d_probs = jnp.einsum(
        "bqhe,bkhe->bhqk", d_heads, split_heads(values), preferred_element_type=jnp.float32
    )
    d_values = jnp.einsum("bhqk,bqhe->bkhe", low_probs, d_heads, preferred_element_type=jnp.float32)
    weighted = jnp.sum(probs * d_probs, axis=-1, keepdims=True)
    d_scores = (probs * (d_probs - weighted)).astype(jnp.bfloat16)
    scale = 1.0 / math.sqrt(HEAD)
    d_query = (
        jnp.einsum("bhqk,bkhe->bqhe", d_scores, split_heads(keys), preferred_element_type=jnp.float32)
        * scale
    )
    d_keys = (
        jnp.einsum("bhqk,bqhe->bkhe", d_scores, split_heads(query), preferred_element_type=jnp.float32)
        * scale
    )
    return tuple(join_heads(d).astype(jnp.bfloat16) for d in (d_query, d_keys, d_values))


def contract(left, right):
    return lax.dot_general(
        left, right, (((0, 1), (0, 1)), ((), ())), preferred_element_type=jnp.float32
    ).astype(jnp.bfloat16)


def against(left, right):
    return lax.dot_general(
        left, right, (((2,), (1,)), ((), ())), preferred_element_type=jnp.float32
    )


def group_rows(piece):
    return lax.all_gather(piece, NARROW, axis=1, tiled=True)


def own_rows(partial):
    return lax.psum_scatter(partial, NARROW, scatter_dimension=1, tiled=True)


def feed_back(partial):
    return own_rows(partial.astype(jnp.bfloat16)).astype(jnp.float32)


def text_total(partial):
    return lax.psum(partial, NARROW)


def by_collectives(
    tokens,
    caption,
    token_mask,
    cotangent,
    gain_self,
    gain_cross,
    gain_feed,
    text_proj,
    query_self,
    key_self,
    value_self,
    out_self,
    query_cross,
    key_cross,
    value_cross,
    out_cross,
    up_proj,
    down_proj,
):
    gain_one = gain_self.astype(jnp.float32)
    gain_two = gain_cross.astype(jnp.float32)
    gain_three = gain_feed.astype(jnp.float32)
    low = jnp.bfloat16

    resid_in = tokens.astype(jnp.float32)
    normed_self, inv_self = normalize(resid_in)
    image_self = group_rows((normed_self * gain_one).astype(low))
    query_sa = times_weight(image_self, query_self).astype(low)
    keys_sa = times_weight(image_self, key_self).astype(low)
    values_sa = times_weight(image_self, value_self).astype(low)
    attended_sa, total_sa = attend(query_sa, keys_sa, values_sa)
    resid_mid = resid_in + own_rows(times_weight(attended_sa, out_self))
    context = text_total(times_weight(caption, text_proj)).astype(low)
    keys_ca = times_weight(context, key_cross).astype(low)
    values_ca = times_weight(context, value_cross).astype(low)
    normed_cross, inv_cross = normalize(resid_mid)
    image_cross = group_rows((normed_cross * gain_two).astype(low))
    query_ca = times_weight(image_cross, query_cross).astype(low)
    attended_ca, total_ca = attend(query_ca, keys_ca, values_ca)
    resid_late = resid_mid + own_rows(times_weight(attended_ca, out_cross))
    normed_feed, inv_feed = normalize(resid_late)
    d_result = cotangent.astype(jnp.float32) * token_mask[:, :, None].astype(jnp.float32)
    d_image = group_rows(d_result.astype(low))
    image_feed = group_rows((normed_feed * gain_three).astype(low))
    pre_act = times_weight(image_feed, up_proj)
    gelu_out, gelu_pull = jax.vjp(jax.nn.gelu, pre_act)
    activ = gelu_out.astype(low)
    resid_out = resid_late + feed_back(times_weight(activ, down_proj))
    d_pre = gelu_pull(against(d_image, down_proj))[0].astype(low)
    part_down = contract(activ, d_image)
    part_up = contract(image_feed, d_pre)
    d_hidden_feed = feed_back(against(d_pre, up_proj))
    part_gain_feed = jnp.sum(d_hidden_feed * normed_feed, axis=(0, 1))
    d_late = d_result + norm_back(d_hidden_feed * gain_three, normed_feed, inv_feed)
    d_image_cross = group_rows(d_late.astype(low))
    part_out_cross = contract(attended_ca, d_image_cross)
    d_attended_ca = against(d_image_cross, out_cross).astype(low)
    d_query_ca, d_keys_ca, d_values_ca = attend_back(
        query_ca, keys_ca, values_ca, total_ca, d_attended_ca
    )
    part_query_cross = contract(image_cross, d_query_ca)
    part_key_cross = contract(context, d_keys_ca)
    part_value_cross = contract(context, d_values_ca)
    d_hidden_cross = own_rows(against(d_query_ca, query_cross))
    d_context = text_total(against(d_keys_ca, key_cross) + against(d_values_ca, value_cross))
    d_context = d_context.astype(low)
    part_text = contract(caption, d_context)
    d_words = against(d_context, text_proj).astype(low)
    part_gain_cross = jnp.sum(d_hidden_cross * normed_cross, axis=(0, 1))
    d_mid = d_late + norm_back(d_hidden_cross * gain_two, normed_cross, inv_cross)
    d_image_self = group_rows(d_mid.astype(low))
    part_out_self = contract(attended_sa, d_image_self)
    d_attended_sa = against(d_image_self, out_self).astype(low)
    d_query_sa, d_keys_sa, d_values_sa = attend_back(
        query_sa, keys_sa, values_sa, total_sa, d_attended_sa
    )
    part_query_self = contract(image_self, d_query_sa)
    part_key_self = contract(image_self, d_keys_sa)
    part_value_self = contract(image_self, d_values_sa)
    d_hidden_self = own_rows(
        against(d_query_sa, query_self)
        + against(d_keys_sa, key_self)
        + against(d_values_sa, value_self)
    )
    part_gain_self = jnp.sum(d_hidden_self * normed_self, axis=(0, 1))
    d_input = d_mid + norm_back(d_hidden_self * gain_one, normed_self, inv_self)
    parts = (
        part_text,
        part_query_self,
        part_key_self,
        part_value_self,
        part_out_self,
        part_query_cross,
        part_key_cross,
        part_value_cross,
        part_out_cross,
        part_up,
        part_down,
    )
    dims = (1, 0, 0, 0, 1, 0, 0, 0, 1, 0, 1)
    summed = [
        lax.psum_scatter(part, WIDE, scatter_dimension=dim, tiled=True)
        for part, dim in zip(parts, dims)
    ]
    gains = lax.psum((part_gain_self, part_gain_cross, part_gain_feed), (WIDE, NARROW))
    return (
        resid_out.astype(low),
        d_input.astype(low),
        d_words,
        *gains,
        *[part.astype(jnp.float32) for part in summed],
    )


RING = 6
HELD = 8


def send(src, dst, sems, index, peer):
    return pltpu.make_async_remote_copy(
        src_ref=src,
        dst_ref=dst,
        send_sem=sems.at[(0,) + index],
        recv_sem=sems.at[(1,) + index],
        device_id=peer,
        device_id_type=MESH,
    )


def greet(barrier, peer):
    pl.semaphore_signal(barrier, inc=1, device_id=peer, device_id_type=MESH)


def each_slab(count, step, slab=16):
    def body(i, carry):
        step(pl.ds(pl.multiple_of(i * slab, slab), slab))
        return carry

    lax.fori_loop(0, count // slab, body, 0)


class Wide:
    def __init__(self, pairs, units, refs):
        (self.mine, self.theirs, self.fromy, self.right, self.left, self.stage,
         self.aslot, self.bslot, self.ysem, self.rsem, self.lsem, self.asem, self.bsem,
         self.osem, self.rfree, self.lfree) = refs
        self.pairs, self.units = pairs, units
        self.asked, self.released, self.gone = set(), set(), set()
        me = lax.axis_index(WIDE)
        self.z, self.y = me // 2, me % 2
        self.has_right, self.has_left = self.z < pairs - 1, self.z > 0
        self.peer = {WIDE: self.z * 2 + 1 - self.y}
        self.next = {WIDE: jnp.minimum(self.z + 1, pairs - 1) * 2 + self.y}
        self.last = {WIDE: jnp.maximum(self.z - 1, 0) * 2 + self.y}
        self.summed = [i for i, unit in enumerate(units) if not unit.trade]
        group = -1
        for i, unit in enumerate(units):
            if i == 0 or unit.rows is not units[i - 1].rows:
                group += 1
            unit.group = group
        self.blk, self.cols = self.mine.shape[2], self.mine.shape[3]

    def meet(self, barrier):
        greet(barrier, self.peer)

        @pl.when(self.has_right)
        def _():
            greet(barrier, self.next)

        @pl.when(self.has_left)
        def _():
            greet(barrier, self.last)

        return 1 + self.has_right.astype(jnp.int32) + self.has_left.astype(jnp.int32)

    def trade(self, i):
        unit = self.units[i]
        return send(unit.columns, unit.nb_columns, unit.sems, (i,), self.peer)

    def loads(self, i):
        unit = self.units[i]
        s, rows = unit.group % 2, unit.count
        copies = []
        if i == 0 or self.units[i - 1].group != unit.group:
            for k in range(self.pairs):
                for part in (0, 1):
                    if part == 0 or not unit.trade:
                        at = (k * 2 + (self.y if part == 0 else 1 - self.y)) * self.blk
                        src = unit.rows.at[:, pl.ds(pl.multiple_of(at, self.blk), self.blk)]
                    else:
                        src = unit.nb_rows.at[:, pl.ds(k * self.blk, self.blk)]
                    copies.append(
                        pltpu.make_async_copy(
                            src, self.aslot.at[s, part, k, pl.ds(0, rows)], self.asem.at[s, part, k]
                        )
                    )
        q = i % 2
        copies.append(
            pltpu.make_async_copy(
                unit.columns, self.bslot.at[q, 0, pl.ds(0, rows)], self.bsem.at[q, 0]
            )
        )
        if unit.trade:
            copies.append(
                pltpu.make_async_copy(
                    unit.nb_columns, self.bslot.at[q, 1, pl.ds(0, rows)], self.bsem.at[q, 1]
                )
            )
        return copies

    def load(self, i):
        unit = self.units[i]
        if unit.trade:
            if not unit.early:
                self.trade(i).wait_recv()
            if unit.halves is not None and (i == 0 or self.units[i - 1].group != unit.group):
                unit.halves.arrive()
        for copy in self.loads(i):
            copy.start()

    def y_copy(self, i, k):
        n = self.summed.index(i)
        return send(self.theirs.at[n % 2, k], self.fromy.at[n, k], self.ysem, (n, k), self.peer)

    def compute(self, i):
        unit = self.units[i]
        s, q, g, rows = unit.group % 2, i % 2, i % HELD, unit.count
        for copy in self.loads(i):
            copy.wait()
        if i >= HELD:
            self.sent(i - HELD)
        if not unit.trade:
            n = self.summed.index(i)
            if n >= 2:
                for k in range(self.pairs):
                    self.y_copy(self.summed[n - 2], k).wait_send()

            def far(k, carry):
                self.theirs[n % 2, k] = lax.dot_general(
                    self.aslot[s, 1, k, :rows], self.bslot[q, 0, :rows], FIRST,
                    preferred_element_type=F32,
                ).astype(LOW)
                return carry

            lax.fori_loop(0, self.pairs, far, 0)
            for k in range(self.pairs):
                self.y_copy(i, k).start()

        def near(k, carry):
            total = lax.dot_general(
                self.aslot[s, 0, k, :rows], self.bslot[q, 0, :rows], FIRST,
                preferred_element_type=F32,
            )
            if unit.trade:
                total = total + lax.dot_general(
                    self.aslot[s, 1, k, :rows], self.bslot[q, 1, :rows], FIRST,
                    preferred_element_type=F32,
                )
            self.mine[g, k] = total.astype(LOW)
            return carry

        lax.fori_loop(0, self.pairs, near, 0)

    def add(self, dst, src):
        def step(s):
            dst[s, :] = dst[s, :] + src[s, :]

        each_slab(self.blk, step, 64)

    def y_add(self, i):
        n = self.summed.index(i)
        for k in range(self.pairs):
            self.y_copy(i, k).wait_recv()
            self.add(self.mine.at[i % HELD, k], self.fromy.at[n, k])

    def r_copy(self, i, t):
        d = jnp.clip(self.pairs - t + self.z, 0, self.pairs - 1)
        return send(self.mine.at[i % HELD, d], self.right.at[i % RING, t - 1], self.rsem, (i, t - 1), self.next)

    def l_copy(self, i, t):
        d = jnp.clip(t - self.pairs + self.z, 0, self.pairs - 1)
        return send(self.mine.at[i % HELD, d], self.left.at[i % RING, t - 1], self.lsem, (i, t - 1), self.last)

    def sends_right(self, t):
        return self.has_right & (t >= self.z + 1)

    def sends_left(self, t):
        return self.has_left & (t >= self.pairs - self.z)

    def credit(self, i, free, when):
        if i >= RING:

            @pl.when(when)
            def _():
                pl.semaphore_wait(free, 1)

    def release(self, i):
        if i in self.released:
            return
        self.released.add(i)
        if not self.units[i].trade:
            self.y_add(i)

        @pl.when(self.z == 0)
        def _():
            if i >= RING:
                pl.semaphore_wait(self.rfree, 1)
            for t in range(1, self.pairs):
                self.r_copy(i, t).start()

        @pl.when(self.z == self.pairs - 1)
        def _():
            if i >= RING:
                pl.semaphore_wait(self.lfree, 1)
            for t in range(1, self.pairs):
                self.l_copy(i, t).start()

    def step(self, i, t):
        g, r = i % HELD, i % RING
        first_right, first_left = t == self.z + 1, t == self.pairs - self.z

        @pl.when(self.sends_right(t) & self.has_left)
        def _():
            self.credit(i, self.rfree, first_right)
            self.r_copy(i, t - 1).wait_recv()
            d = jnp.clip(self.pairs - t + self.z, 0, self.pairs - 1)
            self.add(self.mine.at[g, d], self.right.at[r, t - 2])
            self.r_copy(i, t).start()

        @pl.when(self.sends_left(t) & self.has_right)
        def _():
            self.credit(i, self.lfree, first_left)
            self.l_copy(i, t - 1).wait_recv()
            d = jnp.clip(t - self.pairs + self.z, 0, self.pairs - 1)
            self.add(self.mine.at[g, d], self.left.at[r, t - 2])
            self.l_copy(i, t).start()

    def out_copy(self, i):
        return pltpu.make_async_copy(self.stage.at[i % 2], self.units[i].out, self.osem.at[i % 2])

    def final(self, i):
        g, r, t = i % HELD, i % RING, self.pairs - 1

        @pl.when(self.has_left)
        def _():
            self.r_copy(i, t).wait_recv()
            self.add(self.mine.at[g, self.z], self.right.at[r, t - 1])

        @pl.when(self.has_right)
        def _():
            self.l_copy(i, t).wait_recv()
            self.add(self.mine.at[g, self.z], self.left.at[r, t - 1])

        if i + RING < len(self.units):

            @pl.when(self.has_left)
            def _():
                pl.semaphore_signal(self.rfree, inc=1, device_id=self.last, device_id_type=MESH)

            @pl.when(self.has_right)
            def _():
                pl.semaphore_signal(self.lfree, inc=1, device_id=self.next, device_id_type=MESH)

        if i >= 2:
            self.out_copy(i - 2).wait()

        def step(s):
            self.stage[i % 2, s, :] = self.mine[g, self.z, s, :]

        each_slab(self.blk, step, 64)
        self.out_copy(i).start()

    def sent(self, i):
        for t in range(1, self.pairs):

            @pl.when(self.sends_right(t))
            def _():
                self.r_copy(i, t).wait_send()

            @pl.when(self.sends_left(t))
            def _():
                self.l_copy(i, t).wait_send()

    def ask(self, i):
        if i < len(self.units) and self.units[i].trade and not self.units[i].early and i not in self.asked:
            self.asked.add(i)
            self.trade(i).start()

    def move(self, k):
        count, pairs = len(self.units), self.pairs
        for t in range(pairs - 1, 1, -1):
            if 0 <= k - (t - 1) < count:
                self.step(k - (t - 1), t)
        if 0 <= k - (pairs - 1) < count:
            self.final(k - (pairs - 1))
        if k + 1 < count and not self.units[k + 1].trade:
            self.release(k + 1)

    def leave(self, i):
        if self.units[i].trade and not self.units[i].early and i not in self.gone:
            self.gone.add(i)
            self.trade(i).wait_send()

    def multiply(self, i):
        self.load(i)
        self.compute(i)
        if self.units[i].trade:
            for j in range(i + 1):
                self.release(j)

    def drain(self):
        count = len(self.units)
        for i in range(max(0, count - 2), count):
            self.out_copy(i).wait()
        for i in range(max(0, count - HELD), count):
            self.sent(i)
        for i in self.summed[-2:]:
            for k in range(self.pairs):
                self.y_copy(i, k).wait_send()
        for i in range(count):
            self.leave(i)


VM = pl.BlockSpec(memory_space=pltpu.VMEM)
HB = pl.BlockSpec(memory_space=pl.ANY)


def norm_rows(rows):
    centre = jnp.mean(rows, axis=-1, keepdims=True)
    centred = rows - centre
    variance = jnp.mean(centred * centred, axis=-1, keepdims=True)
    inv_std = lax.rsqrt(variance + 1e-05)
    return centred * inv_std, inv_std


class Narrow:
    def __init__(self):
        self.me = lax.axis_index(NARROW)
        x, c = self.me // 2, self.me % 2
        self.core_at = x * 2 + 1 - c
        self.chip_at = (1 - x) * 2 + c
        self.far_at = (1 - x) * 2 + 1 - c
        self.core = {NARROW: self.core_at}
        self.chip = {NARROW: self.chip_at}

    def meet(self, barrier):
        greet(barrier, self.core)
        greet(barrier, self.chip)
        return 2


class Gather:
    def __init__(self, net, full, own, sems):
        self.net, self.full, self.own, self.sems = net, full, own, sems

    def place(self, b, who):
        at = (b * 4 + who) * self.own
        return self.full.at[pl.ds(pl.multiple_of(at, self.own), self.own), :]

    def mine(self, b):
        return self.place(b, self.net.me)

    def to_core(self, b):
        return send(self.mine(b), self.mine(b), self.sems, (b, 0), self.net.core)

    def to_chip(self, b):
        return send(self.mine(b), self.mine(b), self.sems, (b, 1), self.net.chip)

    def onward(self, b):
        block = self.place(b, self.net.chip_at)
        return send(block, block, self.sems, (b, 2), self.net.core)

    def start(self, b):
        self.to_chip(b).start()
        self.to_core(b).start()

    def forward(self, b):
        self.to_chip(b).wait_recv()
        self.onward(b).start()

    def finish(self, b):
        self.to_core(b).wait_recv()
        self.onward(b).wait_recv()
        self.to_core(b).wait_send()
        self.to_chip(b).wait_send()
        self.onward(b).wait_send()


class Scatter:
    def __init__(self, net, part, landed, outgoing, arrived, sems):
        self.net, self.part, self.landed = net, part, landed
        self.outgoing, self.arrived, self.sems = outgoing, arrived, sems
        self.own = part.shape[1] // 4

    def rows(self, b, who):
        return self.part.at[b, pl.ds(pl.multiple_of(who * self.own, self.own), self.own), :]

    def core_copy(self, b, k):
        who = self.net.far_at if k == 0 else self.net.core_at
        return send(self.rows(b, who), self.landed.at[b, k], self.sems, (b, k), self.net.core)

    def chip_copy(self, b):
        return send(self.outgoing.at[b], self.arrived.at[b], self.sems, (b, 2), self.net.chip)

    def start(self, b):
        self.core_copy(b, 0).start()
        self.core_copy(b, 1).start()

    def cross(self, b):
        self.core_copy(b, 0).wait_recv()
        mine = self.rows(b, self.net.chip_at)

        def step(s):
            total = mine[s, :] + self.landed[b, 0, s, :]
            self.outgoing[b, s, :] = total.astype(self.outgoing.dtype)

        each_slab(self.own, step)
        self.chip_copy(b).start()

    def ready(self, b):
        self.core_copy(b, 1).wait_recv()
        self.chip_copy(b).wait_recv()

    def total(self, b, s):
        near = self.rows(b, self.net.me)[s, :] + self.landed[b, 1, s, :]
        return near + self.arrived[b, s, :].astype(F32)

    def finish(self, b):
        self.core_copy(b, 0).wait_send()
        self.core_copy(b, 1).wait_send()
        self.chip_copy(b).wait_send()


class Halves:
    def __init__(self, net, full, there, pairs, sems, index):
        me = lax.axis_index(WIDE)
        y, rows = me % 2, full.shape[0] // 2
        blk = full.shape[1] // (2 * pairs)
        span = pl.ds(pl.multiple_of(net.me % 2 * rows, rows), rows)
        self.copies = [
            send(
                full.at[span, pl.ds(pl.multiple_of((2 * k + 1 - y) * blk, blk), blk)],
                there.at[span, pl.ds(k * blk, blk)], sems, (index, k), {WIDE: me + 1 - 2 * y},
            )
            for k in range(pairs)
        ]
        self.onward = send(there.at[span], there.at[span], sems, (index, pairs), net.core)

    def start(self):
        for copy in self.copies:
            copy.start()

    def forward(self):
        for copy in self.copies:
            copy.wait_recv()
        self.onward.start()

    def arrive(self):
        self.onward.wait_recv()

    def leave(self):
        for copy in self.copies:
            copy.wait_send()
        self.onward.wait_send()


def scatter_scratch(images, own, width, hop=LOW):
    return [
        pltpu.VMEM((images, 4 * own, width), F32),
        pltpu.VMEM((images, 2, own, width), F32),
        pltpu.VMEM((images, own, width), hop),
        pltpu.VMEM((images, own, width), hop),
        pltpu.SemaphoreType.DMA((2, images, 3)),
    ]


def params(number, limit):
    return pltpu.CompilerParams(
        collective_id=number, has_side_effects=True, vmem_limit_bytes=limit * 1024 * 1024
    )


class Copies:
    def __init__(self, sems):
        self.sems, self.used, self.open = sems, 0, []

    def start(self, src, dst):
        copy = pltpu.make_async_copy(src, dst, self.sems.at[self.used])
        self.used += 1
        copy.start()
        return copy

    def later(self, src, dst):
        self.open.append(self.start(src, dst))

    def close(self):
        for copy in self.open:
            copy.wait()


def columns_of(width, step, tile=512):
    def body(j, carry):
        step(pl.ds(pl.multiple_of(j * tile, tile), tile))
        return carry

    lax.fori_loop(0, width // tile, body, 0)


def dot(left, right, dims=(((1,), (0,)), ((), ()))):
    return lax.dot_general(left, right, dims, preferred_element_type=F32)


def softmax_parts(q, k):
    scores = dot(q, k, LAST) * (1.0 / math.sqrt(HEAD))
    powers = jnp.exp(scores - jnp.max(scores, axis=-1, keepdims=True))
    return powers / jnp.sum(powers, axis=-1, keepdims=True)


def head_columns(j):
    return pl.ds(pl.multiple_of(j * HEAD, HEAD), HEAD)


def heads_forward(b, images, query, keys, values, out):
    many, some = query.shape[0] // images, keys.shape[0] // images
    asked, told = pl.ds(b * many, many), pl.ds(b * some, some)

    def body(j, carry):
        cols = head_columns(j)
        probs = softmax_parts(query[asked, cols], keys[told, cols])
        out[asked, cols] = dot(probs.astype(LOW), values[told, cols]).astype(LOW)
        return carry

    lax.fori_loop(0, query.shape[1] // HEAD, body, 0)


def heads_back(images, query, keys, values, d_att):
    heads = query.shape[1] // HEAD
    many, some = query.shape[0] // images, keys.shape[0] // images
    scale = 1.0 / math.sqrt(HEAD)

    def body(j, carry):
        b = j // heads
        cols = head_columns(j % heads)
        asked = pl.ds(pl.multiple_of(b * many, many), many)
        told = pl.ds(pl.multiple_of(b * some, some), some)
        q, k, v, d = query[asked, cols], keys[told, cols], values[told, cols], d_att[asked, cols]
        probs = softmax_parts(q, k)
        d_probs = dot(d, v, LAST)
        weighted = jnp.sum(probs * d_probs, axis=-1, keepdims=True)
        d_scores = (probs * (d_probs - weighted)).astype(LOW)
        values[told, cols] = dot(probs.astype(LOW), d, FIRST).astype(LOW)
        keys[told, cols] = (dot(d_scores, q, FIRST) * scale).astype(LOW)
        query[asked, cols] = (dot(d_scores, k) * scale).astype(LOW)
        return carry

    lax.fori_loop(0, images * heads, body, 0)


def gelu(u):
    turn = jnp.tanh(math.sqrt(2.0 / math.pi) * (u + 0.044715 * (u * u * u)))
    return 0.5 * u * (1.0 + turn)


def gelu_slope(u):
    c = math.sqrt(2.0 / math.pi)
    turn = jnp.tanh(c * (u + 0.044715 * (u * u * u)))
    return 0.5 * (1.0 + turn) + 0.5 * u * (1.0 - turn * turn) * (c * (1.0 + 0.134145 * (u * u)))


def flat(array):
    return array.reshape(array.shape[0] * array.shape[1], array.shape[2])


def forward_all(pairs, number, given):
    t = given
    images, own, width = t.tokens.shape
    length, words = 4 * own, t.caption.shape[1]
    inner, ff, states = t.query_self.shape[1], t.up_proj.shape[1], t.caption.shape[2]
    rows, word_rows, word_own = images * length, images * words, words // 4
    chunks, text_chunks = ff // inner, states // inner
    half = width // 2
    vars_in = dict(
        tokens=t.tokens, caption=flat(t.caption), cotangent=t.cotangent, text_proj=t.text_proj,
        query_self=t.query_self, key_self=t.key_self, value_self=t.value_self, out_self=t.out_self,
        query_cross=t.query_cross, key_cross=t.key_cross, value_cross=t.value_cross,
        out_cross=t.out_cross, up_proj=t.up_proj,
    )
    sds = jax.ShapeDtypeStruct
    outs = dict(
        image_self=sds((rows, width), LOW), image_cross=sds((rows, width), LOW),
        image_feed=sds((rows, width), LOW), d_image=sds((rows, width), LOW),
        context=sds((word_rows, width), LOW),
        query_sa=sds((rows, inner), LOW), keys_sa=sds((rows, inner), LOW), values_sa=sds((rows, inner), LOW),
        query_ca=sds((rows, inner), LOW), keys_ca=sds((word_rows, inner), LOW), values_ca=sds((word_rows, inner), LOW),
        attended_sa=sds((rows, inner), LOW), attended_ca=sds((rows, inner), LOW),
        resid_mid=sds((images, own, width), F32), resid_late=sds((images, own, width), F32),
        activ=sds((rows, ff), LOW), pre_act=sds((images, length, ff), F32),
        nb_self=sds((rows, half), LOW), nb_low=sds((rows, half), LOW),
        nb_context=sds((word_rows, half), LOW), nb_first=sds((rows, inner), LOW),
    )

    def kernel(*refs):
        h = types.SimpleNamespace(**dict(zip(vars_in, refs)))
        refs = refs[len(vars_in):]
        marks, gain_self, gain_cross, gain_feed = refs[:4]
        refs = refs[4:]
        o = types.SimpleNamespace(**dict(zip(outs, refs)))
        refs = refs[len(outs):]
        scatter_refs, text_refs = refs[:5], refs[5:10]
        (full_s, full_c, full_f, full_d, full_x, gsem_s, gsem_c, gsem_f, gsem_d, gsem_x,
         wn, wt, tok, cot, cap, sq, sk, sv, xq, xk, xv, att_s, att_c, mid, late, act,
         fsem, osem, hsem, asem) = refs[10:]
        net = Narrow()
        fetch, store = Copies(fsem), Copies(osem)
        barrier = pltpu.get_barrier_semaphore()
        me = lax.axis_index(WIDE)
        greet(barrier, {WIDE: me + 1 - 2 * (me % 2)})
        others = net.meet(barrier) + 1

        def whole(j, ref):
            return fetch.start(ref, wn.at[j])

        def band(j, ref, c):
            return fetch.start(ref.at[pl.ds(c * inner, inner)], wt.at[j])

        need_tok = fetch.start(h.tokens, tok)
        need_cap = fetch.start(h.caption, cap)
        need_proj = [band(c, h.text_proj, c) for c in range(text_chunks)]
        need_cot = fetch.start(h.cotangent, cot)
        need_qkv = [whole(j, ref) for j, ref in enumerate((h.query_self, h.key_self, h.value_self))]
        need_out_self = fetch.start(h.out_self, wt.at[2])
        need_kv = [whole(4, h.key_cross), whole(5, h.value_cross)]
        need_query_cross = whole(3, h.query_cross)
        need_out_cross = fetch.start(h.out_cross, wt.at[3])
        need_up = {3: fetch.start(h.up_proj.at[:, pl.ds(3 * inner, inner)], wn.at[6])}
        gather_s = Gather(net, full_s, own, gsem_s)
        gather_c = Gather(net, full_c, own, gsem_c)
        gather_f = Gather(net, full_f, own, gsem_f)
        gather_d = Gather(net, full_d, own, gsem_d)
        gather_x = Gather(net, full_x, word_own, gsem_x)
        scatter, text = Scatter(net, *scatter_refs), Scatter(net, *text_refs)
        part = scatter.part

        def of(b, n=length):
            return pl.ds(b * n, n)

        need_tok.wait()
        pl.semaphore_wait(barrier, others)
        for b in range(images):
            mine = gather_s.mine(b)

            def step(s, b=b, mine=mine):
                normed, _ = norm_rows(tok[b, s, :].astype(F32))
                mine[s, :] = (normed * gain_self[...].astype(F32)[None]).astype(LOW)

            each_slab(own, step)
            gather_s.start(b)
        need_cap.wait()
        for need in need_proj:
            need.wait()
        for b in range(images):

            def step(cols, b=b):
                total = None
                for c in range(text_chunks):
                    term = dot(cap[of(b, words), pl.ds(c * inner, inner)], wt[c, :, cols])
                    total = term if total is None else total + term
                text.part[b, :, cols] = total

            columns_of(width, step)
            text.start(b)
        need_cot.wait()
        for b in range(images):
            mine = gather_d.mine(b)

            def step(s, b=b, mine=mine):
                mine[s, :] = (cot[b, s, :].astype(F32) * marks[b, s, :]).astype(LOW)

            each_slab(own, step)

        def project(b, source, weights, targets, n=length):
            for j, target in zip(weights, targets):
                target[of(b, n), :] = dot(source[of(b, n), :], wn[j]).astype(LOW)

        def back_out(b, attended, j):
            def step(cols):
                part[b, :, cols] = dot(attended[of(b), :], wt[j, :, cols])

            columns_of(width, step)
            scatter.start(b)

        gather_s.forward(0)
        text.cross(0)
        text.cross(1)
        gather_d.start(0)
        for b in range(images):
            gather_s.finish(b)
            if b == 0:
                for need in need_qkv:
                    need.wait()
            project(b, full_s, (0, 1, 2), (sq, sk, sv))
            if b + 1 < images:
                gather_s.forward(b + 1)
            heads_forward(b, images, sq, sk, sv, att_s)
            if b == 0:
                need_out_self.wait()
            back_out(b, att_s, 2)
            if b == 0:
                scatter.cross(b)
        store.later(full_s, o.image_self)
        for ref, out in ((sq, o.query_sa), (sk, o.keys_sa), (sv, o.values_sa), (att_s, o.attended_sa)):
            store.later(ref, out)
        for c in range(3):
            need_up[c] = fetch.start(h.up_proj.at[:, pl.ds(c * inner, inner)], wn.at[c])
        for b in range(images):
            text.ready(b)
            mine = gather_x.mine(b)

            def step(s, b=b, mine=mine):
                mine[s, :] = text.total(b, s).astype(LOW)

            each_slab(word_own, step)
        scatter.cross(1)
        for b in range(images):
            gather_x.start(b)
        halves_self = Halves(net, full_s, o.nb_self, pairs, hsem, 0)
        halves_self.start()

        def rows_out(b, source, target, gain, gather):
            scatter.ready(b)
            mine = gather.mine(b)

            def step(s):
                kept = source[b, s, :].astype(F32) + scatter.total(b, s)
                target[b, s, :] = kept
                normed, _ = norm_rows(kept)
                mine[s, :] = (normed * gain[...].astype(F32)[None]).astype(LOW)

            each_slab(own, step)
            gather.start(b)

        rows_out(0, tok, mid, gain_cross, gather_c)
        gather_d.start(1)
        for b in range(images):
            gather_x.forward(b)
        rows_out(1, tok, mid, gain_cross, gather_c)
        store.later(mid, o.resid_mid)
        for need in need_kv:
            need.wait()
        for b in range(images):
            gather_x.finish(b)
            project(b, full_x, (4, 5), (xk, xv), words)
            text.finish(b)
        halves_context = Halves(net, full_x, o.nb_context, pairs, hsem, 1)
        halves_context.start()
        store.later(full_x, o.context)
        store.later(xk, o.keys_ca)
        store.later(xv, o.values_ca)
        need_query_cross.wait()
        gather_c.forward(0)
        for b in range(images):
            gather_c.finish(b)
            project(b, full_c, (3,), (xq,))
            if b + 1 < images:
                gather_c.forward(b + 1)
            heads_forward(b, images, xq, xk, xv, att_c)
            scatter.finish(b)
            if b == 0:
                need_out_cross.wait()
            back_out(b, att_c, 3)
            if b == 0:
                for j in range(images):
                    gather_d.forward(j)
                scatter.cross(b)
                for j in range(images):
                    gather_d.finish(j)
                halves_low = Halves(net, full_d, o.nb_low, pairs, hsem, 2)
                halves_low.start()
                store.later(full_d, o.d_image)
        store.later(full_c, o.image_cross)
        store.later(xq, o.query_ca)
        store.later(att_c, o.attended_ca)
        scatter.cross(1)
        halves_self.forward()
        halves_context.forward()
        rows_out(0, mid, late, gain_feed, gather_f)
        rows_out(1, mid, late, gain_feed, gather_f)
        store.later(late, o.resid_late)
        halves_low.forward()
        first = [
            send(act.at[of(b), pl.ds(0, inner)], o.nb_first.at[of(b)], asem, (b,), {WIDE: me + 1 - 2 * (me % 2)})
            for b in range(images)
        ]
        gather_f.forward(0)
        for b in range(images):
            gather_f.finish(b)
            scatter.finish(b)
            for c in range(chunks):
                if b == 0:
                    need_up[c].wait()
                cols = pl.ds(c * inner, inner)
                part[b, :, cols] = dot(full_f[of(b), :], wn[6 if c == 3 else c])
                if b == 0 and c == 1:
                    gather_f.forward(1)

                def step(s, b=b, cols=cols):
                    act[pl.ds(pl.multiple_of(b * length + s.start, 16), 16), cols] = gelu(part[b, s, cols]).astype(LOW)

                each_slab(length, step)
                if c == 0:
                    first[b].start()
        store.later(act, o.activ)
        store.later(part, o.pre_act)
        store.later(full_f, o.image_feed)
        for halves in (halves_self, halves_context, halves_low):
            halves.arrive()
            halves.leave()
        for copy in first:
            copy.wait()
        store.close()

    V, DS = pltpu.VMEM, pltpu.SemaphoreType.DMA
    gsem = DS((2, images, 3))
    scratch = scatter_scratch(images, own, width) + scatter_scratch(images, word_own, width, F32)
    scratch += [V((rows, width), LOW)] * 4 + [V((word_rows, width), LOW)] + [gsem] * 5
    scratch += [
        V((7, width, inner), LOW), V((4, inner, width), LOW),
        V((images, own, width), LOW), V((images, own, width), LOW), V((word_rows, states), LOW),
        V((rows, inner), LOW), V((rows, inner), LOW), V((rows, inner), LOW),
        V((rows, inner), LOW), V((word_rows, inner), LOW), V((word_rows, inner), LOW),
        V((rows, inner), LOW), V((rows, inner), LOW),
        V((images, own, width), F32), V((images, own, width), F32), V((rows, ff), LOW),
        DS((40,)), DS((40,)), DS((2, 3, pairs + 1)), DS((2, images)),
    ]
    result = pl.pallas_call(
        kernel,
        out_shape=list(outs.values()),
        in_specs=[HB] * len(vars_in) + [VM] * 4,
        out_specs=[HB] * len(outs),
        scratch_shapes=scratch,
        compiler_params=params(number, 62),
        name="forward_all",
    )(*vars_in.values(), t.marks, *t.gains)
    return types.SimpleNamespace(**dict(zip(outs, result)))


def backward_all(pairs, number, given, kept):
    t = given
    images, own, width = t.tokens.shape
    length, words = 4 * own, t.caption.shape[1]
    inner, ff, states = t.query_self.shape[1], t.up_proj.shape[1], t.caption.shape[2]
    rows, word_rows, word_own = images * length, images * words, words // 4
    chunks, text_chunks = ff // inner, states // inner
    half, blk = width // 2, width // (2 * pairs)
    count = 2 * chunks + text_chunks + 8
    vars_in = dict(
        vars(kept),
        tokens=t.tokens, caption=flat(t.caption), cotangent=t.cotangent, text_proj=t.text_proj,
        query_self=t.query_self, key_self=t.key_self, value_self=t.value_self, out_self=t.out_self,
        query_cross=t.query_cross, key_cross=t.key_cross, value_cross=t.value_cross,
        out_cross=t.out_cross, up_proj=t.up_proj, down_proj=t.down_proj,
    )

    def kernel(*refs):
        h = types.SimpleNamespace(**dict(zip(vars_in, refs)))
        refs = refs[len(vars_in):]
        marks, gain_self, gain_cross, gain_feed = refs[:4]
        grads_out, words_out, tokens_out, layer_out, gain_out, nb_cols, nb_feed, nb_cross = refs[4:12]
        refs = refs[12:]
        scatter_refs = refs[:5]
        (full_c, full_s, full_x, gsem_c, gsem_s, gsem_x, text_sem,
         big, d_att, wa, wb, xq, xk, xv, sq, sk, sv, cot, late, mid, tok, low_rows, word_grad,
         fsem, osem, nbsem, hsem, gacc, gland, gsems) = refs[5:35]
        net = Narrow()
        units = []

        def unit(trade, rows_ref, nb_rows, columns, size, halves=None, early=None):
            i = len(units)
            there = nb_cols.at[i, pl.ds(0, size)] if early is None else early
            units.append(types.SimpleNamespace(
                trade=trade, rows=rows_ref, nb_rows=nb_rows, columns=columns, count=size, halves=halves,
                nb_columns=there, sems=nbsem, out=grads_out.at[i], early=early is not None,
            ))

        def chunk(ref, c):
            return ref.at[:, pl.ds(c * inner, inner)]

        halves_feed = Halves(net, h.image_feed, nb_feed, pairs, hsem, 0)
        for c in range(chunks):
            unit(True, h.d_image, h.nb_low, chunk(h.activ, c), rows, None, h.nb_first if c == 0 else None)
        for c in range(chunks):
            unit(True, h.image_feed, nb_feed, chunk(big, c), rows, halves_feed)
        unit(False, full_c, None, h.attended_ca, rows)
        unit(True, h.context, h.nb_context, xk, word_rows)
        unit(True, h.context, h.nb_context, xv, word_rows)
        halves_cross = Halves(net, h.image_cross, nb_cross, pairs, hsem, 1)
        unit(True, h.image_cross, nb_cross, xq, rows, halves_cross)
        for c in range(text_chunks):
            unit(False, full_x, None, chunk(h.caption, c), word_rows)
        unit(False, full_s, None, h.attended_sa, rows)
        unit(True, h.image_self, h.nb_self, sq, rows)
        unit(True, h.image_self, h.nb_self, sk, rows)
        unit(True, h.image_self, h.nb_self, sv, rows)
        wide = Wide(pairs, units, refs[35:])
        fetch, store = Copies(fsem), Copies(osem)

        def of(b, n=length):
            return pl.ds(b * n, n)

        barrier = pltpu.get_barrier_semaphore()
        far = {WIDE: (wide.z + 2) % pairs * 2 + wide.y}
        near = {WIDE: (wide.z + 1 - 2 * (wide.z % 2)) * 2 + wide.y}
        greet(barrier, far)
        others = wide.meet(barrier) + net.meet(barrier) + 1

        def up_chunk(c):
            return fetch.start(chunk(h.up_proj, c), wa.at[c % 2])

        need_image = fetch.start(h.d_image, full_s)

        def down_chunk(c):
            return fetch.start(h.down_proj.at[pl.ds(c * inner, inner)], wb.at[c % 2])

        need_down = {c: down_chunk(c) for c in range(2)}
        need_pre = fetch.start(h.pre_act, scatter_refs[0])
        need_up = {c: up_chunk(c) for c in range(2)}
        need_cot = fetch.start(h.cotangent, cot)
        need_late = fetch.start(h.resid_late, late)
        need_ca = [fetch.start(a, b) for a, b in ((h.query_ca, xq), (h.keys_ca, xk), (h.values_ca, xv))]
        need_mid = fetch.start(h.resid_mid, mid)
        need_sa = [fetch.start(a, b) for a, b in ((h.query_sa, sq), (h.keys_sa, sk), (h.values_sa, sv))]
        need_tok = fetch.start(h.tokens, tok)
        pl.semaphore_wait(barrier, others)
        wide.ask(1)
        wide.ask(2)
        wide.multiply(0)
        scatter = Scatter(net, *scatter_refs)
        part = scatter.part
        gather_c, gather_s = Gather(net, full_c, own, gsem_c), Gather(net, full_s, own, gsem_s)
        gather_x = Gather(net, full_x, word_own, gsem_x)

        need_image.wait()
        need_pre.wait()
        for c in range(chunks):
            need_down[c].wait()
            cols = pl.ds(c * inner, inner)
            for b in range(images):
                slope = dot(full_s[of(b), :], wb[c % 2], LAST)
                big[of(b), cols] = (gelu_slope(part[b, :, cols]) * slope).astype(LOW)
            if c + 2 < chunks:
                need_down[c + 2] = down_chunk(c + 2)
            if c == 1:
                wide.ask(3)
                halves_feed.start()
        need_out = fetch.start(h.out_cross, wb.at[0])
        need_out_self = fetch.start(h.out_self, wb.at[1])
        wide.multiply(1)
        wide.ask(4)
        wide.move(1)
        for c in range(chunks):
            need_up[c].wait()
            for b in range(images):

                def step(cols, b=b, c=c):
                    term = dot(big[of(b), pl.ds(c * inner, inner)], wa[c % 2, cols, :], LAST)
                    part[b, :, cols] = term if c == 0 else part[b, :, cols] + term

                columns_of(width, step)
                if c == chunks - 1:
                    scatter.start(b)
            if c + 2 < chunks:
                need_up[c + 2] = up_chunk(c + 2)
        need_query = fetch.start(h.query_cross, wa.at[0])
        need_key = fetch.start(h.key_cross, wa.at[1])
        gacc[...] = jnp.zeros_like(gacc)

        def back_rows(b, above, mask, source, gain, slot, keep, mine):
            scatter.ready(b)

            def step(s):
                d_hidden = scatter.total(b, s)
                normed, inv_std = norm_rows(source[b, s, :].astype(F32))
                gacc[slot : slot + 1, :] += jnp.sum(d_hidden * normed, axis=0, keepdims=True)
                top = above[b, s, :].astype(F32)
                if mask is not None:
                    top = top * mask[b, s, :]
                scaled = d_hidden * gain[...].astype(F32)[None]
                inside = scaled - jnp.mean(scaled, axis=-1, keepdims=True)
                inside = inside - normed * jnp.mean(scaled * normed, axis=-1, keepdims=True)
                d_rows = top + inv_std * inside
                if keep is not None:
                    keep[b, s, :] = d_rows
                mine[s, :] = d_rows.astype(LOW)

            each_slab(own, step)

        def multiply(b, target, lefts, rights, n=length):
            def step(cols):
                total = None
                for left, j in zip(lefts, rights):
                    term = dot(left[of(b, n), :], wa[j, cols, :], LAST)
                    total = term if total is None else total + term
                target[b, :, cols] = total

            columns_of(width, step)

        def out_back(b, full, j):
            d_att[of(b), :] = dot(full[of(b), :], wb[j], LAST).astype(LOW)

        wide.multiply(2)
        wide.ask(5)
        wide.move(2)
        for b in range(images):
            scatter.cross(b)
        wide.multiply(3)
        wide.ask(6)
        need_cot.wait()
        need_late.wait()
        for b in range(images):
            back_rows(b, cot, marks, late, gain_feed, 2, late, gather_c.mine(b))
            gather_c.start(b)
        wide.move(3)
        for b in range(images):
            gather_c.forward(b)
        halves_feed.forward()
        wide.multiply(4)
        wide.ask(7)
        need_out.wait()
        for b in range(images):
            scatter.finish(b)
            gather_c.finish(b)
            out_back(b, full_c, 0)
        need_text = fetch.start(h.text_proj.at[pl.ds(0, inner)], wb.at[0])
        wide.move(4)
        for need in need_ca:
            need.wait()
        heads_back(images, xq, xk, xv, d_att)
        need_query.wait()
        for b in range(images):
            multiply(b, part, [xq], [0])
            scatter.start(b)
        need_value = fetch.start(h.value_cross, wa.at[0])
        wide.multiply(5)
        for b in range(images):
            scatter.cross(b)
        wide.multiply(6)
        wide.move(5)
        need_mid.wait()
        for b in range(images):
            back_rows(b, late, None, mid, gain_cross, 1, mid, gather_s.mine(b))
            gather_s.start(b)
        need_again = fetch.start(h.resid_late, late)
        wide.multiply(7)
        wide.multiply(8)
        wide.ask(9)
        wide.ask(10)
        halves_cross.start()
        for b in range(images):
            gather_s.forward(b)
        wide.move(6)
        for b in range(images):
            scatter.finish(b)
            gather_s.finish(b)
        text = Scatter(
            net, part.at[:, pl.ds(0, words)], scatter.landed.at[:, :, pl.ds(0, word_own)],
            scatter.outgoing.at[:, pl.ds(0, word_own)], scatter.arrived.at[:, pl.ds(0, word_own)], text_sem,
        )
        need_key.wait()
        need_value.wait()
        for b in range(images):
            multiply(b, text.part, [xk, xv], [1, 0], words)
            text.start(b)
        need_qkv = [fetch.start(h.query_self, wa.at[0]), fetch.start(h.key_self, wa.at[1])]
        need_out_self.wait()
        for b in range(images):
            out_back(b, full_s, 1)
        need_second = fetch.start(h.text_proj.at[pl.ds(inner, inner)], wb.at[1])
        for b in range(images):
            text.cross(b)
        for need in need_sa:
            need.wait()
        heads_back(images, sq, sk, sv, d_att)
        wide.move(7)
        for b in range(images):
            text.ready(b)
            mine = gather_x.mine(b)

            def step(s, b=b, mine=mine):
                mine[s, :] = text.total(b, s).astype(LOW)

            each_slab(word_own, step)
            gather_x.start(b)
        for b in range(images):
            gather_x.forward(b)
        wide.multiply(9)
        wide.ask(11)
        for b in range(images):
            text.finish(b)
            gather_x.finish(b)
        for c, need in enumerate((need_text, need_second)):
            need.wait()
            word_grad[:, pl.ds(c * inner, inner)] = dot(full_x[...], wb[c], LAST).astype(LOW)
        store.later(word_grad, words_out)
        need_down = {c: down_chunk(c) for c in range(2)}
        wide.move(8)
        for need in need_qkv:
            need.wait()
        for b in range(images):
            multiply(b, part, [sq, sk], [0, 1])
        need_value = fetch.start(h.value_self, wa.at[0])
        for c in range(chunks):
            wide.leave(chunks + c)
        need_act = fetch.start(h.activ, big)
        wide.multiply(10)
        halves_cross.forward()
        need_value.wait()
        for b in range(images):

            def step(cols, b=b):
                part[b, :, cols] += dot(sv[of(b), :], wa[0, cols, :], LAST)

            columns_of(width, step)
            scatter.start(b)
        wide.multiply(11)
        wide.move(9)
        for b in range(images):
            scatter.cross(b)
        wide.multiply(12)
        wide.move(10)
        need_tok.wait()
        for b in range(images):
            back_rows(b, mid, None, tok, gain_self, 0, None, low_rows.at[b])
        store.later(low_rows, tokens_out)
        for b in range(images):
            scatter.finish(b)
        wide.multiply(13)
        wide.ask(15)
        wide.move(11)
        for j, peer in enumerate((net.core, net.chip, wide.peer, near, far)):
            trip = send(gacc, gland.at[j], gsems, (j,), peer)
            trip.start()
            trip.wait()
            gacc[...] = gacc[...] + gland[j]
        store.later(gacc, gain_out)
        wide.multiply(14)
        wide.ask(16)
        wide.move(12)
        need_act.wait()
        for c in range(chunks):
            need_down[c].wait()
            for b in range(images):

                def step(cols, b=b, c=c):
                    term = dot(big[of(b), pl.ds(c * inner, inner)], wb[c % 2, :, cols])
                    part[b, :, cols] = term if c == 0 else part[b, :, cols] + term

                columns_of(width, step)
            if c + 2 < chunks:
                need_down[c + 2] = down_chunk(c + 2)
            if c == 1:
                wide.multiply(15)
                wide.ask(17)
                wide.move(13)
        for b in range(images):
            scatter.start(b)
        wide.multiply(16)
        wide.move(14)
        for b in range(images):
            scatter.cross(b)
        wide.multiply(17)
        wide.move(15)
        need_again.wait()
        for b in range(images):
            scatter.ready(b)

            def step(s, b=b):
                tok[b, s, :] = (late[b, s, :] + scatter.total(b, s)).astype(LOW)

            each_slab(own, step)
            scatter.finish(b)
        store.later(tok, layer_out)
        for k in range(16, count + pairs - 1):
            wide.move(k)
        wide.drain()
        halves_feed.leave()
        halves_cross.leave()
        store.close()

    V, DS = pltpu.VMEM, pltpu.SemaphoreType.DMA
    gsem = DS((2, images, 3))
    sums = 2 + text_chunks
    scratch = scatter_scratch(images, own, width)
    scratch += [V((rows, width), LOW), V((rows, width), LOW), V((word_rows, width), LOW)] + [gsem] * 4
    scratch += [
        V((rows, ff), LOW), V((rows, inner), LOW), V((2, width, inner), LOW), V((2, inner, width), LOW),
        V((rows, inner), LOW), V((word_rows, inner), LOW), V((word_rows, inner), LOW),
        V((rows, inner), LOW), V((rows, inner), LOW), V((rows, inner), LOW),
        V((images, own, width), LOW), V((images, own, width), F32), V((images, own, width), F32),
        V((images, own, width), LOW), V((images, own, width), LOW), V((word_rows, states), LOW),
        DS((48,)), DS((8,)), DS((2, count)), DS((2, 2, pairs + 1)), V((8, width), F32), V((5, 8, width), F32), DS((2, 5)),
    ]
    scratch += [
        V((HELD, pairs, blk, inner), LOW), V((2, pairs, blk, inner), LOW), V((sums, pairs, blk, inner), LOW),
        V((RING, pairs - 1, blk, inner), LOW), V((RING, pairs - 1, blk, inner), LOW), V((2, blk, inner), LOW),
        V((2, 2, pairs, rows, blk), LOW), V((2, 2, rows, inner), LOW),
        DS((2, sums, pairs)), DS((2, count, pairs - 1)), DS((2, count, pairs - 1)),
        DS((2, 2, pairs)), DS((2, 2)), DS((2,)),
        pltpu.SemaphoreType.REGULAR, pltpu.SemaphoreType.REGULAR,
    ]
    sds = jax.ShapeDtypeStruct
    result = pl.pallas_call(
        kernel,
        out_shape=[
            sds((count, blk, inner), LOW), sds((word_rows, states), LOW), sds((images, own, width), LOW),
            sds((images, own, width), LOW), sds((8, width), F32), sds((count, rows, inner), LOW), sds((rows, half), LOW),
            sds((rows, half), LOW),
        ],
        in_specs=[HB] * len(vars_in) + [VM] * 4,
        out_specs=[HB] * 8,
        scratch_shapes=scratch,
        compiler_params=params(number, 62),
        name="backward_all",
    )(*vars_in.values(), t.marks, *t.gains)
    return result[:5]


def spread(blocks, places, shapes, whole, gains):
    count, blk, inner = blocks.shape
    more = len(whole)

    def kernel(*refs):
        blocks_ref, whole_in, gains_ref, refs = refs[0], refs[1 : 1 + more], refs[1 + more], refs[2 + more :]
        outs, whole_out, refs = refs[: len(shapes)], refs[len(shapes) : len(shapes) + more], refs[len(shapes) + more :]
        gains_out, refs = refs[:3], refs[3:]
        for j, row in enumerate(gains_out):
            row[...] = gains_ref[j, :]
        held, flat_stage, turned_stage, isem, osem, wsem, *kept = refs
        ins = [pltpu.make_async_copy(blocks_ref.at[i], held.at[i], isem.at[i]) for i in range(count)]
        for copy in ins:
            copy.start()
        done, plain, turns = [], 0, 0
        came = [pltpu.make_async_copy(whole_in[j], kept[j], wsem.at[0, j]) for j in range(more)]
        for copy in came:
            copy.start()
        for i, (which, row, col, turned) in enumerate(places):
            ins[i].wait()
            if turned:
                stage = turned_stage.at[turns]
                turns += 1
                for j in range(0, inner, 128):
                    stage[pl.ds(j, 128), :] = held[i, :, pl.ds(j, 128)].astype(F32).T
                place = outs[which].at[pl.ds(row, inner), pl.ds(col, blk)]
            else:
                stage = flat_stage.at[plain]
                plain += 1
                stage[...] = held[i].astype(F32)
                place = outs[which].at[pl.ds(row, blk), pl.ds(col, inner)]
            done.append(pltpu.make_async_copy(stage, place, osem.at[i]))
            done[-1].start()
        for j in range(more):
            came[j].wait()
            done.append(pltpu.make_async_copy(kept[j], whole_out[j], wsem.at[1, j]))
            done[-1].start()
        for copy in done:
            copy.wait()

    turns = sum(1 for place in places if place[3])
    V, DS = pltpu.VMEM, pltpu.SemaphoreType.DMA
    return pl.pallas_call(
        kernel,
        out_shape=[jax.ShapeDtypeStruct(shape, F32) for shape in shapes]
        + [jax.ShapeDtypeStruct(array.shape, array.dtype) for array in whole]
        + [jax.ShapeDtypeStruct(gains.shape[1:], F32)] * 3,
        in_specs=[HB] * (1 + more) + [VM],
        out_specs=[HB] * (len(shapes) + more) + [VM] * 3,
        scratch_shapes=[
            V((count, blk, inner), LOW), V((count - turns, blk, inner), F32), V((turns, inner, blk), F32),
            DS((count,)), DS((count,)), DS((2, more)),
        ] + [V(array.shape, array.dtype) for array in whole],
        compiler_params=pltpu.CompilerParams(vmem_limit_bytes=62 * 1024 * 1024),
        name="spread",
    )(blocks, *whole, gains)


def by_kernels(
    tokens, caption, token_mask, cotangent, gain_self, gain_cross, gain_feed, text_proj,
    query_self, key_self, value_self, out_self, query_cross, key_cross, value_cross, out_cross, up_proj, down_proj,
):
    given = types.SimpleNamespace(
        tokens=tokens, caption=caption, cotangent=cotangent, text_proj=text_proj,
        query_self=query_self, key_self=key_self, value_self=value_self, out_self=out_self,
        query_cross=query_cross, key_cross=key_cross, value_cross=value_cross, out_cross=out_cross,
        up_proj=up_proj, down_proj=down_proj, marks=token_mask[:, :, None].astype(F32),
        gains=[gain_self, gain_cross, gain_feed],
    )
    pairs = lax.axis_size(WIDE) // 2
    kept = forward_all(pairs, 1, given)
    grads, d_words, d_tokens, layer_out, gains = backward_all(pairs, 2, given, kept)
    inner = query_self.shape[1]
    blk = query_self.shape[0] // (2 * pairs)
    ff, text = up_proj.shape[1] // inner, caption.shape[2] // inner
    places = [(10, c * inner, 0, True) for c in range(ff)]
    places += [(9, 0, c * inner, False) for c in range(ff)]
    places += [(8, 0, 0, True), (6, 0, 0, False), (7, 0, 0, False), (5, 0, 0, False)]
    places += [(0, c * inner, 0, True) for c in range(text)]
    places += [(4, 0, 0, True), (1, 0, 0, False), (2, 0, 0, False), (3, 0, 0, False)]
    shapes = [(text * inner, blk)] + [(blk, inner)] * 3 + [(inner, blk)] + [(blk, inner)] * 3 + [(inner, blk)]
    shapes += [(blk, ff * inner), (ff * inner, blk)]
    out = spread(grads, places, shapes, [layer_out, d_tokens, d_words], gains)
    sums, (layer_out, d_tokens, d_words, *gains) = out[: len(shapes)], out[len(shapes) :]
    return (layer_out, d_tokens, d_words.reshape(caption.shape), *gains, *sums)


def local(
    tokens,
    caption,
    token_mask,
    cotangent,
    gain_self,
    gain_cross,
    gain_feed,
    text_proj,
    query_self,
    key_self,
    value_self,
    out_self,
    query_cross,
    key_cross,
    value_cross,
    out_cross,
    up_proj,
    down_proj,
):
    given = (tokens, caption, token_mask, cotangent, gain_self, gain_cross, gain_feed, text_proj, query_self, key_self, value_self, out_self, query_cross, key_cross, value_cross, out_cross, up_proj, down_proj)
    if lax.axis_size(WIDE) != 8 or lax.axis_size(NARROW) != 4:
        return by_collectives(*given)
    return by_kernels(*given)


def solution(mesh):
    in_specs = (
        P(WIDE, NARROW, None),
        P(WIDE, None, NARROW),
        P(WIDE, NARROW),
        P(WIDE, NARROW, None),
        P(),
        P(),
        P(),
        P(NARROW, None),
        P(None, NARROW),
        P(None, NARROW),
        P(None, NARROW),
        P(NARROW, None),
        P(None, NARROW),
        P(None, NARROW),
        P(None, NARROW),
        P(NARROW, None),
        P(None, NARROW),
        P(NARROW, None),
    )
    out_specs = (
        P(WIDE, NARROW, None),
        P(WIDE, NARROW, None),
        P(WIDE, None, NARROW),
        P(),
        P(),
        P(),
        P(NARROW, WIDE),
        P(WIDE, NARROW),
        P(WIDE, NARROW),
        P(WIDE, NARROW),
        P(NARROW, WIDE),
        P(WIDE, NARROW),
        P(WIDE, NARROW),
        P(WIDE, NARROW),
        P(NARROW, WIDE),
        P(WIDE, NARROW),
        P(NARROW, WIDE),
    )
    return jax.shard_map(local, mesh=mesh, in_specs=in_specs, out_specs=out_specs, check_vma=False)
```

```python
import math
import types

import jax
import jax.numpy as jnp
from jax import lax
from jax.experimental import pallas as pl
from jax.experimental.pallas import tpu as pltpu
from jax.sharding import PartitionSpec as P

HEAD = 128
MESH = pl.DeviceIdType.MESH
WIDE, NARROW = "wide", "narrow"
LOW, F32 = jnp.bfloat16, jnp.float32
LAST, FIRST = (((1,), (1,)), ((), ())), (((0,), (0,)), ((), ()))

def normalize(rows):
    centre = jnp.mean(rows, axis=-1, keepdims=True)
    centred = rows - centre
    variance = jnp.mean(centred * centred, axis=-1, keepdims=True)
    inv_std = lax.rsqrt(variance + 1e-05)
    return (centred * inv_std, inv_std)


def norm_back(d_normed, normed, inv_std):
    inner = d_normed - jnp.mean(d_normed, axis=-1, keepdims=True)
    inner = inner - normed * jnp.mean(d_normed * normed, axis=-1, keepdims=True)
    return inv_std * inner


def times_weight(left, right):
    return jnp.dot(left, right, preferred_element_type=jnp.float32)


def split_heads(matrix):
    return matrix.reshape(matrix.shape[0], matrix.shape[1], matrix.shape[2] // HEAD, HEAD)


def join_heads(heads):
    return heads.reshape(heads.shape[0], heads.shape[1], heads.shape[2] * HEAD)


def head_scores(query, keys):
    scores = jnp.einsum(
        "bqhe,bkhe->bhqk", split_heads(query), split_heads(keys), preferred_element_type=jnp.float32
    )
    return scores * (1.0 / math.sqrt(HEAD))


def attend(query, keys, values):
    scores = head_scores(query, keys)
    peak = jnp.max(scores, axis=-1, keepdims=True)
    powers = jnp.exp(scores - peak)
    summed = jnp.sum(powers, axis=-1, keepdims=True)
    low_probs = (powers / summed).astype(jnp.bfloat16)
    attended = jnp.einsum(
        "bhqk,bkhe->bqhe", low_probs, split_heads(values), preferred_element_type=jnp.float32
    )
    return join_heads(attended).astype(jnp.bfloat16), peak + jnp.log(summed)


def attend_back(query, keys, values, log_total, d_attended):
    probs = jnp.exp(head_scores(query, keys) - log_total)
    low_probs = probs.astype(jnp.bfloat16)
    d_heads = split_heads(d_attended)
    d_probs = jnp.einsum(
        "bqhe,bkhe->bhqk", d_heads, split_heads(values), preferred_element_type=jnp.float32
    )
    d_values = jnp.einsum("bhqk,bqhe->bkhe", low_probs, d_heads, preferred_element_type=jnp.float32)
    weighted = jnp.sum(probs * d_probs, axis=-1, keepdims=True)
    d_scores = (probs * (d_probs - weighted)).astype(jnp.bfloat16)
    scale = 1.0 / math.sqrt(HEAD)
    d_query = (
        jnp.einsum("bhqk,bkhe->bqhe", d_scores, split_heads(keys), preferred_element_type=jnp.float32)
        * scale
    )
    d_keys = (
        jnp.einsum("bhqk,bqhe->bkhe", d_scores, split_heads(query), preferred_element_type=jnp.float32)
        * scale
    )
    return tuple(join_heads(d).astype(jnp.bfloat16) for d in (d_query, d_keys, d_values))


def contract(left, right):
    return lax.dot_general(
        left, right, (((0, 1), (0, 1)), ((), ())), preferred_element_type=jnp.float32
    ).astype(jnp.bfloat16)


def against(left, right):
    return lax.dot_general(
        left, right, (((2,), (1,)), ((), ())), preferred_element_type=jnp.float32
    )


def group_rows(piece):
    return lax.all_gather(piece, NARROW, axis=1, tiled=True)


def own_rows(partial):
    return lax.psum_scatter(partial, NARROW, scatter_dimension=1, tiled=True)


def feed_back(partial):
    return own_rows(partial.astype(jnp.bfloat16)).astype(jnp.float32)


def text_total(partial):
    return lax.psum(partial, NARROW)


def by_collectives(
    tokens,
    caption,
    token_mask,
    cotangent,
    gain_self,
    gain_cross,
    gain_feed,
    text_proj,
    query_self,
    key_self,
    value_self,
    out_self,
    query_cross,
    key_cross,
    value_cross,
    out_cross,
    up_proj,
    down_proj,
):
    gain_one = gain_self.astype(jnp.float32)
    gain_two = gain_cross.astype(jnp.float32)
    gain_three = gain_feed.astype(jnp.float32)
    low = jnp.bfloat16

    resid_in = tokens.astype(jnp.float32)
    normed_self, inv_self = normalize(resid_in)
    image_self = group_rows((normed_self * gain_one).astype(low))
    query_sa = times_weight(image_self, query_self).astype(low)
    keys_sa = times_weight(image_self, key_self).astype(low)
    values_sa = times_weight(image_self, value_self).astype(low)
    attended_sa, total_sa = attend(query_sa, keys_sa, values_sa)
    resid_mid = resid_in + own_rows(times_weight(attended_sa, out_self))
    context = text_total(times_weight(caption, text_proj)).astype(low)
    keys_ca = times_weight(context, key_cross).astype(low)
    values_ca = times_weight(context, value_cross).astype(low)
    normed_cross, inv_cross = normalize(resid_mid)
    image_cross = group_rows((normed_cross * gain_two).astype(low))
    query_ca = times_weight(image_cross, query_cross).astype(low)
    attended_ca, total_ca = attend(query_ca, keys_ca, values_ca)
    resid_late = resid_mid + own_rows(times_weight(attended_ca, out_cross))
    normed_feed, inv_feed = normalize(resid_late)
    d_result = cotangent.astype(jnp.float32) * token_mask[:, :, None].astype(jnp.float32)
    d_image = group_rows(d_result.astype(low))
    image_feed = group_rows((normed_feed * gain_three).astype(low))
    pre_act = times_weight(image_feed, up_proj)
    gelu_out, gelu_pull = jax.vjp(jax.nn.gelu, pre_act)
    activ = gelu_out.astype(low)
    resid_out = resid_late + feed_back(times_weight(activ, down_proj))
    d_pre = gelu_pull(against(d_image, down_proj))[0].astype(low)
    part_down = contract(activ, d_image)
    part_up = contract(image_feed, d_pre)
    d_hidden_feed = feed_back(against(d_pre, up_proj))
    part_gain_feed = jnp.sum(d_hidden_feed * normed_feed, axis=(0, 1))
    d_late = d_result + norm_back(d_hidden_feed * gain_three, normed_feed, inv_feed)
    d_image_cross = group_rows(d_late.astype(low))
    part_out_cross = contract(attended_ca, d_image_cross)
    d_attended_ca = against(d_image_cross, out_cross).astype(low)
    d_query_ca, d_keys_ca, d_values_ca = attend_back(
        query_ca, keys_ca, values_ca, total_ca, d_attended_ca
    )
    part_query_cross = contract(image_cross, d_query_ca)
    part_key_cross = contract(context, d_keys_ca)
    part_value_cross = contract(context, d_values_ca)
    d_hidden_cross = own_rows(against(d_query_ca, query_cross))
    d_context = text_total(against(d_keys_ca, key_cross) + against(d_values_ca, value_cross))
    d_context = d_context.astype(low)
    part_text = contract(caption, d_context)
    d_words = against(d_context, text_proj).astype(low)
    part_gain_cross = jnp.sum(d_hidden_cross * normed_cross, axis=(0, 1))
    d_mid = d_late + norm_back(d_hidden_cross * gain_two, normed_cross, inv_cross)
    d_image_self = group_rows(d_mid.astype(low))
    part_out_self = contract(attended_sa, d_image_self)
    d_attended_sa = against(d_image_self, out_self).astype(low)
    d_query_sa, d_keys_sa, d_values_sa = attend_back(
        query_sa, keys_sa, values_sa, total_sa, d_attended_sa
    )
    part_query_self = contract(image_self, d_query_sa)
    part_key_self = contract(image_self, d_keys_sa)
    part_value_self = contract(image_self, d_values_sa)
    d_hidden_self = own_rows(
        against(d_query_sa, query_self)
        + against(d_keys_sa, key_self)
        + against(d_values_sa, value_self)
    )
    part_gain_self = jnp.sum(d_hidden_self * normed_self, axis=(0, 1))
    d_input = d_mid + norm_back(d_hidden_self * gain_one, normed_self, inv_self)
    parts = (
        part_text,
        part_query_self,
        part_key_self,
        part_value_self,
        part_out_self,
        part_query_cross,
        part_key_cross,
        part_value_cross,
        part_out_cross,
        part_up,
        part_down,
    )
    dims = (1, 0, 0, 0, 1, 0, 0, 0, 1, 0, 1)
    summed = [
        lax.psum_scatter(part, WIDE, scatter_dimension=dim, tiled=True)
        for part, dim in zip(parts, dims)
    ]
    gains = lax.psum((part_gain_self, part_gain_cross, part_gain_feed), (WIDE, NARROW))
    return (
        resid_out.astype(low),
        d_input.astype(low),
        d_words,
        *gains,
        *[part.astype(jnp.float32) for part in summed],
    )


RING = 6
HELD = 8


def send(src, dst, sems, index, peer):
    return pltpu.make_async_remote_copy(
        src_ref=src,
        dst_ref=dst,
        send_sem=sems.at[(0,) + index],
        recv_sem=sems.at[(1,) + index],
        device_id=peer,
        device_id_type=MESH,
    )


def greet(barrier, peer):
    pl.semaphore_signal(barrier, inc=1, device_id=peer, device_id_type=MESH)


def each_slab(count, step, slab=16):
    def body(i, carry):
        step(pl.ds(pl.multiple_of(i * slab, slab), slab))
        return carry

    lax.fori_loop(0, count // slab, body, 0)


class Wide:
    def __init__(self, pairs, units, refs):
        (self.mine, self.right, self.left, self.stage, self.aslot, self.bslot, self.rsem, self.lsem, self.asem,
         self.bsem, self.osem, self.rfree, self.lfree) = refs
        self.pairs, self.units = pairs, units
        self.asked, self.gone = set(), set()
        me = lax.axis_index(WIDE)
        self.z, self.y = me // 2, me % 2
        self.has_right, self.has_left = self.z < pairs - 1, self.z > 0
        self.peer = {WIDE: self.z * 2 + 1 - self.y}
        self.next = {WIDE: jnp.minimum(self.z + 1, pairs - 1) * 2 + self.y}
        self.last = {WIDE: jnp.maximum(self.z - 1, 0) * 2 + self.y}
        group = -1
        for i, unit in enumerate(units):
            if i == 0 or unit.rows is not units[i - 1].rows:
                group += 1
            unit.group = group
        self.blk, self.cols = self.mine.shape[2], self.mine.shape[3]

    def meet(self, barrier):
        greet(barrier, self.peer)

        @pl.when(self.has_right)
        def _():
            greet(barrier, self.next)

        @pl.when(self.has_left)
        def _():
            greet(barrier, self.last)

        return 1 + self.has_right.astype(jnp.int32) + self.has_left.astype(jnp.int32)

    def trade(self, i):
        unit = self.units[i]
        return send(unit.columns, unit.nb_columns, unit.sems, (i,), self.peer)

    def loads(self, i):
        unit = self.units[i]
        s, rows = unit.group % 2, unit.count
        copies = []
        if i == 0 or self.units[i - 1].group != unit.group:
            for k in range(self.pairs):
                at = pl.multiple_of((k * 2 + self.y) * self.blk, self.blk)
                sources = (unit.rows.at[:, pl.ds(at, self.blk)], unit.nb_rows.at[:, pl.ds(k * self.blk, self.blk)])
                for part, src in enumerate(sources):
                    copies.append(
                        pltpu.make_async_copy(
                            src, self.aslot.at[s, part, k, pl.ds(0, rows)], self.asem.at[s, part, k]
                        )
                    )
        q = i % 2
        for part, src in enumerate((unit.columns, unit.nb_columns)):
            copies.append(
                pltpu.make_async_copy(src, self.bslot.at[q, part, pl.ds(0, rows)], self.bsem.at[q, part])
            )
        return copies

    def load(self, i):
        unit = self.units[i]
        if not unit.early:
            self.trade(i).wait_recv()
        if unit.halves is not None and (i == 0 or self.units[i - 1].group != unit.group):
            unit.halves.arrive()
        for copy in self.loads(i):
            copy.start()

    def compute(self, i):
        unit = self.units[i]
        s, q, g, rows = unit.group % 2, i % 2, i % HELD, unit.count
        for copy in self.loads(i):
            copy.wait()
        if i >= HELD:
            self.sent(i - HELD)

        def body(k, carry):
            total = None
            for part in (0, 1):
                term = lax.dot_general(
                    self.aslot[s, part, k, :rows], self.bslot[q, part, :rows], FIRST, preferred_element_type=F32
                )
                total = term if total is None else total + term
            self.mine[g, k] = total.astype(LOW)
            return carry

        lax.fori_loop(0, self.pairs, body, 0)

    def add(self, dst, src):
        def step(s):
            dst[s, :] = dst[s, :] + src[s, :]

        each_slab(self.blk, step, 64)

    def r_copy(self, i, t):
        d = jnp.clip(self.pairs - t + self.z, 0, self.pairs - 1)
        return send(self.mine.at[i % HELD, d], self.right.at[i % RING, t - 1], self.rsem, (i, t - 1), self.next)

    def l_copy(self, i, t):
        d = jnp.clip(t - self.pairs + self.z, 0, self.pairs - 1)
        return send(self.mine.at[i % HELD, d], self.left.at[i % RING, t - 1], self.lsem, (i, t - 1), self.last)

    def sends_right(self, t):
        return self.has_right & (t >= self.z + 1)

    def sends_left(self, t):
        return self.has_left & (t >= self.pairs - self.z)

    def credit(self, i, free, when):
        if i >= RING:

            @pl.when(when)
            def _():
                pl.semaphore_wait(free, 1)

    def release(self, i):
        @pl.when(self.z == 0)
        def _():
            if i >= RING:
                pl.semaphore_wait(self.rfree, 1)
            for t in range(1, self.pairs):
                self.r_copy(i, t).start()

        @pl.when(self.z == self.pairs - 1)
        def _():
            if i >= RING:
                pl.semaphore_wait(self.lfree, 1)
            for t in range(1, self.pairs):
                self.l_copy(i, t).start()

    def step(self, i, t):
        g, r = i % HELD, i % RING
        first_right, first_left = t == self.z + 1, t == self.pairs - self.z

        @pl.when(self.sends_right(t) & self.has_left)
        def _():
            self.credit(i, self.rfree, first_right)
            self.r_copy(i, t - 1).wait_recv()
            d = jnp.clip(self.pairs - t + self.z, 0, self.pairs - 1)
            self.add(self.mine.at[g, d], self.right.at[r, t - 2])
            self.r_copy(i, t).start()

        @pl.when(self.sends_left(t) & self.has_right)
        def _():
            self.credit(i, self.lfree, first_left)
            self.l_copy(i, t - 1).wait_recv()
            d = jnp.clip(t - self.pairs + self.z, 0, self.pairs - 1)
            self.add(self.mine.at[g, d], self.left.at[r, t - 2])
            self.l_copy(i, t).start()

    def out_copy(self, i):
        return pltpu.make_async_copy(self.stage.at[i % 2], self.units[i].out, self.osem.at[i % 2])

    def final(self, i):
        g, r, t = i % HELD, i % RING, self.pairs - 1

        @pl.when(self.has_left)
        def _():
            self.r_copy(i, t).wait_recv()
            self.add(self.mine.at[g, self.z], self.right.at[r, t - 1])

        @pl.when(self.has_right)
        def _():
            self.l_copy(i, t).wait_recv()
            self.add(self.mine.at[g, self.z], self.left.at[r, t - 1])

        if i + RING < len(self.units):

            @pl.when(self.has_left)
            def _():
                pl.semaphore_signal(self.rfree, inc=1, device_id=self.last, device_id_type=MESH)

            @pl.when(self.has_right)
            def _():
                pl.semaphore_signal(self.lfree, inc=1, device_id=self.next, device_id_type=MESH)

        if i >= 2:
            self.out_copy(i - 2).wait()

        def step(s):
            self.stage[i % 2, s, :] = self.mine[g, self.z, s, :]

        each_slab(self.blk, step, 64)
        self.out_copy(i).start()

    def sent(self, i):
        for t in range(1, self.pairs):

            @pl.when(self.sends_right(t))
            def _():
                self.r_copy(i, t).wait_send()

            @pl.when(self.sends_left(t))
            def _():
                self.l_copy(i, t).wait_send()

    def ask(self, i):
        if i < len(self.units) and not self.units[i].early and i not in self.asked:
            self.asked.add(i)
            self.trade(i).start()

    def move(self, k):
        count, pairs = len(self.units), self.pairs
        for t in range(pairs - 1, 1, -1):
            if 0 <= k - (t - 1) < count:
                self.step(k - (t - 1), t)
        if 0 <= k - (pairs - 1) < count:
            self.final(k - (pairs - 1))

    def leave(self, i):
        if not self.units[i].early and i not in self.gone:
            self.gone.add(i)
            self.trade(i).wait_send()

    def multiply(self, i, loaded=False):
        if not loaded:
            self.load(i)
        self.compute(i)
        self.release(i)

    def drain(self):
        count = len(self.units)
        for i in range(max(0, count - 2), count):
            self.out_copy(i).wait()
        for i in range(max(0, count - HELD), count):
            self.sent(i)
        for i in range(count):
            self.leave(i)


VM = pl.BlockSpec(memory_space=pltpu.VMEM)
HB = pl.BlockSpec(memory_space=pl.ANY)


def norm_rows(rows):
    centre = jnp.mean(rows, axis=-1, keepdims=True)
    centred = rows - centre
    variance = jnp.mean(centred * centred, axis=-1, keepdims=True)
    inv_std = lax.rsqrt(variance + 1e-05)
    return centred * inv_std, inv_std


class Narrow:
    def __init__(self):
        self.me = lax.axis_index(NARROW)
        x, c = self.me // 2, self.me % 2
        self.core_at = x * 2 + 1 - c
        self.chip_at = (1 - x) * 2 + c
        self.far_at = (1 - x) * 2 + 1 - c
        self.core = {NARROW: self.core_at}
        self.chip = {NARROW: self.chip_at}

    def meet(self, barrier):
        greet(barrier, self.core)
        greet(barrier, self.chip)
        return 2


class Gather:
    def __init__(self, net, full, own, sems):
        self.net, self.full, self.own, self.sems = net, full, own, sems

    def place(self, b, who):
        at = (b * 4 + who) * self.own
        return self.full.at[pl.ds(pl.multiple_of(at, self.own), self.own), :]

    def mine(self, b):
        return self.place(b, self.net.me)

    def to_core(self, b):
        return send(self.mine(b), self.mine(b), self.sems, (b, 0), self.net.core)

    def to_chip(self, b):
        return send(self.mine(b), self.mine(b), self.sems, (b, 1), self.net.chip)

    def onward(self, b):
        block = self.place(b, self.net.chip_at)
        return send(block, block, self.sems, (b, 2), self.net.core)

    def start(self, b):
        self.to_chip(b).start()
        self.to_core(b).start()

    def forward(self, b):
        self.to_chip(b).wait_recv()
        self.onward(b).start()

    def finish(self, b):
        self.to_core(b).wait_recv()
        self.onward(b).wait_recv()
        self.to_core(b).wait_send()
        self.to_chip(b).wait_send()
        self.onward(b).wait_send()


class Scatter:
    def __init__(self, net, part, landed, outgoing, arrived, sems):
        self.net, self.part, self.landed = net, part, landed
        self.outgoing, self.arrived, self.sems = outgoing, arrived, sems
        self.own = part.shape[1] // 4

    def rows(self, b, who):
        return self.part.at[b, pl.ds(pl.multiple_of(who * self.own, self.own), self.own), :]

    def core_copy(self, b, k):
        who = self.net.far_at if k == 0 else self.net.core_at
        return send(self.rows(b, who), self.landed.at[b, k], self.sems, (b, k), self.net.core)

    def chip_copy(self, b):
        return send(self.outgoing.at[b], self.arrived.at[b], self.sems, (b, 2), self.net.chip)

    def start(self, b):
        self.core_copy(b, 0).start()
        self.core_copy(b, 1).start()

    def cross(self, b):
        self.core_copy(b, 0).wait_recv()
        mine = self.rows(b, self.net.chip_at)

        def step(s):
            total = mine[s, :] + self.landed[b, 0, s, :]
            self.outgoing[b, s, :] = total.astype(self.outgoing.dtype)

        each_slab(self.own, step)
        self.chip_copy(b).start()

    def ready(self, b):
        self.core_copy(b, 1).wait_recv()
        self.chip_copy(b).wait_recv()

    def total(self, b, s):
        near = self.rows(b, self.net.me)[s, :] + self.landed[b, 1, s, :]
        return near + self.arrived[b, s, :].astype(F32)

    def finish(self, b):
        self.core_copy(b, 0).wait_send()
        self.core_copy(b, 1).wait_send()
        self.chip_copy(b).wait_send()


class Halves:
    def __init__(self, net, full, there, pairs, sems, index):
        me = lax.axis_index(WIDE)
        y, rows = me % 2, full.shape[0] // 2
        blk = full.shape[1] // (2 * pairs)
        span = pl.ds(pl.multiple_of(net.me % 2 * rows, rows), rows)
        self.copies = [
            send(
                full.at[span, pl.ds(pl.multiple_of((2 * k + 1 - y) * blk, blk), blk)],
                there.at[span, pl.ds(k * blk, blk)], sems, (index, k), {WIDE: me + 1 - 2 * y},
            )
            for k in range(pairs)
        ]
        self.onward = send(there.at[span], there.at[span], sems, (index, pairs), net.core)

    def start(self):
        for copy in self.copies:
            copy.start()

    def forward(self):
        for copy in self.copies:
            copy.wait_recv()
        self.onward.start()

    def arrive(self):
        self.onward.wait_recv()

    def leave(self):
        for copy in self.copies:
            copy.wait_send()
        self.onward.wait_send()


def scatter_scratch(images, own, width, hop=LOW):
    return [
        pltpu.VMEM((images, 4 * own, width), F32),
        pltpu.VMEM((images, 2, own, width), F32),
        pltpu.VMEM((images, own, width), hop),
        pltpu.VMEM((images, own, width), hop),
        pltpu.SemaphoreType.DMA((2, images, 3)),
    ]


def params(number, limit):
    return pltpu.CompilerParams(
        collective_id=number, has_side_effects=True, vmem_limit_bytes=limit * 1024 * 1024
    )


class Copies:
    def __init__(self, sems):
        self.sems, self.used, self.open = sems, 0, []

    def start(self, src, dst):
        copy = pltpu.make_async_copy(src, dst, self.sems.at[self.used])
        self.used += 1
        copy.start()
        return copy

    def later(self, src, dst):
        self.open.append(self.start(src, dst))

    def close(self):
        for copy in self.open:
            copy.wait()


def columns_of(width, step, tile=512):
    def body(j, carry):
        step(pl.ds(pl.multiple_of(j * tile, tile), tile))
        return carry

    lax.fori_loop(0, width // tile, body, 0)


def dot(left, right, dims=(((1,), (0,)), ((), ()))):
    return lax.dot_general(left, right, dims, preferred_element_type=F32)


def softmax_parts(q, k):
    scores = dot(q, k, LAST) * (1.0 / math.sqrt(HEAD))
    powers = jnp.exp(scores - jnp.max(scores, axis=-1, keepdims=True))
    return powers / jnp.sum(powers, axis=-1, keepdims=True)


def head_columns(j):
    return pl.ds(pl.multiple_of(j * HEAD, HEAD), HEAD)


def heads_forward(b, images, query, keys, values, out):
    many, some = query.shape[0] // images, keys.shape[0] // images
    asked, told = pl.ds(b * many, many), pl.ds(b * some, some)

    def body(j, carry):
        cols = head_columns(j)
        probs = softmax_parts(query[asked, cols], keys[told, cols])
        out[asked, cols] = dot(probs.astype(LOW), values[told, cols]).astype(LOW)
        return carry

    lax.fori_loop(0, query.shape[1] // HEAD, body, 0)


def heads_back(images, query, keys, values, d_att):
    heads = query.shape[1] // HEAD
    many, some = query.shape[0] // images, keys.shape[0] // images
    scale = 1.0 / math.sqrt(HEAD)

    def body(j, carry):
        b = j // heads
        cols = head_columns(j % heads)
        asked = pl.ds(pl.multiple_of(b * many, many), many)
        told = pl.ds(pl.multiple_of(b * some, some), some)
        q, k, v, d = query[asked, cols], keys[told, cols], values[told, cols], d_att[asked, cols]
        probs = softmax_parts(q, k)
        d_probs = dot(d, v, LAST)
        weighted = jnp.sum(probs * d_probs, axis=-1, keepdims=True)
        d_scores = (probs * (d_probs - weighted)).astype(LOW)
        values[told, cols] = dot(probs.astype(LOW), d, FIRST).astype(LOW)
        keys[told, cols] = (dot(d_scores, q, FIRST) * scale).astype(LOW)
        query[asked, cols] = (dot(d_scores, k) * scale).astype(LOW)
        return carry

    lax.fori_loop(0, images * heads, body, 0)


def gelu(u):
    turn = jnp.tanh(math.sqrt(2.0 / math.pi) * (u + 0.044715 * (u * u * u)))
    return 0.5 * u * (1.0 + turn)


def gelu_slope(u):
    c = math.sqrt(2.0 / math.pi)
    turn = jnp.tanh(c * (u + 0.044715 * (u * u * u)))
    return 0.5 * (1.0 + turn) + 0.5 * u * (1.0 - turn * turn) * (c * (1.0 + 0.134145 * (u * u)))


def flat(array):
    return array.reshape(array.shape[0] * array.shape[1], array.shape[2])


def forward_all(pairs, number, given):
    t = given
    images, own, width = t.tokens.shape
    length, words = 4 * own, t.caption.shape[1]
    inner, ff, states = t.query_self.shape[1], t.up_proj.shape[1], t.caption.shape[2]
    rows, word_rows, word_own = images * length, images * words, words // 4
    chunks, text_chunks = ff // inner, states // inner
    half = width // 2
    vars_in = dict(
        tokens=t.tokens, caption=flat(t.caption), cotangent=t.cotangent, text_proj=t.text_proj,
        query_self=t.query_self, key_self=t.key_self, value_self=t.value_self, out_self=t.out_self,
        query_cross=t.query_cross, key_cross=t.key_cross, value_cross=t.value_cross,
        out_cross=t.out_cross, up_proj=t.up_proj,
    )
    sds = jax.ShapeDtypeStruct
    outs = dict(
        image_self=sds((rows, width), LOW), image_cross=sds((rows, width), LOW),
        image_feed=sds((rows, width), LOW), d_image=sds((rows, width), LOW),
        context=sds((word_rows, width), LOW),
        query_sa=sds((rows, inner), LOW), keys_sa=sds((rows, inner), LOW), values_sa=sds((rows, inner), LOW),
        query_ca=sds((rows, inner), LOW), keys_ca=sds((word_rows, inner), LOW), values_ca=sds((word_rows, inner), LOW),
        attended_sa=sds((rows, inner), LOW), attended_ca=sds((rows, inner), LOW),
        resid_mid=sds((images, own, width), F32), resid_late=sds((images, own, width), F32),
        activ=sds((rows, ff), LOW), pre_act=sds((images, length, ff), F32),
        nb_self=sds((rows, half), LOW), nb_low=sds((rows, half), LOW),
        nb_context=sds((word_rows, half), LOW), nb_first=sds((rows, inner), LOW), nb_caption=sds((word_rows, states), LOW),
        nb_att_sa=sds((rows, inner), LOW), nb_att_ca=sds((rows, inner), LOW),
    )

    def kernel(*refs):
        h = types.SimpleNamespace(**dict(zip(vars_in, refs)))
        refs = refs[len(vars_in):]
        marks, gain_self, gain_cross, gain_feed = refs[:4]
        refs = refs[4:]
        o = types.SimpleNamespace(**dict(zip(outs, refs)))
        refs = refs[len(outs):]
        scatter_refs, text_refs = refs[:5], refs[5:10]
        (full_s, full_c, full_f, full_d, full_x, gsem_s, gsem_c, gsem_f, gsem_d, gsem_x,
         wn, wt, tok, cot, cap, sq, sk, sv, xq, xk, xv, att_s, att_c, mid, late, act,
         fsem, osem, hsem, asem) = refs[10:]
        net = Narrow()
        fetch, store = Copies(fsem), Copies(osem)
        barrier = pltpu.get_barrier_semaphore()
        me = lax.axis_index(WIDE)
        pair = {WIDE: me + 1 - 2 * (me % 2)}
        greet(barrier, pair)
        others = net.meet(barrier) + 1

        def whole(j, ref):
            return fetch.start(ref, wn.at[j])

        def band(j, ref, c):
            return fetch.start(ref.at[pl.ds(c * inner, inner)], wt.at[j])

        need_tok = fetch.start(h.tokens, tok)
        need_cap = fetch.start(h.caption, cap)
        need_proj = [band(c, h.text_proj, c) for c in range(text_chunks)]
        need_cot = fetch.start(h.cotangent, cot)
        need_qkv = [whole(j, ref) for j, ref in enumerate((h.query_self, h.key_self, h.value_self))]
        need_out_self = fetch.start(h.out_self, wt.at[2])
        need_kv = [whole(4, h.key_cross), whole(5, h.value_cross)]
        need_query_cross = whole(3, h.query_cross)
        need_out_cross = fetch.start(h.out_cross, wt.at[3])
        need_up = {3: fetch.start(h.up_proj.at[:, pl.ds(3 * inner, inner)], wn.at[6])}
        gather_s = Gather(net, full_s, own, gsem_s)
        gather_c = Gather(net, full_c, own, gsem_c)
        gather_f = Gather(net, full_f, own, gsem_f)
        gather_d = Gather(net, full_d, own, gsem_d)
        gather_x = Gather(net, full_x, word_own, gsem_x)
        scatter, text = Scatter(net, *scatter_refs), Scatter(net, *text_refs)
        part = scatter.part

        def of(b, n=length):
            return pl.ds(b * n, n)

        need_tok.wait()
        pl.semaphore_wait(barrier, others)
        for b in range(images):
            mine = gather_s.mine(b)

            def step(s, b=b, mine=mine):
                normed, _ = norm_rows(tok[b, s, :].astype(F32))
                mine[s, :] = (normed * gain_self[...].astype(F32)[None]).astype(LOW)

            each_slab(own, step)
            gather_s.start(b)
        need_cap.wait()
        first = [send(cap, o.nb_caption, asem, (images,), pair)]
        first[0].start()
        for need in need_proj:
            need.wait()
        for b in range(images):

            def step(cols, b=b):
                total = None
                for c in range(text_chunks):
                    term = dot(cap[of(b, words), pl.ds(c * inner, inner)], wt[c, :, cols])
                    total = term if total is None else total + term
                text.part[b, :, cols] = total

            columns_of(width, step)
            text.start(b)
        need_cot.wait()
        for b in range(images):
            mine = gather_d.mine(b)

            def step(s, b=b, mine=mine):
                mine[s, :] = (cot[b, s, :].astype(F32) * marks[b, s, :]).astype(LOW)

            each_slab(own, step)

        def project(b, source, weights, targets, n=length):
            for j, target in zip(weights, targets):
                target[of(b, n), :] = dot(source[of(b, n), :], wn[j]).astype(LOW)

        def back_out(b, attended, j):
            def step(cols):
                part[b, :, cols] = dot(attended[of(b), :], wt[j, :, cols])

            columns_of(width, step)
            scatter.start(b)

        gather_s.forward(0)
        text.cross(0)
        text.cross(1)
        gather_d.start(0)
        for b in range(images):
            gather_s.finish(b)
            if b == 0:
                for need in need_qkv:
                    need.wait()
            project(b, full_s, (0, 1, 2), (sq, sk, sv))
            if b + 1 < images:
                gather_s.forward(b + 1)
            heads_forward(b, images, sq, sk, sv, att_s)
            if b == 0:
                need_out_self.wait()
            back_out(b, att_s, 2)
            if b == 0:
                scatter.cross(b)
        store.later(full_s, o.image_self)
        for ref, out in ((sq, o.query_sa), (sk, o.keys_sa), (sv, o.values_sa), (att_s, o.attended_sa)):
            store.later(ref, out)
        for c in range(3):
            need_up[c] = fetch.start(h.up_proj.at[:, pl.ds(c * inner, inner)], wn.at[c])
        for b in range(images):
            text.ready(b)
            mine = gather_x.mine(b)

            def step(s, b=b, mine=mine):
                mine[s, :] = text.total(b, s).astype(LOW)

            each_slab(word_own, step)
        scatter.cross(1)
        for b in range(images):
            gather_x.start(b)
        halves_self = Halves(net, full_s, o.nb_self, pairs, hsem, 0)
        halves_self.start()
        first.append(send(att_s, o.nb_att_sa, asem, (images + 1,), pair))
        first[-1].start()

        def rows_out(b, source, target, gain, gather):
            scatter.ready(b)
            mine = gather.mine(b)

            def step(s):
                kept = source[b, s, :].astype(F32) + scatter.total(b, s)
                target[b, s, :] = kept
                normed, _ = norm_rows(kept)
                mine[s, :] = (normed * gain[...].astype(F32)[None]).astype(LOW)

            each_slab(own, step)
            gather.start(b)

        rows_out(0, tok, mid, gain_cross, gather_c)
        gather_d.start(1)
        for b in range(images):
            gather_x.forward(b)
        rows_out(1, tok, mid, gain_cross, gather_c)
        store.later(mid, o.resid_mid)
        for need in need_kv:
            need.wait()
        for b in range(images):
            gather_x.finish(b)
            project(b, full_x, (4, 5), (xk, xv), words)
            text.finish(b)
        halves_context = Halves(net, full_x, o.nb_context, pairs, hsem, 1)
        halves_context.start()
        store.later(full_x, o.context)
        store.later(xk, o.keys_ca)
        store.later(xv, o.values_ca)
        need_query_cross.wait()
        gather_c.forward(0)
        for b in range(images):
            gather_c.finish(b)
            project(b, full_c, (3,), (xq,))
            if b + 1 < images:
                gather_c.forward(b + 1)
            heads_forward(b, images, xq, xk, xv, att_c)
            scatter.finish(b)
            if b == 0:
                need_out_cross.wait()
            back_out(b, att_c, 3)
            if b == 0:
                for j in range(images):
                    gather_d.forward(j)
                scatter.cross(b)
                for j in range(images):
                    gather_d.finish(j)
                halves_low = Halves(net, full_d, o.nb_low, pairs, hsem, 2)
                halves_low.start()
                store.later(full_d, o.d_image)
        first.append(send(att_c, o.nb_att_ca, asem, (images + 2,), pair))
        first[-1].start()
        store.later(full_c, o.image_cross)
        store.later(xq, o.query_ca)
        store.later(att_c, o.attended_ca)
        scatter.cross(1)
        halves_self.forward()
        halves_context.forward()
        rows_out(0, mid, late, gain_feed, gather_f)
        rows_out(1, mid, late, gain_feed, gather_f)
        store.later(late, o.resid_late)
        halves_low.forward()
        first += [
            send(act.at[of(b), pl.ds(0, inner)], o.nb_first.at[of(b)], asem, (b,), pair) for b in range(images)
        ]
        gather_f.forward(0)
        for b in range(images):
            gather_f.finish(b)
            scatter.finish(b)
            for c in range(chunks):
                if b == 0:
                    need_up[c].wait()
                cols = pl.ds(c * inner, inner)
                part[b, :, cols] = dot(full_f[of(b), :], wn[6 if c == 3 else c])
                if b == 0 and c == 1:
                    gather_f.forward(1)

                def step(s, b=b, cols=cols):
                    act[pl.ds(pl.multiple_of(b * length + s.start, 16), 16), cols] = gelu(part[b, s, cols]).astype(LOW)

                each_slab(length, step)
                if c == 0:
                    first[3 + b].start()
        store.later(act, o.activ)
        store.later(part, o.pre_act)
        store.later(full_f, o.image_feed)
        for halves in (halves_self, halves_context, halves_low):
            halves.arrive()
            halves.leave()
        for copy in first:
            copy.wait()
        store.close()

    V, DS = pltpu.VMEM, pltpu.SemaphoreType.DMA
    gsem = DS((2, images, 3))
    scratch = scatter_scratch(images, own, width) + scatter_scratch(images, word_own, width, F32)
    scratch += [V((rows, width), LOW)] * 4 + [V((word_rows, width), LOW)] + [gsem] * 5
    scratch += [
        V((7, width, inner), LOW), V((4, inner, width), LOW),
        V((images, own, width), LOW), V((images, own, width), LOW), V((word_rows, states), LOW),
        V((rows, inner), LOW), V((rows, inner), LOW), V((rows, inner), LOW),
        V((rows, inner), LOW), V((word_rows, inner), LOW), V((word_rows, inner), LOW),
        V((rows, inner), LOW), V((rows, inner), LOW),
        V((images, own, width), F32), V((images, own, width), F32), V((rows, ff), LOW),
        DS((40,)), DS((40,)), DS((2, 3, pairs + 1)), DS((2, images + 3)),
    ]
    result = pl.pallas_call(
        kernel,
        out_shape=list(outs.values()),
        in_specs=[HB] * len(vars_in) + [VM] * 4,
        out_specs=[HB] * len(outs),
        scratch_shapes=scratch,
        compiler_params=params(number, 62),
        name="forward_all",
    )(*vars_in.values(), t.marks, *t.gains)
    return types.SimpleNamespace(**dict(zip(outs, result)))


def backward_all(pairs, number, given, kept):
    t = given
    images, own, width = t.tokens.shape
    length, words = 4 * own, t.caption.shape[1]
    inner, ff, states = t.query_self.shape[1], t.up_proj.shape[1], t.caption.shape[2]
    rows, word_rows, word_own = images * length, images * words, words // 4
    chunks, text_chunks = ff // inner, states // inner
    half, blk = width // 2, width // (2 * pairs)
    count = 2 * chunks + text_chunks + 8
    vars_in = dict(
        vars(kept),
        tokens=t.tokens, caption=flat(t.caption), cotangent=t.cotangent, text_proj=t.text_proj,
        query_self=t.query_self, key_self=t.key_self, value_self=t.value_self, out_self=t.out_self,
        query_cross=t.query_cross, key_cross=t.key_cross, value_cross=t.value_cross,
        out_cross=t.out_cross, up_proj=t.up_proj, down_proj=t.down_proj,
    )

    def kernel(*refs):
        h = types.SimpleNamespace(**dict(zip(vars_in, refs)))
        refs = refs[len(vars_in):]
        marks, gain_self, gain_cross, gain_feed = refs[:4]
        grads_out, words_out, tokens_out, layer_out, gain_out, nb_cols, nb_feed, nb_cross, nb_late, nb_mid, nb_words = refs[4:15]
        refs = refs[15:]
        scatter_refs = refs[:5]
        (full_c, full_s, full_x, gsem_c, gsem_s, gsem_x, text_sem,
         big, d_att, wa, wb, xq, xk, xv, sq, sk, sv, cot, late, mid, tok, low_rows, word_grad,
         fsem, osem, nbsem, hsem, gacc, gland, gsems) = refs[5:35]
        net = Narrow()
        units = []

        def unit(rows_ref, nb_rows, columns, size, halves=None, early=None):
            i = len(units)
            there = nb_cols.at[i, pl.ds(0, size)] if early is None else early
            units.append(types.SimpleNamespace(
                rows=rows_ref, nb_rows=nb_rows, columns=columns, count=size, halves=halves,
                nb_columns=there, sems=nbsem, out=grads_out.at[i], early=early is not None,
            ))

        def chunk(ref, c):
            return ref.at[:, pl.ds(c * inner, inner)]

        halves_feed = Halves(net, h.image_feed, nb_feed, pairs, hsem, 0)
        halves_cross = Halves(net, h.image_cross, nb_cross, pairs, hsem, 1)
        halves_late = Halves(net, full_c, nb_late, pairs, hsem, 2)
        halves_mid = Halves(net, full_s, nb_mid, pairs, hsem, 3)
        halves_words = Halves(net, full_x, nb_words, pairs, hsem, 4)
        for c in range(chunks):
            unit(h.d_image, h.nb_low, chunk(h.activ, c), rows, None, h.nb_first if c == 0 else None)
        for c in range(chunks):
            unit(h.image_feed, nb_feed, chunk(big, c), rows, halves_feed)
        unit(full_c, nb_late, h.attended_ca, rows, halves_late, h.nb_att_ca)
        unit(h.context, h.nb_context, xk, word_rows)
        unit(h.context, h.nb_context, xv, word_rows)
        unit(h.image_cross, nb_cross, xq, rows, halves_cross)
        for c in range(text_chunks):
            unit(full_x, nb_words, chunk(h.caption, c), word_rows, halves_words, chunk(h.nb_caption, c))
        unit(full_s, nb_mid, h.attended_sa, rows, halves_mid, h.nb_att_sa)
        for column in (sq, sk, sv):
            unit(h.image_self, h.nb_self, column, rows)
        wide = Wide(pairs, units, refs[35:])
        fetch, store = Copies(fsem), Copies(osem)

        def of(b, n=length):
            return pl.ds(b * n, n)

        barrier = pltpu.get_barrier_semaphore()
        far = {WIDE: (wide.z + 2) % pairs * 2 + wide.y}
        near = {WIDE: (wide.z + 1 - 2 * (wide.z % 2)) * 2 + wide.y}
        greet(barrier, far)
        others = wide.meet(barrier) + net.meet(barrier) + 1

        def up_chunk(c):
            return fetch.start(chunk(h.up_proj, c), wa.at[c % 2])

        wide.load(0)
        need_image = fetch.start(h.d_image, full_s)

        def down_chunk(c):
            return fetch.start(h.down_proj.at[pl.ds(c * inner, inner)], wb.at[c % 2])

        need_down = {c: down_chunk(c) for c in range(2)}
        need_pre = fetch.start(h.pre_act, scatter_refs[0])
        need_up = {c: up_chunk(c) for c in range(2)}
        need_cot = fetch.start(h.cotangent, cot)
        need_late = fetch.start(h.resid_late, late)
        need_ca = [fetch.start(a, b) for a, b in ((h.query_ca, xq), (h.keys_ca, xk), (h.values_ca, xv))]
        need_mid = fetch.start(h.resid_mid, mid)
        need_sa = [fetch.start(a, b) for a, b in ((h.query_sa, sq), (h.keys_sa, sk), (h.values_sa, sv))]
        need_tok = fetch.start(h.tokens, tok)
        pl.semaphore_wait(barrier, others)
        wide.ask(1)
        wide.ask(2)
        wide.multiply(0, True)
        scatter = Scatter(net, *scatter_refs)
        part = scatter.part
        gather_c, gather_s = Gather(net, full_c, own, gsem_c), Gather(net, full_s, own, gsem_s)
        gather_x = Gather(net, full_x, word_own, gsem_x)

        need_image.wait()
        need_pre.wait()
        for c in range(chunks):
            need_down[c].wait()
            cols = pl.ds(c * inner, inner)
            for b in range(images):
                slope = dot(full_s[of(b), :], wb[c % 2], LAST)
                big[of(b), cols] = (gelu_slope(part[b, :, cols]) * slope).astype(LOW)
            if c + 2 < chunks:
                need_down[c + 2] = down_chunk(c + 2)
            if c == 1:
                wide.ask(3)
                halves_feed.start()
        need_out = fetch.start(h.out_cross, wb.at[0])
        need_out_self = fetch.start(h.out_self, wb.at[1])
        wide.multiply(1)
        wide.ask(4)
        wide.move(1)
        for c in range(chunks):
            need_up[c].wait()
            for b in range(images):

                def step(cols, b=b, c=c):
                    term = dot(big[of(b), pl.ds(c * inner, inner)], wa[c % 2, cols, :], LAST)
                    part[b, :, cols] = term if c == 0 else part[b, :, cols] + term

                columns_of(width, step)
                if c == chunks - 1:
                    scatter.start(b)
            if c + 2 < chunks:
                need_up[c + 2] = up_chunk(c + 2)
        need_query = fetch.start(h.query_cross, wa.at[0])
        need_key = fetch.start(h.key_cross, wa.at[1])
        gacc[...] = jnp.zeros_like(gacc)

        def back_rows(b, above, mask, source, gain, slot, keep, mine):
            scatter.ready(b)

            def step(s):
                d_hidden = scatter.total(b, s)
                normed, inv_std = norm_rows(source[b, s, :].astype(F32))
                gacc[slot : slot + 1, :] += jnp.sum(d_hidden * normed, axis=0, keepdims=True)
                top = above[b, s, :].astype(F32)
                if mask is not None:
                    top = top * mask[b, s, :]
                scaled = d_hidden * gain[...].astype(F32)[None]
                inside = scaled - jnp.mean(scaled, axis=-1, keepdims=True)
                inside = inside - normed * jnp.mean(scaled * normed, axis=-1, keepdims=True)
                d_rows = top + inv_std * inside
                if keep is not None:
                    keep[b, s, :] = d_rows
                mine[s, :] = d_rows.astype(LOW)

            each_slab(own, step)

        def multiply(b, target, lefts, rights, n=length):
            def step(cols):
                total = None
                for left, j in zip(lefts, rights):
                    term = dot(left[of(b, n), :], wa[j, cols, :], LAST)
                    total = term if total is None else total + term
                target[b, :, cols] = total

            columns_of(width, step)

        def out_back(b, full, j):
            d_att[of(b), :] = dot(full[of(b), :], wb[j], LAST).astype(LOW)

        wide.multiply(2)
        wide.ask(5)
        wide.move(2)
        for b in range(images):
            scatter.cross(b)
        wide.multiply(3)
        wide.ask(6)
        need_cot.wait()
        need_late.wait()
        for b in range(images):
            back_rows(b, cot, marks, late, gain_feed, 2, late, gather_c.mine(b))
            gather_c.start(b)
        wide.move(3)
        halves_feed.forward()
        for b in range(images):
            gather_c.forward(b)
        wide.multiply(4)
        wide.ask(7)
        need_out.wait()
        for b in range(images):
            scatter.finish(b)
            gather_c.finish(b)
            out_back(b, full_c, 0)
        halves_late.start()
        need_text = fetch.start(h.text_proj.at[pl.ds(0, inner)], wb.at[0])
        wide.move(4)
        wide.multiply(5)
        for need in need_ca:
            need.wait()
        heads_back(images, xq, xk, xv, d_att)
        wide.ask(9)
        wide.ask(10)
        halves_cross.start()
        need_query.wait()
        for b in range(images):
            multiply(b, part, [xq], [0])
            scatter.start(b)
        need_value = fetch.start(h.value_cross, wa.at[0])
        wide.multiply(6)
        wide.ask(11)
        for b in range(images):
            scatter.cross(b)
        wide.move(5)
        need_mid.wait()
        for b in range(images):
            back_rows(b, late, None, mid, gain_cross, 1, mid, gather_s.mine(b))
            gather_s.start(b)
        need_again = fetch.start(h.resid_late, late)
        wide.multiply(7)
        halves_late.forward()
        wide.move(6)
        for b in range(images):
            gather_s.forward(b)
        wide.multiply(8)
        for b in range(images):
            scatter.finish(b)
            gather_s.finish(b)
        halves_mid.start()
        text = Scatter(
            net, part.at[:, pl.ds(0, words)], scatter.landed.at[:, :, pl.ds(0, word_own)],
            scatter.outgoing.at[:, pl.ds(0, word_own)], scatter.arrived.at[:, pl.ds(0, word_own)], text_sem,
        )
        need_key.wait()
        need_value.wait()
        for b in range(images):
            multiply(b, text.part, [xk, xv], [1, 0], words)
            text.start(b)
        need_qkv = [fetch.start(h.query_self, wa.at[0]), fetch.start(h.key_self, wa.at[1])]
        need_out_self.wait()
        for b in range(images):
            out_back(b, full_s, 1)
        need_second = fetch.start(h.text_proj.at[pl.ds(inner, inner)], wb.at[1])
        wide.move(7)
        for b in range(images):
            text.cross(b)
        wide.multiply(9)
        for need in need_sa:
            need.wait()
        heads_back(images, sq, sk, sv, d_att)
        for b in range(images):
            text.ready(b)
            mine = gather_x.mine(b)

            def step(s, b=b, mine=mine):
                mine[s, :] = text.total(b, s).astype(LOW)

            each_slab(word_own, step)
            gather_x.start(b)
        wide.multiply(10)
        halves_cross.forward()
        wide.move(8)
        for b in range(images):
            gather_x.forward(b)
        for b in range(images):
            text.finish(b)
            gather_x.finish(b)
        halves_words.start()
        for c, need in enumerate((need_text, need_second)):
            need.wait()
            word_grad[:, pl.ds(c * inner, inner)] = dot(full_x[...], wb[c], LAST).astype(LOW)
        store.later(word_grad, words_out)
        need_down = {c: down_chunk(c) for c in range(2)}
        for need in need_qkv:
            need.wait()
        for b in range(images):
            multiply(b, part, [sq, sk], [0, 1])
        need_value = fetch.start(h.value_self, wa.at[0])
        wide.multiply(11)
        for c in range(chunks):
            wide.leave(chunks + c)
        need_act = fetch.start(h.activ, big)
        wide.move(9)
        need_value.wait()
        for b in range(images):

            def step(cols, b=b):
                part[b, :, cols] += dot(sv[of(b), :], wa[0, cols, :], LAST)

            columns_of(width, step)
            scatter.start(b)
        halves_words.forward()
        wide.multiply(12)
        for b in range(images):
            scatter.cross(b)
        wide.move(10)
        need_tok.wait()
        for b in range(images):
            back_rows(b, mid, None, tok, gain_self, 0, None, low_rows.at[b])
        store.later(low_rows, tokens_out)
        for b in range(images):
            scatter.finish(b)
        wide.ask(15)
        halves_mid.forward()
        wide.multiply(13)
        wide.move(11)
        trips = [
            send(gacc, gland.at[j], gsems, (j,), peer)
            for j, peer in enumerate((net.core, net.chip, wide.peer, near, far))
        ]

        def trip(j):
            if j > 0:
                trips[j - 1].wait()
                gacc[...] = gacc[...] + gland[j - 1]
            if j < len(trips):
                trips[j].start()

        def forward_chunk(c):
            need_down[c].wait()
            for b in range(images):

                def step(cols, b=b):
                    term = dot(big[of(b), pl.ds(c * inner, inner)], wb[c % 2, :, cols])
                    part[b, :, cols] = term if c == 0 else part[b, :, cols] + term

                columns_of(width, step)
            if c + 2 < chunks:
                need_down[c + 2] = down_chunk(c + 2)

        trip(0)
        wide.multiply(14)
        wide.ask(16)
        trip(1)
        wide.move(12)
        trip(2)
        wide.multiply(15)
        wide.ask(17)
        trip(3)
        wide.move(13)
        wide.multiply(16)
        need_act.wait()
        forward_chunk(0)
        wide.move(14)
        forward_chunk(1)
        wide.multiply(17)
        wide.move(15)
        for c in range(2, chunks):
            forward_chunk(c)
        for b in range(images):
            scatter.start(b)
        wide.move(16)
        for b in range(images):
            scatter.cross(b)
        trip(4)
        wide.move(17)
        need_again.wait()
        for b in range(images):
            scatter.ready(b)

            def step(s, b=b):
                tok[b, s, :] = (late[b, s, :] + scatter.total(b, s)).astype(LOW)

            each_slab(own, step)
            scatter.finish(b)
        store.later(tok, layer_out)
        for k in range(18, count + pairs - 1):
            wide.move(k)
        trip(5)
        store.later(gacc, gain_out)
        wide.drain()
        for halves in (halves_feed, halves_cross, halves_late, halves_mid, halves_words):
            halves.leave()
        store.close()

    V, DS = pltpu.VMEM, pltpu.SemaphoreType.DMA
    gsem = DS((2, images, 3))
    scratch = scatter_scratch(images, own, width)
    scratch += [V((rows, width), LOW), V((rows, width), LOW), V((word_rows, width), LOW)] + [gsem] * 4
    scratch += [
        V((rows, ff), LOW), V((rows, inner), LOW), V((2, width, inner), LOW), V((2, inner, width), LOW),
        V((rows, inner), LOW), V((word_rows, inner), LOW), V((word_rows, inner), LOW),
        V((rows, inner), LOW), V((rows, inner), LOW), V((rows, inner), LOW),
        V((images, own, width), LOW), V((images, own, width), F32), V((images, own, width), F32),
        V((images, own, width), LOW), V((images, own, width), LOW), V((word_rows, states), LOW),
        DS((48,)), DS((8,)), DS((2, count)), DS((2, 5, pairs + 1)), V((8, width), F32), V((5, 8, width), F32), DS((2, 5)),
    ]
    scratch += [
        V((HELD, pairs, blk, inner), LOW),
        V((RING, pairs - 1, blk, inner), LOW), V((RING, pairs - 1, blk, inner), LOW), V((2, blk, inner), LOW),
        V((2, 2, pairs, rows, blk), LOW), V((2, 2, rows, inner), LOW),
        DS((2, count, pairs - 1)), DS((2, count, pairs - 1)),
        DS((2, 2, pairs)), DS((2, 2)), DS((2,)),
        pltpu.SemaphoreType.REGULAR, pltpu.SemaphoreType.REGULAR,
    ]
    sds = jax.ShapeDtypeStruct
    result = pl.pallas_call(
        kernel,
        out_shape=[
            sds((count, blk, inner), LOW), sds((word_rows, states), LOW), sds((images, own, width), LOW),
            sds((images, own, width), LOW), sds((8, width), F32), sds((count, rows, inner), LOW), sds((rows, half), LOW),
            sds((rows, half), LOW), sds((rows, half), LOW), sds((rows, half), LOW), sds((word_rows, half), LOW),
        ],
        in_specs=[HB] * len(vars_in) + [VM] * 4,
        out_specs=[HB] * 11,
        scratch_shapes=scratch,
        compiler_params=params(number, 62),
        name="backward_all",
    )(*vars_in.values(), t.marks, *t.gains)
    return result[:5]


def spread(blocks, places, shapes, whole, gains):
    count, blk, inner = blocks.shape
    more = len(whole)

    def kernel(*refs):
        blocks_ref, whole_in, gains_ref, refs = refs[0], refs[1 : 1 + more], refs[1 + more], refs[2 + more :]
        outs, whole_out, refs = refs[: len(shapes)], refs[len(shapes) : len(shapes) + more], refs[len(shapes) + more :]
        gains_out, refs = refs[:3], refs[3:]
        for j, row in enumerate(gains_out):
            row[...] = gains_ref[j, :]
        held, flat_stage, turned_stage, isem, osem, wsem, *kept = refs
        ins = [pltpu.make_async_copy(blocks_ref.at[i], held.at[i], isem.at[i]) for i in range(count)]
        for copy in ins:
            copy.start()
        done, plain, turns = [], 0, 0
        came = [pltpu.make_async_copy(whole_in[j], kept[j], wsem.at[0, j]) for j in range(more)]
        for copy in came:
            copy.start()
        for i, (which, row, col, turned) in enumerate(places):
            ins[i].wait()
            if turned:
                stage = turned_stage.at[turns]
                turns += 1
                for j in range(0, inner, 128):
                    stage[pl.ds(j, 128), :] = held[i, :, pl.ds(j, 128)].astype(F32).T
                place = outs[which].at[pl.ds(row, inner), pl.ds(col, blk)]
            else:
                stage = flat_stage.at[plain]
                plain += 1
                stage[...] = held[i].astype(F32)
                place = outs[which].at[pl.ds(row, blk), pl.ds(col, inner)]
            done.append(pltpu.make_async_copy(stage, place, osem.at[i]))
            done[-1].start()
        for j in range(more):
            came[j].wait()
            done.append(pltpu.make_async_copy(kept[j], whole_out[j], wsem.at[1, j]))
            done[-1].start()
        for copy in done:
            copy.wait()

    turns = sum(1 for place in places if place[3])
    V, DS = pltpu.VMEM, pltpu.SemaphoreType.DMA
    return pl.pallas_call(
        kernel,
        out_shape=[jax.ShapeDtypeStruct(shape, F32) for shape in shapes]
        + [jax.ShapeDtypeStruct(array.shape, array.dtype) for array in whole]
        + [jax.ShapeDtypeStruct(gains.shape[1:], F32)] * 3,
        in_specs=[HB] * (1 + more) + [VM],
        out_specs=[HB] * (len(shapes) + more) + [VM] * 3,
        scratch_shapes=[
            V((count, blk, inner), LOW), V((count - turns, blk, inner), F32), V((turns, inner, blk), F32),
            DS((count,)), DS((count,)), DS((2, more)),
        ] + [V(array.shape, array.dtype) for array in whole],
        compiler_params=pltpu.CompilerParams(vmem_limit_bytes=62 * 1024 * 1024),
        name="spread",
    )(blocks, *whole, gains)


def by_kernels(
    tokens, caption, token_mask, cotangent, gain_self, gain_cross, gain_feed, text_proj,
    query_self, key_self, value_self, out_self, query_cross, key_cross, value_cross, out_cross, up_proj, down_proj,
):
    given = types.SimpleNamespace(
        tokens=tokens, caption=caption, cotangent=cotangent, text_proj=text_proj,
        query_self=query_self, key_self=key_self, value_self=value_self, out_self=out_self,
        query_cross=query_cross, key_cross=key_cross, value_cross=value_cross, out_cross=out_cross,
        up_proj=up_proj, down_proj=down_proj, marks=token_mask[:, :, None].astype(F32),
        gains=[gain_self, gain_cross, gain_feed],
    )
    pairs = lax.axis_size(WIDE) // 2
    kept = forward_all(pairs, 1, given)
    grads, d_words, d_tokens, layer_out, gains = backward_all(pairs, 2, given, kept)
    inner = query_self.shape[1]
    blk = query_self.shape[0] // (2 * pairs)
    ff, text = up_proj.shape[1] // inner, caption.shape[2] // inner
    places = [(10, c * inner, 0, True) for c in range(ff)]
    places += [(9, 0, c * inner, False) for c in range(ff)]
    places += [(8, 0, 0, True), (6, 0, 0, False), (7, 0, 0, False), (5, 0, 0, False)]
    places += [(0, c * inner, 0, True) for c in range(text)]
    places += [(4, 0, 0, True), (1, 0, 0, False), (2, 0, 0, False), (3, 0, 0, False)]
    shapes = [(text * inner, blk)] + [(blk, inner)] * 3 + [(inner, blk)] + [(blk, inner)] * 3 + [(inner, blk)]
    shapes += [(blk, ff * inner), (ff * inner, blk)]
    out = spread(grads, places, shapes, [layer_out, d_tokens, d_words], gains)
    sums, (layer_out, d_tokens, d_words, *gains) = out[: len(shapes)], out[len(shapes) :]
    return (layer_out, d_tokens, d_words.reshape(caption.shape), *gains, *sums)


def local(
    tokens,
    caption,
    token_mask,
    cotangent,
    gain_self,
    gain_cross,
    gain_feed,
    text_proj,
    query_self,
    key_self,
    value_self,
    out_self,
    query_cross,
    key_cross,
    value_cross,
    out_cross,
    up_proj,
    down_proj,
):
    given = (tokens, caption, token_mask, cotangent, gain_self, gain_cross, gain_feed, text_proj, query_self, key_self, value_self, out_self, query_cross, key_cross, value_cross, out_cross, up_proj, down_proj)
    if lax.axis_size(WIDE) != 8 or lax.axis_size(NARROW) != 4:
        return by_collectives(*given)
    return by_kernels(*given)


def solution(mesh):
    in_specs = (
        P(WIDE, NARROW, None),
        P(WIDE, None, NARROW),
        P(WIDE, NARROW),
        P(WIDE, NARROW, None),
        P(),
        P(),
        P(),
        P(NARROW, None),
        P(None, NARROW),
        P(None, NARROW),
        P(None, NARROW),
        P(NARROW, None),
        P(None, NARROW),
        P(None, NARROW),
        P(None, NARROW),
        P(NARROW, None),
        P(None, NARROW),
        P(NARROW, None),
    )
    out_specs = (
        P(WIDE, NARROW, None),
        P(WIDE, NARROW, None),
        P(WIDE, None, NARROW),
        P(),
        P(),
        P(),
        P(NARROW, WIDE),
        P(WIDE, NARROW),
        P(WIDE, NARROW),
        P(WIDE, NARROW),
        P(NARROW, WIDE),
        P(WIDE, NARROW),
        P(WIDE, NARROW),
        P(WIDE, NARROW),
        P(NARROW, WIDE),
        P(WIDE, NARROW),
        P(NARROW, WIDE),
    )
    return jax.shard_map(local, mesh=mesh, in_specs=in_specs, out_specs=out_specs, check_vma=False)
```

```python
import math
import types

import jax
import jax.numpy as jnp
from jax import lax
from jax.experimental import pallas as pl
from jax.experimental.pallas import tpu as pltpu
from jax.sharding import PartitionSpec as P

HEAD = 128
MESH = pl.DeviceIdType.MESH
WIDE, NARROW = "wide", "narrow"
LOW, F32 = jnp.bfloat16, jnp.float32
LAST, FIRST = (((1,), (1,)), ((), ())), (((0,), (0,)), ((), ()))

def normalize(rows):
    centre = jnp.mean(rows, axis=-1, keepdims=True)
    centred = rows - centre
    variance = jnp.mean(centred * centred, axis=-1, keepdims=True)
    inv_std = lax.rsqrt(variance + 1e-05)
    return (centred * inv_std, inv_std)


def norm_back(d_normed, normed, inv_std):
    inner = d_normed - jnp.mean(d_normed, axis=-1, keepdims=True)
    inner = inner - normed * jnp.mean(d_normed * normed, axis=-1, keepdims=True)
    return inv_std * inner


def times_weight(left, right):
    return jnp.dot(left, right, preferred_element_type=jnp.float32)


def split_heads(matrix):
    return matrix.reshape(matrix.shape[0], matrix.shape[1], matrix.shape[2] // HEAD, HEAD)


def join_heads(heads):
    return heads.reshape(heads.shape[0], heads.shape[1], heads.shape[2] * HEAD)


def head_scores(query, keys):
    scores = jnp.einsum(
        "bqhe,bkhe->bhqk", split_heads(query), split_heads(keys), preferred_element_type=jnp.float32
    )
    return scores * (1.0 / math.sqrt(HEAD))


def attend(query, keys, values):
    scores = head_scores(query, keys)
    peak = jnp.max(scores, axis=-1, keepdims=True)
    powers = jnp.exp(scores - peak)
    summed = jnp.sum(powers, axis=-1, keepdims=True)
    low_probs = (powers / summed).astype(jnp.bfloat16)
    attended = jnp.einsum(
        "bhqk,bkhe->bqhe", low_probs, split_heads(values), preferred_element_type=jnp.float32
    )
    return join_heads(attended).astype(jnp.bfloat16), peak + jnp.log(summed)


def attend_back(query, keys, values, log_total, d_attended):
    probs = jnp.exp(head_scores(query, keys) - log_total)
    low_probs = probs.astype(jnp.bfloat16)
    d_heads = split_heads(d_attended)
    d_probs = jnp.einsum(
        "bqhe,bkhe->bhqk", d_heads, split_heads(values), preferred_element_type=jnp.float32
    )
    d_values = jnp.einsum("bhqk,bqhe->bkhe", low_probs, d_heads, preferred_element_type=jnp.float32)
    weighted = jnp.sum(probs * d_probs, axis=-1, keepdims=True)
    d_scores = (probs * (d_probs - weighted)).astype(jnp.bfloat16)
    scale = 1.0 / math.sqrt(HEAD)
    d_query = (
        jnp.einsum("bhqk,bkhe->bqhe", d_scores, split_heads(keys), preferred_element_type=jnp.float32)
        * scale
    )
    d_keys = (
        jnp.einsum("bhqk,bqhe->bkhe", d_scores, split_heads(query), preferred_element_type=jnp.float32)
        * scale
    )
    return tuple(join_heads(d).astype(jnp.bfloat16) for d in (d_query, d_keys, d_values))


def contract(left, right):
    return lax.dot_general(
        left, right, (((0, 1), (0, 1)), ((), ())), preferred_element_type=jnp.float32
    ).astype(jnp.bfloat16)


def against(left, right):
    return lax.dot_general(
        left, right, (((2,), (1,)), ((), ())), preferred_element_type=jnp.float32
    )


def group_rows(piece):
    return lax.all_gather(piece, NARROW, axis=1, tiled=True)


def own_rows(partial):
    return lax.psum_scatter(partial, NARROW, scatter_dimension=1, tiled=True)


def feed_back(partial):
    return own_rows(partial.astype(jnp.bfloat16)).astype(jnp.float32)


def text_total(partial):
    return lax.psum(partial, NARROW)


def by_collectives(
    tokens,
    caption,
    token_mask,
    cotangent,
    gain_self,
    gain_cross,
    gain_feed,
    text_proj,
    query_self,
    key_self,
    value_self,
    out_self,
    query_cross,
    key_cross,
    value_cross,
    out_cross,
    up_proj,
    down_proj,
):
    gain_one = gain_self.astype(jnp.float32)
    gain_two = gain_cross.astype(jnp.float32)
    gain_three = gain_feed.astype(jnp.float32)
    low = jnp.bfloat16

    resid_in = tokens.astype(jnp.float32)
    normed_self, inv_self = normalize(resid_in)
    image_self = group_rows((normed_self * gain_one).astype(low))
    query_sa = times_weight(image_self, query_self).astype(low)
    keys_sa = times_weight(image_self, key_self).astype(low)
    values_sa = times_weight(image_self, value_self).astype(low)
    attended_sa, total_sa = attend(query_sa, keys_sa, values_sa)
    resid_mid = resid_in + own_rows(times_weight(attended_sa, out_self))
    context = text_total(times_weight(caption, text_proj)).astype(low)
    keys_ca = times_weight(context, key_cross).astype(low)
    values_ca = times_weight(context, value_cross).astype(low)
    normed_cross, inv_cross = normalize(resid_mid)
    image_cross = group_rows((normed_cross * gain_two).astype(low))
    query_ca = times_weight(image_cross, query_cross).astype(low)
    attended_ca, total_ca = attend(query_ca, keys_ca, values_ca)
    resid_late = resid_mid + own_rows(times_weight(attended_ca, out_cross))
    normed_feed, inv_feed = normalize(resid_late)
    d_result = cotangent.astype(jnp.float32) * token_mask[:, :, None].astype(jnp.float32)
    d_image = group_rows(d_result.astype(low))
    image_feed = group_rows((normed_feed * gain_three).astype(low))
    pre_act = times_weight(image_feed, up_proj)
    gelu_out, gelu_pull = jax.vjp(jax.nn.gelu, pre_act)
    activ = gelu_out.astype(low)
    resid_out = resid_late + feed_back(times_weight(activ, down_proj))
    d_pre = gelu_pull(against(d_image, down_proj))[0].astype(low)
    part_down = contract(activ, d_image)
    part_up = contract(image_feed, d_pre)
    d_hidden_feed = feed_back(against(d_pre, up_proj))
    part_gain_feed = jnp.sum(d_hidden_feed * normed_feed, axis=(0, 1))
    d_late = d_result + norm_back(d_hidden_feed * gain_three, normed_feed, inv_feed)
    d_image_cross = group_rows(d_late.astype(low))
    part_out_cross = contract(attended_ca, d_image_cross)
    d_attended_ca = against(d_image_cross, out_cross).astype(low)
    d_query_ca, d_keys_ca, d_values_ca = attend_back(
        query_ca, keys_ca, values_ca, total_ca, d_attended_ca
    )
    part_query_cross = contract(image_cross, d_query_ca)
    part_key_cross = contract(context, d_keys_ca)
    part_value_cross = contract(context, d_values_ca)
    d_hidden_cross = own_rows(against(d_query_ca, query_cross))
    d_context = text_total(against(d_keys_ca, key_cross) + against(d_values_ca, value_cross))
    d_context = d_context.astype(low)
    part_text = contract(caption, d_context)
    d_words = against(d_context, text_proj).astype(low)
    part_gain_cross = jnp.sum(d_hidden_cross * normed_cross, axis=(0, 1))
    d_mid = d_late + norm_back(d_hidden_cross * gain_two, normed_cross, inv_cross)
    d_image_self = group_rows(d_mid.astype(low))
    part_out_self = contract(attended_sa, d_image_self)
    d_attended_sa = against(d_image_self, out_self).astype(low)
    d_query_sa, d_keys_sa, d_values_sa = attend_back(
        query_sa, keys_sa, values_sa, total_sa, d_attended_sa
    )
    part_query_self = contract(image_self, d_query_sa)
    part_key_self = contract(image_self, d_keys_sa)
    part_value_self = contract(image_self, d_values_sa)
    d_hidden_self = own_rows(
        against(d_query_sa, query_self)
        + against(d_keys_sa, key_self)
        + against(d_values_sa, value_self)
    )
    part_gain_self = jnp.sum(d_hidden_self * normed_self, axis=(0, 1))
    d_input = d_mid + norm_back(d_hidden_self * gain_one, normed_self, inv_self)
    parts = (
        part_text,
        part_query_self,
        part_key_self,
        part_value_self,
        part_out_self,
        part_query_cross,
        part_key_cross,
        part_value_cross,
        part_out_cross,
        part_up,
        part_down,
    )
    dims = (1, 0, 0, 0, 1, 0, 0, 0, 1, 0, 1)
    summed = [
        lax.psum_scatter(part, WIDE, scatter_dimension=dim, tiled=True)
        for part, dim in zip(parts, dims)
    ]
    gains = lax.psum((part_gain_self, part_gain_cross, part_gain_feed), (WIDE, NARROW))
    return (
        resid_out.astype(low),
        d_input.astype(low),
        d_words,
        *gains,
        *[part.astype(jnp.float32) for part in summed],
    )


RING = 6
HELD = 8


def send(src, dst, sems, index, peer):
    return pltpu.make_async_remote_copy(
        src_ref=src,
        dst_ref=dst,
        send_sem=sems.at[(0,) + index],
        recv_sem=sems.at[(1,) + index],
        device_id=peer,
        device_id_type=MESH,
    )


def greet(barrier, peer):
    pl.semaphore_signal(barrier, inc=1, device_id=peer, device_id_type=MESH)


def each_slab(count, step, slab=16):
    def body(i, carry):
        step(pl.ds(pl.multiple_of(i * slab, slab), slab))
        return carry

    lax.fori_loop(0, count // slab, body, 0)


class Wide:
    def __init__(self, pairs, units, refs):
        (self.mine, self.right, self.left, self.stage, self.aslot, self.bslot, self.rsem, self.lsem, self.asem,
         self.bsem, self.osem, self.rfree, self.lfree, self.fara, self.farb, self.fasem, self.fbsem) = refs
        self.pairs, self.units = pairs, units
        self.asked, self.gone = set(), set()
        me = lax.axis_index(WIDE)
        self.z, self.y = me // 2, me % 2
        self.has_right, self.has_left = self.z < pairs - 1, self.z > 0
        self.peer = {WIDE: self.z * 2 + 1 - self.y}
        self.end = (self.z == 0) | (self.z == pairs - 1)
        self.inner = (self.z > 0) & (self.z < pairs - 1)
        self.beside = {WIDE: (self.z + 1 - 2 * (self.z % 2)) * 2 + self.y}
        self.next = {WIDE: jnp.minimum(self.z + 1, pairs - 1) * 2 + self.y}
        self.last = {WIDE: jnp.maximum(self.z - 1, 0) * 2 + self.y}
        group = -1
        for i, unit in enumerate(units):
            if i == 0 or unit.rows is not units[i - 1].rows:
                group += 1
            unit.group = group
        self.blk, self.cols = self.mine.shape[2], self.mine.shape[3]

    def meet(self, barrier):
        greet(barrier, self.peer)

        @pl.when(self.has_right)
        def _():
            greet(barrier, self.next)

        @pl.when(self.has_left)
        def _():
            greet(barrier, self.last)

        return 1 + self.has_right.astype(jnp.int32) + self.has_left.astype(jnp.int32)

    def trade(self, i):
        unit = self.units[i]
        return send(unit.columns, unit.nb_columns, unit.sems, (i,), self.peer)

    def loads(self, i):
        unit = self.units[i]
        s, rows = unit.group % 2, unit.count
        copies = []
        if i == 0 or self.units[i - 1].group != unit.group:
            for k in range(self.pairs):
                at = pl.multiple_of((k * 2 + self.y) * self.blk, self.blk)
                sources = (unit.rows.at[:, pl.ds(at, self.blk)], unit.nb_rows.at[:, pl.ds(k * self.blk, self.blk)])
                for part, src in enumerate(sources):
                    copies.append(
                        pltpu.make_async_copy(
                            src, self.aslot.at[s, part, k, pl.ds(0, rows)], self.asem.at[s, part, k]
                        )
                    )
        q = i % 2
        for part, src in enumerate((unit.columns, unit.nb_columns)):
            copies.append(
                pltpu.make_async_copy(src, self.bslot.at[q, part, pl.ds(0, rows)], self.bsem.at[q, part])
            )
        return copies

    def load(self, i):
        unit = self.units[i]
        if not unit.early:
            self.trade(i).wait_recv()
        if unit.halves is not None and (i == 0 or self.units[i - 1].group != unit.group):
            unit.halves.arrive()
        for copy in self.loads(i):
            copy.start()

    def compute(self, i):
        unit = self.units[i]
        s, q, g, rows = unit.group % 2, i % 2, i % HELD, unit.count
        for copy in self.loads(i):
            copy.wait()
        if i >= HELD:
            self.sent(i - HELD)

        def body(k, carry):
            total = None
            for part in (0, 1):
                term = lax.dot_general(
                    self.aslot[s, part, k, :rows], self.bslot[q, part, :rows], FIRST, preferred_element_type=F32
                )
                total = term if total is None else total + term
            self.mine[g, k] = total.astype(LOW)
            return carry

        lax.fori_loop(0, self.pairs, body, 0)

    def add(self, dst, src):
        def step(s):
            dst[s, :] = dst[s, :] + src[s, :]

        each_slab(self.blk, step, 64)

    def r_copy(self, i, t):
        d = jnp.clip(self.pairs - t + self.z, 0, self.pairs - 1)
        return send(self.mine.at[i % HELD, d], self.right.at[i % RING, t - 1], self.rsem, (i, t - 1), self.next)

    def l_copy(self, i, t):
        d = jnp.clip(t - self.pairs + self.z, 0, self.pairs - 1)
        return send(self.mine.at[i % HELD, d], self.left.at[i % RING, t - 1], self.lsem, (i, t - 1), self.last)

    def sends_right(self, t):
        return self.has_right & (t >= self.z + 1)

    def sends_left(self, t):
        return self.has_left & (t >= self.pairs - self.z)

    def credit(self, i, free, when):
        if i >= RING:

            @pl.when(when)
            def _():
                pl.semaphore_wait(free, 1)

    def release(self, i):
        helped = self.units[i].help is not None

        @pl.when(self.z == 0)
        def _():
            if i >= RING:
                pl.semaphore_wait(self.rfree, 1)
            if not helped:
                for t in range(1, self.pairs):
                    self.r_copy(i, t).start()

        @pl.when(self.z == self.pairs - 1)
        def _():
            if i >= RING:
                pl.semaphore_wait(self.lfree, 1)
            if not helped:
                for t in range(1, self.pairs):
                    self.l_copy(i, t).start()

        if helped:

            @pl.when(self.end)
            def _():
                for ship in self.units[i].help.ships:
                    ship.start()

    def assist(self, i):
        unit = self.units[i]
        g, rows = i % HELD, unit.count
        away = jnp.where(self.z == 1, 0, self.pairs - 1)

        @pl.when(self.inner)
        def _():
            for ship in unit.help.ships:
                ship.wait_recv()
            unit.help.arrive()
            copies = []
            for part in (0, 1):
                for k in range(self.pairs):
                    src = unit.help.rows[part].at[:, pl.ds(k * self.blk, self.blk)]
                    copies.append(pltpu.make_async_copy(src, self.fara.at[part, k], self.fasem.at[part, k]))
                copies.append(
                    pltpu.make_async_copy(unit.help.columns[part], self.farb.at[part], self.fbsem.at[part])
                )
            for copy in copies:
                copy.start()
            for copy in copies:
                copy.wait()

            def body(k, carry):
                @pl.when(k != away)
                def _():
                    total = self.mine[g, k].astype(F32)
                    for part in (0, 1):
                        total = total + lax.dot_general(
                            self.fara[part, k], self.farb[part], FIRST, preferred_element_type=F32
                        )
                    self.mine[g, k] = total.astype(LOW)

                return carry

            lax.fori_loop(0, self.pairs, body, 0)

    def step(self, i, t):
        g, r = i % HELD, i % RING
        first_right, first_left = t == self.z + 1, t == self.pairs - self.z
        helped = self.units[i].help is not None

        @pl.when(self.sends_right(t) & self.has_left)
        def _():
            self.credit(i, self.rfree, first_right)

            @pl.when(self.z > 1 if helped else self.z > 0)
            def _():
                self.r_copy(i, t - 1).wait_recv()
                d = jnp.clip(self.pairs - t + self.z, 0, self.pairs - 1)
                self.add(self.mine.at[g, d], self.right.at[r, t - 2])

            self.r_copy(i, t).start()

        @pl.when(self.sends_left(t) & self.has_right)
        def _():
            self.credit(i, self.lfree, first_left)

            @pl.when(self.z < self.pairs - 2 if helped else self.z < self.pairs - 1)
            def _():
                self.l_copy(i, t - 1).wait_recv()
                d = jnp.clip(t - self.pairs + self.z, 0, self.pairs - 1)
                self.add(self.mine.at[g, d], self.left.at[r, t - 2])

            self.l_copy(i, t).start()

    def out_copy(self, i):
        return pltpu.make_async_copy(self.stage.at[i % 2], self.units[i].out, self.osem.at[i % 2])

    def final(self, i):
        g, r, t = i % HELD, i % RING, self.pairs - 1
        helped = self.units[i].help is not None

        @pl.when(self.z > 1 if helped else self.z > 0)
        def _():
            self.r_copy(i, t).wait_recv()
            self.add(self.mine.at[g, self.z], self.right.at[r, t - 1])

        @pl.when(self.z < self.pairs - 2 if helped else self.z < self.pairs - 1)
        def _():
            self.l_copy(i, t).wait_recv()
            self.add(self.mine.at[g, self.z], self.left.at[r, t - 1])

        if i + RING < len(self.units):

            @pl.when(self.has_left)
            def _():
                pl.semaphore_signal(self.rfree, inc=1, device_id=self.last, device_id_type=MESH)

            @pl.when(self.has_right)
            def _():
                pl.semaphore_signal(self.lfree, inc=1, device_id=self.next, device_id_type=MESH)

        if i >= 2:
            self.out_copy(i - 2).wait()

        def step(s):
            self.stage[i % 2, s, :] = self.mine[g, self.z, s, :]

        each_slab(self.blk, step, 64)
        self.out_copy(i).start()

    def sent(self, i):
        helped = self.units[i].help is not None
        for t in range(1, self.pairs):

            @pl.when(self.sends_right(t) & self.has_left if helped else self.sends_right(t))
            def _():
                self.r_copy(i, t).wait_send()

            @pl.when(self.sends_left(t) & self.has_right if helped else self.sends_left(t))
            def _():
                self.l_copy(i, t).wait_send()

    def ask(self, i):
        if i < len(self.units) and not self.units[i].early and i not in self.asked:
            self.asked.add(i)
            self.trade(i).start()

    def move(self, k):
        count, pairs = len(self.units), self.pairs
        if 0 <= k - 1 < count and self.units[k - 1].help is not None:
            self.assist(k - 1)
        for t in range(pairs - 1, 1, -1):
            if 0 <= k - (t - 1) < count:
                self.step(k - (t - 1), t)
        if 0 <= k - (pairs - 1) < count:
            self.final(k - (pairs - 1))

    def leave(self, i):
        if not self.units[i].early and i not in self.gone:
            self.gone.add(i)
            self.trade(i).wait_send()

    def multiply(self, i, loaded=False):
        if not loaded:
            self.load(i)
        self.compute(i)
        self.release(i)

    def drain(self):
        count = len(self.units)
        for i in range(max(0, count - 2), count):
            self.out_copy(i).wait()
        for i in range(max(0, count - HELD), count):
            self.sent(i)
        for i in range(count):
            self.leave(i)
            if self.units[i].help is not None:

                @pl.when(self.end)
                def _():
                    for ship in self.units[i].help.ships:
                        ship.wait_send()

                @pl.when(self.inner)
                def _():
                    self.units[i].help.leave()


VM = pl.BlockSpec(memory_space=pltpu.VMEM)
HB = pl.BlockSpec(memory_space=pl.ANY)


def norm_rows(rows):
    centre = jnp.mean(rows, axis=-1, keepdims=True)
    centred = rows - centre
    variance = jnp.mean(centred * centred, axis=-1, keepdims=True)
    inv_std = lax.rsqrt(variance + 1e-05)
    return centred * inv_std, inv_std


class Narrow:
    def __init__(self):
        self.me = lax.axis_index(NARROW)
        x, c = self.me // 2, self.me % 2
        self.core_at = x * 2 + 1 - c
        self.chip_at = (1 - x) * 2 + c
        self.far_at = (1 - x) * 2 + 1 - c
        self.core = {NARROW: self.core_at}
        self.chip = {NARROW: self.chip_at}

    def meet(self, barrier):
        greet(barrier, self.core)
        greet(barrier, self.chip)
        return 2


class Gather:
    def __init__(self, net, full, own, sems):
        self.net, self.full, self.own, self.sems = net, full, own, sems

    def place(self, b, who):
        at = (b * 4 + who) * self.own
        return self.full.at[pl.ds(pl.multiple_of(at, self.own), self.own), :]

    def mine(self, b):
        return self.place(b, self.net.me)

    def to_core(self, b):
        return send(self.mine(b), self.mine(b), self.sems, (b, 0), self.net.core)

    def to_chip(self, b):
        return send(self.mine(b), self.mine(b), self.sems, (b, 1), self.net.chip)

    def onward(self, b):
        block = self.place(b, self.net.chip_at)
        return send(block, block, self.sems, (b, 2), self.net.core)

    def start(self, b):
        self.to_chip(b).start()
        self.to_core(b).start()

    def forward(self, b):
        self.to_chip(b).wait_recv()
        self.onward(b).start()

    def finish(self, b):
        self.to_core(b).wait_recv()
        self.onward(b).wait_recv()
        self.to_core(b).wait_send()
        self.to_chip(b).wait_send()
        self.onward(b).wait_send()


class Scatter:
    def __init__(self, net, part, landed, outgoing, arrived, sems):
        self.net, self.part, self.landed = net, part, landed
        self.outgoing, self.arrived, self.sems = outgoing, arrived, sems
        self.own = part.shape[1] // 4

    def rows(self, b, who):
        return self.part.at[b, pl.ds(pl.multiple_of(who * self.own, self.own), self.own), :]

    def core_copy(self, b, k):
        who = self.net.far_at if k == 0 else self.net.core_at
        return send(self.rows(b, who), self.landed.at[b, k], self.sems, (b, k), self.net.core)

    def chip_copy(self, b):
        return send(self.outgoing.at[b], self.arrived.at[b], self.sems, (b, 2), self.net.chip)

    def start(self, b):
        self.core_copy(b, 0).start()
        self.core_copy(b, 1).start()

    def cross(self, b):
        self.core_copy(b, 0).wait_recv()
        mine = self.rows(b, self.net.chip_at)

        def step(s):
            total = mine[s, :] + self.landed[b, 0, s, :]
            self.outgoing[b, s, :] = total.astype(self.outgoing.dtype)

        each_slab(self.own, step)
        self.chip_copy(b).start()

    def ready(self, b):
        self.core_copy(b, 1).wait_recv()
        self.chip_copy(b).wait_recv()

    def total(self, b, s):
        near = self.rows(b, self.net.me)[s, :] + self.landed[b, 1, s, :]
        return near + self.arrived[b, s, :].astype(F32)

    def finish(self, b):
        self.core_copy(b, 0).wait_send()
        self.core_copy(b, 1).wait_send()
        self.chip_copy(b).wait_send()


class Halves:
    def __init__(self, net, full, there, pairs, sems, index):
        me = lax.axis_index(WIDE)
        y, rows = me % 2, full.shape[0] // 2
        blk = full.shape[1] // (2 * pairs)
        span = pl.ds(pl.multiple_of(net.me % 2 * rows, rows), rows)
        self.copies = [
            send(
                full.at[span, pl.ds(pl.multiple_of((2 * k + 1 - y) * blk, blk), blk)],
                there.at[span, pl.ds(k * blk, blk)], sems, (index, k), {WIDE: me + 1 - 2 * y},
            )
            for k in range(pairs)
        ]
        self.onward = send(there.at[span], there.at[span], sems, (index, pairs), net.core)

    def start(self):
        for copy in self.copies:
            copy.start()

    def forward(self):
        for copy in self.copies:
            copy.wait_recv()
        self.onward.start()

    def arrive(self):
        self.onward.wait_recv()

    def leave(self):
        for copy in self.copies:
            copy.wait_send()
        self.onward.wait_send()


class Help:
    def __init__(self, ships, rows, columns, onward=()):
        self.ships, self.rows, self.columns, self.onward = ships, rows, columns, onward

    def arrive(self):
        for copy in self.onward:
            copy.start()
        for copy in self.onward:
            copy.wait_recv()

    def leave(self):
        for copy in self.onward:
            copy.wait_send()


def scatter_scratch(images, own, width, hop=LOW):
    return [
        pltpu.VMEM((images, 4 * own, width), F32),
        pltpu.VMEM((images, 2, own, width), F32),
        pltpu.VMEM((images, own, width), hop),
        pltpu.VMEM((images, own, width), hop),
        pltpu.SemaphoreType.DMA((2, images, 3)),
    ]


def params(number, limit):
    return pltpu.CompilerParams(
        collective_id=number, has_side_effects=True, vmem_limit_bytes=limit * 1024 * 1024
    )


class Copies:
    def __init__(self, sems):
        self.sems, self.used, self.open = sems, 0, []

    def start(self, src, dst):
        copy = pltpu.make_async_copy(src, dst, self.sems.at[self.used])
        self.used += 1
        copy.start()
        return copy

    def later(self, src, dst):
        self.open.append(self.start(src, dst))

    def close(self):
        for copy in self.open:
            copy.wait()


def columns_of(width, step, tile=512):
    def body(j, carry):
        step(pl.ds(pl.multiple_of(j * tile, tile), tile))
        return carry

    lax.fori_loop(0, width // tile, body, 0)


def dot(left, right, dims=(((1,), (0,)), ((), ()))):
    return lax.dot_general(left, right, dims, preferred_element_type=F32)


def softmax_parts(q, k):
    scores = dot(q, k, LAST) * (1.0 / math.sqrt(HEAD))
    powers = jnp.exp(scores - jnp.max(scores, axis=-1, keepdims=True))
    return powers / jnp.sum(powers, axis=-1, keepdims=True)


def head_columns(j):
    return pl.ds(pl.multiple_of(j * HEAD, HEAD), HEAD)


def heads_forward(b, images, query, keys, values, out):
    many, some = query.shape[0] // images, keys.shape[0] // images
    asked, told = pl.ds(b * many, many), pl.ds(b * some, some)

    def body(j, carry):
        cols = head_columns(j)
        probs = softmax_parts(query[asked, cols], keys[told, cols])
        out[asked, cols] = dot(probs.astype(LOW), values[told, cols]).astype(LOW)
        return carry

    lax.fori_loop(0, query.shape[1] // HEAD, body, 0)


def heads_back(images, query, keys, values, d_att):
    heads = query.shape[1] // HEAD
    many, some = query.shape[0] // images, keys.shape[0] // images
    scale = 1.0 / math.sqrt(HEAD)

    def body(j, carry):
        b = j // heads
        cols = head_columns(j % heads)
        asked = pl.ds(pl.multiple_of(b * many, many), many)
        told = pl.ds(pl.multiple_of(b * some, some), some)
        q, k, v, d = query[asked, cols], keys[told, cols], values[told, cols], d_att[asked, cols]
        probs = softmax_parts(q, k)
        d_probs = dot(d, v, LAST)
        weighted = jnp.sum(probs * d_probs, axis=-1, keepdims=True)
        d_scores = (probs * (d_probs - weighted)).astype(LOW)
        values[told, cols] = dot(probs.astype(LOW), d, FIRST).astype(LOW)
        keys[told, cols] = (dot(d_scores, q, FIRST) * scale).astype(LOW)
        query[asked, cols] = (dot(d_scores, k) * scale).astype(LOW)
        return carry

    lax.fori_loop(0, images * heads, body, 0)


def gelu(u):
    turn = jnp.tanh(math.sqrt(2.0 / math.pi) * (u + 0.044715 * (u * u * u)))
    return 0.5 * u * (1.0 + turn)


def gelu_slope(u):
    c = math.sqrt(2.0 / math.pi)
    turn = jnp.tanh(c * (u + 0.044715 * (u * u * u)))
    return 0.5 * (1.0 + turn) + 0.5 * u * (1.0 - turn * turn) * (c * (1.0 + 0.134145 * (u * u)))


def flat(array):
    return array.reshape(array.shape[0] * array.shape[1], array.shape[2])


def forward_all(pairs, number, given):
    t = given
    images, own, width = t.tokens.shape
    length, words = 4 * own, t.caption.shape[1]
    inner, ff, states = t.query_self.shape[1], t.up_proj.shape[1], t.caption.shape[2]
    rows, word_rows, word_own = images * length, images * words, words // 4
    chunks, text_chunks = ff // inner, states // inner
    half = width // 2
    vars_in = dict(
        tokens=t.tokens, caption=flat(t.caption), cotangent=t.cotangent, text_proj=t.text_proj,
        query_self=t.query_self, key_self=t.key_self, value_self=t.value_self, out_self=t.out_self,
        query_cross=t.query_cross, key_cross=t.key_cross, value_cross=t.value_cross,
        out_cross=t.out_cross, up_proj=t.up_proj,
    )
    sds = jax.ShapeDtypeStruct
    outs = dict(
        image_self=sds((rows, width), LOW), image_cross=sds((rows, width), LOW),
        image_feed=sds((rows, width), LOW), d_image=sds((rows, width), LOW),
        context=sds((word_rows, width), LOW),
        query_sa=sds((rows, inner), LOW), keys_sa=sds((rows, inner), LOW), values_sa=sds((rows, inner), LOW),
        query_ca=sds((rows, inner), LOW), keys_ca=sds((word_rows, inner), LOW), values_ca=sds((word_rows, inner), LOW),
        attended_sa=sds((rows, inner), LOW), attended_ca=sds((rows, inner), LOW),
        resid_mid=sds((images, own, width), F32), resid_late=sds((images, own, width), F32),
        activ=sds((rows, ff), LOW), pre_act=sds((images, length, ff), F32),
        nb_self=sds((rows, half), LOW), nb_low=sds((rows, half), LOW),
        nb_context=sds((word_rows, half), LOW), nb_first=sds((rows, inner), LOW), nb_caption=sds((word_rows, states), LOW),
        far_caption=sds((2, word_rows, states), LOW), far_context=sds((2, word_rows, half), LOW),
        nb_att_sa=sds((rows, inner), LOW), nb_att_ca=sds((rows, inner), LOW),
    )

    def kernel(*refs):
        h = types.SimpleNamespace(**dict(zip(vars_in, refs)))
        refs = refs[len(vars_in):]
        marks, gain_self, gain_cross, gain_feed = refs[:4]
        refs = refs[4:]
        o = types.SimpleNamespace(**dict(zip(outs, refs)))
        refs = refs[len(outs):]
        scatter_refs, text_refs = refs[:5], refs[5:10]
        (full_s, full_c, full_f, full_d, full_x, gsem_s, gsem_c, gsem_f, gsem_d, gsem_x,
         wn, wt, tok, cot, cap, sq, sk, sv, xq, xk, xv, att_s, att_c, mid, late, act,
         fsem, osem, hsem, asem, zsem) = refs[10:]
        net = Narrow()
        fetch, store = Copies(fsem), Copies(osem)
        barrier = pltpu.get_barrier_semaphore()
        me = lax.axis_index(WIDE)
        pair = {WIDE: me + 1 - 2 * (me % 2)}
        greet(barrier, pair)
        z, y = me // 2, me % 2
        beside = {WIDE: (z + 1 - 2 * (z % 2)) * 2 + y}
        greet(barrier, beside)
        others = net.meet(barrier) + 2
        end = (z == 0) | (z == pairs - 1)
        blk = width // (2 * pairs)
        ships = [
            send(cap, o.far_caption.at[0], zsem, (0,), beside),
            send(o.nb_caption, o.far_caption.at[1], zsem, (1,), beside),
            send(o.nb_context, o.far_context.at[1], zsem, (2,), beside),
        ] + [
            send(
                full_x.at[:, pl.ds(pl.multiple_of((2 * k + y) * blk, blk), blk)],
                o.far_context.at[0, :, pl.ds(k * blk, blk)], zsem, (3 + k,), beside,
            )
            for k in range(pairs)
        ]

        def whole(j, ref):
            return fetch.start(ref, wn.at[j])

        def band(j, ref, c):
            return fetch.start(ref.at[pl.ds(c * inner, inner)], wt.at[j])

        need_tok = fetch.start(h.tokens, tok)
        need_cap = fetch.start(h.caption, cap)
        need_proj = [band(c, h.text_proj, c) for c in range(text_chunks)]
        need_cot = fetch.start(h.cotangent, cot)
        need_qkv = [whole(j, ref) for j, ref in enumerate((h.query_self, h.key_self, h.value_self))]
        need_out_self = fetch.start(h.out_self, wt.at[2])
        need_kv = [whole(4, h.key_cross), whole(5, h.value_cross)]
        need_query_cross = whole(3, h.query_cross)
        need_out_cross = fetch.start(h.out_cross, wt.at[3])
        need_up = {3: fetch.start(h.up_proj.at[:, pl.ds(3 * inner, inner)], wn.at[6])}
        gather_s = Gather(net, full_s, own, gsem_s)
        gather_c = Gather(net, full_c, own, gsem_c)
        gather_f = Gather(net, full_f, own, gsem_f)
        gather_d = Gather(net, full_d, own, gsem_d)
        gather_x = Gather(net, full_x, word_own, gsem_x)
        scatter, text = Scatter(net, *scatter_refs), Scatter(net, *text_refs)
        part = scatter.part

        def of(b, n=length):
            return pl.ds(b * n, n)

        need_tok.wait()
        pl.semaphore_wait(barrier, others)
        for b in range(images):
            mine = gather_s.mine(b)

            def step(s, b=b, mine=mine):
                normed, _ = norm_rows(tok[b, s, :].astype(F32))
                mine[s, :] = (normed * gain_self[...].astype(F32)[None]).astype(LOW)

            each_slab(own, step)
            gather_s.start(b)
        need_cap.wait()
        first = [send(cap, o.nb_caption, asem, (images,), pair)]
        first[0].start()

        @pl.when(end)
        def _():
            ships[0].start()

        for need in need_proj:
            need.wait()
        for b in range(images):

            def step(cols, b=b):
                total = None
                for c in range(text_chunks):
                    term = dot(cap[of(b, words), pl.ds(c * inner, inner)], wt[c, :, cols])
                    total = term if total is None else total + term
                text.part[b, :, cols] = total

            columns_of(width, step)
            text.start(b)
        need_cot.wait()
        for b in range(images):
            mine = gather_d.mine(b)

            def step(s, b=b, mine=mine):
                mine[s, :] = (cot[b, s, :].astype(F32) * marks[b, s, :]).astype(LOW)

            each_slab(own, step)

        def project(b, source, weights, targets, n=length):
            for j, target in zip(weights, targets):
                target[of(b, n), :] = dot(source[of(b, n), :], wn[j]).astype(LOW)

        def back_out(b, attended, j):
            def step(cols):
                part[b, :, cols] = dot(attended[of(b), :], wt[j, :, cols])

            columns_of(width, step)
            scatter.start(b)

        gather_s.forward(0)
        text.cross(0)
        text.cross(1)
        gather_d.start(0)
        for b in range(images):
            gather_s.finish(b)
            if b == 0:
                for need in need_qkv:
                    need.wait()
            project(b, full_s, (0, 1, 2), (sq, sk, sv))
            if b + 1 < images:
                gather_s.forward(b + 1)
            heads_forward(b, images, sq, sk, sv, att_s)
            if b == 0:
                need_out_self.wait()
            back_out(b, att_s, 2)
            if b == 0:
                scatter.cross(b)
        store.later(full_s, o.image_self)
        for ref, out in ((sq, o.query_sa), (sk, o.keys_sa), (sv, o.values_sa), (att_s, o.attended_sa)):
            store.later(ref, out)
        for c in range(3):
            need_up[c] = fetch.start(h.up_proj.at[:, pl.ds(c * inner, inner)], wn.at[c])
        for b in range(images):
            text.ready(b)
            mine = gather_x.mine(b)

            def step(s, b=b, mine=mine):
                mine[s, :] = text.total(b, s).astype(LOW)

            each_slab(word_own, step)
        scatter.cross(1)
        for b in range(images):
            gather_x.start(b)
        halves_self = Halves(net, full_s, o.nb_self, pairs, hsem, 0)
        halves_self.start()
        first.append(send(att_s, o.nb_att_sa, asem, (images + 1,), pair))
        first[-1].start()

        def rows_out(b, source, target, gain, gather):
            scatter.ready(b)
            mine = gather.mine(b)

            def step(s):
                kept = source[b, s, :].astype(F32) + scatter.total(b, s)
                target[b, s, :] = kept
                normed, _ = norm_rows(kept)
                mine[s, :] = (normed * gain[...].astype(F32)[None]).astype(LOW)

            each_slab(own, step)
            gather.start(b)

        rows_out(0, tok, mid, gain_cross, gather_c)
        gather_d.start(1)
        for b in range(images):
            gather_x.forward(b)
        rows_out(1, tok, mid, gain_cross, gather_c)
        store.later(mid, o.resid_mid)
        for need in need_kv:
            need.wait()
        for b in range(images):
            gather_x.finish(b)
            project(b, full_x, (4, 5), (xk, xv), words)
            text.finish(b)
        halves_context = Halves(net, full_x, o.nb_context, pairs, hsem, 1)
        halves_context.start()
        first[0].wait_recv()

        @pl.when(end)
        def _():
            for ship in ships[3:]:
                ship.start()
            ships[1].start()

        store.later(full_x, o.context)
        store.later(xk, o.keys_ca)
        store.later(xv, o.values_ca)
        need_query_cross.wait()
        gather_c.forward(0)
        for b in range(images):
            gather_c.finish(b)
            project(b, full_c, (3,), (xq,))
            if b + 1 < images:
                gather_c.forward(b + 1)
            heads_forward(b, images, xq, xk, xv, att_c)
            scatter.finish(b)
            if b == 0:
                need_out_cross.wait()
            back_out(b, att_c, 3)
            if b == 0:
                for j in range(images):
                    gather_d.forward(j)
                scatter.cross(b)
                for j in range(images):
                    gather_d.finish(j)
                halves_low = Halves(net, full_d, o.nb_low, pairs, hsem, 2)
                halves_low.start()
                store.later(full_d, o.d_image)
        first.append(send(att_c, o.nb_att_ca, asem, (images + 2,), pair))
        first[-1].start()
        store.later(full_c, o.image_cross)
        store.later(xq, o.query_ca)
        store.later(att_c, o.attended_ca)
        scatter.cross(1)
        halves_self.forward()
        halves_context.forward()
        rows_out(0, mid, late, gain_feed, gather_f)
        rows_out(1, mid, late, gain_feed, gather_f)
        store.later(late, o.resid_late)
        halves_low.forward()
        halves_context.arrive()

        @pl.when(end)
        def _():
            ships[2].start()

        first += [
            send(act.at[of(b), pl.ds(0, inner)], o.nb_first.at[of(b)], asem, (b,), pair) for b in range(images)
        ]
        gather_f.forward(0)
        for b in range(images):
            gather_f.finish(b)
            scatter.finish(b)
            for c in range(chunks):
                if b == 0:
                    need_up[c].wait()
                cols = pl.ds(c * inner, inner)
                part[b, :, cols] = dot(full_f[of(b), :], wn[6 if c == 3 else c])
                if b == 0 and c == 1:
                    gather_f.forward(1)

                def step(s, b=b, cols=cols):
                    act[pl.ds(pl.multiple_of(b * length + s.start, 16), 16), cols] = gelu(part[b, s, cols]).astype(LOW)

                each_slab(length, step)
                if c == 0:
                    first[3 + b].start()
        store.later(act, o.activ)
        store.later(part, o.pre_act)
        store.later(full_f, o.image_feed)
        for halves in (halves_self, halves_context, halves_low):
            if halves is not halves_context:
                halves.arrive()
            halves.leave()
        first[0].wait_send()
        for copy in first[1:]:
            copy.wait()

        @pl.when(end)
        def _():
            for ship in ships:
                ship.wait_send()

        @pl.when(jnp.logical_not(end))
        def _():
            for ship in ships:
                ship.wait_recv()

        store.close()

    V, DS = pltpu.VMEM, pltpu.SemaphoreType.DMA
    gsem = DS((2, images, 3))
    scratch = scatter_scratch(images, own, width) + scatter_scratch(images, word_own, width, F32)
    scratch += [V((rows, width), LOW)] * 4 + [V((word_rows, width), LOW)] + [gsem] * 5
    scratch += [
        V((7, width, inner), LOW), V((4, inner, width), LOW),
        V((images, own, width), LOW), V((images, own, width), LOW), V((word_rows, states), LOW),
        V((rows, inner), LOW), V((rows, inner), LOW), V((rows, inner), LOW),
        V((rows, inner), LOW), V((word_rows, inner), LOW), V((word_rows, inner), LOW),
        V((rows, inner), LOW), V((rows, inner), LOW),
        V((images, own, width), F32), V((images, own, width), F32), V((rows, ff), LOW),
        DS((40,)), DS((40,)), DS((2, 3, pairs + 1)), DS((2, images + 3)), DS((2, pairs + 3)),
    ]
    result = pl.pallas_call(
        kernel,
        out_shape=list(outs.values()),
        in_specs=[HB] * len(vars_in) + [VM] * 4,
        out_specs=[HB] * len(outs),
        scratch_shapes=scratch,
        compiler_params=params(number, 62),
        name="forward_all",
    )(*vars_in.values(), t.marks, *t.gains)
    return types.SimpleNamespace(**dict(zip(outs, result)))


def backward_all(pairs, number, given, kept):
    t = given
    images, own, width = t.tokens.shape
    length, words = 4 * own, t.caption.shape[1]
    inner, ff, states = t.query_self.shape[1], t.up_proj.shape[1], t.caption.shape[2]
    rows, word_rows, word_own = images * length, images * words, words // 4
    chunks, text_chunks = ff // inner, states // inner
    half, blk = width // 2, width // (2 * pairs)
    count = 2 * chunks + text_chunks + 8
    vars_in = dict(
        vars(kept),
        tokens=t.tokens, caption=flat(t.caption), cotangent=t.cotangent, text_proj=t.text_proj,
        query_self=t.query_self, key_self=t.key_self, value_self=t.value_self, out_self=t.out_self,
        query_cross=t.query_cross, key_cross=t.key_cross, value_cross=t.value_cross,
        out_cross=t.out_cross, up_proj=t.up_proj, down_proj=t.down_proj,
    )

    def kernel(*refs):
        h = types.SimpleNamespace(**dict(zip(vars_in, refs)))
        refs = refs[len(vars_in):]
        marks, gain_self, gain_cross, gain_feed = refs[:4]
        grads_out, words_out, tokens_out, layer_out, gain_out, nb_cols, nb_feed, nb_cross, nb_late, nb_mid, nb_words, far_cols, far_words = refs[4:17]
        refs = refs[17:]
        scatter_refs = refs[:5]
        (full_c, full_s, full_x, gsem_c, gsem_s, gsem_x, text_sem,
         big, d_att, wa, wb, xq, xk, xv, sq, sk, sv, cot, late, mid, tok, low_rows, word_grad,
         fsem, osem, nbsem, hsem, gacc, gland, gsems, zsem, wordsem) = refs[5:37]
        net = Narrow()
        units = []

        def unit(rows_ref, nb_rows, columns, size, halves=None, early=None, help=None):
            i = len(units)
            there = nb_cols.at[i, pl.ds(0, size)] if early is None else early
            units.append(types.SimpleNamespace(
                rows=rows_ref, nb_rows=nb_rows, columns=columns, count=size, halves=halves,
                nb_columns=there, sems=nbsem, out=grads_out.at[i], early=early is not None, help=help,
            ))

        def chunk(ref, c):
            return ref.at[:, pl.ds(c * inner, inner)]

        halves_feed = Halves(net, h.image_feed, nb_feed, pairs, hsem, 0)
        halves_cross = Halves(net, h.image_cross, nb_cross, pairs, hsem, 1)
        halves_late = Halves(net, full_c, nb_late, pairs, hsem, 2)
        halves_mid = Halves(net, full_s, nb_mid, pairs, hsem, 3)
        halves_words = Halves(net, full_x, nb_words, pairs, hsem, 4)
        for c in range(chunks):
            unit(h.d_image, h.nb_low, chunk(h.activ, c), rows, None, h.nb_first if c == 0 else None)
        for c in range(chunks):
            unit(h.image_feed, nb_feed, chunk(big, c), rows, halves_feed)
        unit(full_c, nb_late, h.attended_ca, rows, halves_late, h.nb_att_ca)
        me = lax.axis_index(WIDE)
        z, y = me // 2, me % 2
        beside = {WIDE: (z + 1 - 2 * (z % 2)) * 2 + y}
        far_rows = (h.far_context.at[0], h.far_context.at[1])
        for j, column in enumerate((xk, xv)):
            theirs = nb_cols.at[len(units), pl.ds(0, word_rows)]
            ships = [
                send(src, far_cols.at[j, part], zsem, (2 * j + part,), beside) for part, src in enumerate((column, theirs))
            ]
            help = Help(ships, far_rows, (far_cols.at[j, 0], far_cols.at[j, 1]))
            unit(h.context, h.nb_context, column, word_rows, None, None, help)
        unit(h.image_cross, nb_cross, xq, rows, halves_cross)
        part_rows = word_rows // 2
        span = pl.ds(pl.multiple_of(net.me % 2 * part_rows, part_rows), part_rows)
        ships = [send(nb_words.at[span], far_words.at[1, span], zsem, (4,), beside)] + [
            send(
                full_x.at[span, pl.ds(pl.multiple_of((2 * k + y) * blk, blk), blk)],
                far_words.at[0, span, pl.ds(k * blk, blk)], zsem, (5 + k,), beside,
            )
            for k in range(pairs)
        ]
        onward = [send(far_words.at[j, span], far_words.at[j, span], wordsem, (j,), net.core) for j in range(2)]
        for c in range(text_chunks):
            help = Help(
                ships if c == 0 else [], (far_words.at[0], far_words.at[1]),
                (chunk(h.far_caption.at[0], c), chunk(h.far_caption.at[1], c)), onward if c == 0 else [],
            )
            unit(full_x, nb_words, chunk(h.caption, c), word_rows, halves_words, chunk(h.nb_caption, c), help)
        unit(full_s, nb_mid, h.attended_sa, rows, halves_mid, h.nb_att_sa)
        for column in (sq, sk, sv):
            unit(h.image_self, h.nb_self, column, rows)
        wide = Wide(pairs, units, refs[37:])
        fetch, store = Copies(fsem), Copies(osem)

        def of(b, n=length):
            return pl.ds(b * n, n)

        barrier = pltpu.get_barrier_semaphore()
        far = {WIDE: (wide.z + 2) % pairs * 2 + wide.y}
        near = {WIDE: (wide.z + 1 - 2 * (wide.z % 2)) * 2 + wide.y}
        greet(barrier, far)
        others = wide.meet(barrier) + net.meet(barrier) + 1

        def up_chunk(c):
            return fetch.start(chunk(h.up_proj, c), wa.at[c % 2])

        wide.load(0)
        need_image = fetch.start(h.d_image, full_s)

        def down_chunk(c):
            return fetch.start(h.down_proj.at[pl.ds(c * inner, inner)], wb.at[c % 2])

        need_down = {c: down_chunk(c) for c in range(2)}
        need_pre = fetch.start(h.pre_act, scatter_refs[0])
        need_up = {c: up_chunk(c) for c in range(2)}
        need_cot = fetch.start(h.cotangent, cot)
        need_late = fetch.start(h.resid_late, late)
        need_ca = [fetch.start(a, b) for a, b in ((h.query_ca, xq), (h.keys_ca, xk), (h.values_ca, xv))]
        need_mid = fetch.start(h.resid_mid, mid)
        need_sa = [fetch.start(a, b) for a, b in ((h.query_sa, sq), (h.keys_sa, sk), (h.values_sa, sv))]
        need_tok = fetch.start(h.tokens, tok)
        pl.semaphore_wait(barrier, others)
        wide.ask(1)
        wide.ask(2)
        wide.multiply(0, True)
        scatter = Scatter(net, *scatter_refs)
        part = scatter.part
        gather_c, gather_s = Gather(net, full_c, own, gsem_c), Gather(net, full_s, own, gsem_s)
        gather_x = Gather(net, full_x, word_own, gsem_x)

        need_image.wait()
        need_pre.wait()
        for c in range(chunks):
            need_down[c].wait()
            cols = pl.ds(c * inner, inner)
            for b in range(images):
                slope = dot(full_s[of(b), :], wb[c % 2], LAST)
                big[of(b), cols] = (gelu_slope(part[b, :, cols]) * slope).astype(LOW)
            if c + 2 < chunks:
                need_down[c + 2] = down_chunk(c + 2)
            if c == 1:
                wide.ask(3)
                halves_feed.start()
        need_out = fetch.start(h.out_cross, wb.at[0])
        need_out_self = fetch.start(h.out_self, wb.at[1])
        wide.multiply(1)
        wide.ask(4)
        wide.move(1)
        for c in range(chunks):
            need_up[c].wait()
            for b in range(images):

                def step(cols, b=b, c=c):
                    term = dot(big[of(b), pl.ds(c * inner, inner)], wa[c % 2, cols, :], LAST)
                    part[b, :, cols] = term if c == 0 else part[b, :, cols] + term

                columns_of(width, step)
                if c == chunks - 1:
                    scatter.start(b)
            if c + 2 < chunks:
                need_up[c + 2] = up_chunk(c + 2)
        need_query = fetch.start(h.query_cross, wa.at[0])
        need_key = fetch.start(h.key_cross, wa.at[1])
        gacc[...] = jnp.zeros_like(gacc)

        def back_rows(b, above, mask, source, gain, slot, keep, mine):
            scatter.ready(b)

            def step(s):
                d_hidden = scatter.total(b, s)
                normed, inv_std = norm_rows(source[b, s, :].astype(F32))
                gacc[slot : slot + 1, :] += jnp.sum(d_hidden * normed, axis=0, keepdims=True)
                top = above[b, s, :].astype(F32)
                if mask is not None:
                    top = top * mask[b, s, :]
                scaled = d_hidden * gain[...].astype(F32)[None]
                inside = scaled - jnp.mean(scaled, axis=-1, keepdims=True)
                inside = inside - normed * jnp.mean(scaled * normed, axis=-1, keepdims=True)
                d_rows = top + inv_std * inside
                if keep is not None:
                    keep[b, s, :] = d_rows
                mine[s, :] = d_rows.astype(LOW)

            each_slab(own, step)

        def multiply(b, target, lefts, rights, n=length):
            def step(cols):
                total = None
                for left, j in zip(lefts, rights):
                    term = dot(left[of(b, n), :], wa[j, cols, :], LAST)
                    total = term if total is None else total + term
                target[b, :, cols] = total

            columns_of(width, step)

        def out_back(b, full, j):
            d_att[of(b), :] = dot(full[of(b), :], wb[j], LAST).astype(LOW)

        wide.multiply(2)
        wide.ask(5)
        wide.move(2)
        for b in range(images):
            scatter.cross(b)
        wide.multiply(3)
        wide.ask(6)
        need_cot.wait()
        need_late.wait()
        for b in range(images):
            back_rows(b, cot, marks, late, gain_feed, 2, late, gather_c.mine(b))
            gather_c.start(b)
        wide.move(3)
        halves_feed.forward()
        for b in range(images):
            gather_c.forward(b)
        wide.multiply(4)
        wide.ask(7)
        need_out.wait()
        for b in range(images):
            scatter.finish(b)
            gather_c.finish(b)
            out_back(b, full_c, 0)
        halves_late.start()
        need_text = fetch.start(h.text_proj.at[pl.ds(0, inner)], wb.at[0])
        wide.move(4)
        wide.multiply(5)
        for need in need_ca:
            need.wait()
        heads_back(images, xq, xk, xv, d_att)
        wide.ask(9)
        wide.ask(10)
        halves_cross.start()
        need_query.wait()
        for b in range(images):
            multiply(b, part, [xq], [0])
            scatter.start(b)
        need_value = fetch.start(h.value_cross, wa.at[0])
        wide.multiply(6)
        wide.ask(11)
        for b in range(images):
            scatter.cross(b)
        wide.move(5)
        need_mid.wait()
        for b in range(images):
            back_rows(b, late, None, mid, gain_cross, 1, mid, gather_s.mine(b))
            gather_s.start(b)
        need_again = fetch.start(h.resid_late, late)
        wide.multiply(7)
        halves_late.forward()
        wide.move(6)
        for b in range(images):
            gather_s.forward(b)
        wide.multiply(8)
        for b in range(images):
            scatter.finish(b)
            gather_s.finish(b)
        halves_mid.start()
        text = Scatter(
            net, part.at[:, pl.ds(0, words)], scatter.landed.at[:, :, pl.ds(0, word_own)],
            scatter.outgoing.at[:, pl.ds(0, word_own)], scatter.arrived.at[:, pl.ds(0, word_own)], text_sem,
        )
        need_key.wait()
        need_value.wait()
        for b in range(images):
            multiply(b, text.part, [xk, xv], [1, 0], words)
            text.start(b)
        need_qkv = [fetch.start(h.query_self, wa.at[0]), fetch.start(h.key_self, wa.at[1])]
        need_out_self.wait()
        for b in range(images):
            out_back(b, full_s, 1)
        need_second = fetch.start(h.text_proj.at[pl.ds(inner, inner)], wb.at[1])
        wide.move(7)
        for b in range(images):
            text.cross(b)
        wide.multiply(9)
        for need in need_sa:
            need.wait()
        heads_back(images, sq, sk, sv, d_att)
        for b in range(images):
            text.ready(b)
            mine = gather_x.mine(b)

            def step(s, b=b, mine=mine):
                mine[s, :] = text.total(b, s).astype(LOW)

            each_slab(word_own, step)
            gather_x.start(b)
        wide.multiply(10)
        halves_cross.forward()
        wide.move(8)
        for b in range(images):
            gather_x.forward(b)
        for b in range(images):
            text.finish(b)
            gather_x.finish(b)
        halves_words.start()
        for c, need in enumerate((need_text, need_second)):
            need.wait()
            word_grad[:, pl.ds(c * inner, inner)] = dot(full_x[...], wb[c], LAST).astype(LOW)
        store.later(word_grad, words_out)
        need_down = {c: down_chunk(c) for c in range(2)}
        for need in need_qkv:
            need.wait()
        for b in range(images):
            multiply(b, part, [sq, sk], [0, 1])
        need_value = fetch.start(h.value_self, wa.at[0])
        wide.multiply(11)
        for c in range(chunks):
            wide.leave(chunks + c)
        need_act = fetch.start(h.activ, big)
        wide.move(9)
        need_value.wait()
        for b in range(images):

            def step(cols, b=b):
                part[b, :, cols] += dot(sv[of(b), :], wa[0, cols, :], LAST)

            columns_of(width, step)
            scatter.start(b)
        halves_words.forward()
        wide.multiply(12)
        for b in range(images):
            scatter.cross(b)
        wide.move(10)
        need_tok.wait()
        for b in range(images):
            back_rows(b, mid, None, tok, gain_self, 0, None, low_rows.at[b])
        store.later(low_rows, tokens_out)
        for b in range(images):
            scatter.finish(b)
        wide.ask(15)
        halves_mid.forward()
        wide.multiply(13)
        wide.move(11)
        trips = [
            send(gacc, gland.at[j], gsems, (j,), peer)
            for j, peer in enumerate((net.core, net.chip, wide.peer, near, far))
        ]

        def trip(j):
            if j > 0:
                trips[j - 1].wait()
                gacc[...] = gacc[...] + gland[j - 1]
            if j < len(trips):
                trips[j].start()

        def forward_chunk(c):
            need_down[c].wait()
            for b in range(images):

                def step(cols, b=b):
                    term = dot(big[of(b), pl.ds(c * inner, inner)], wb[c % 2, :, cols])
                    part[b, :, cols] = term if c == 0 else part[b, :, cols] + term

                columns_of(width, step)
            if c + 2 < chunks:
                need_down[c + 2] = down_chunk(c + 2)

        trip(0)
        wide.multiply(14)
        wide.ask(16)
        trip(1)
        wide.move(12)
        trip(2)
        wide.multiply(15)
        wide.ask(17)
        trip(3)
        wide.move(13)
        wide.multiply(16)
        need_act.wait()
        forward_chunk(0)
        wide.move(14)
        forward_chunk(1)
        wide.multiply(17)
        wide.move(15)
        for c in range(2, chunks):
            forward_chunk(c)
        for b in range(images):
            scatter.start(b)
        wide.move(16)
        for b in range(images):
            scatter.cross(b)
        trip(4)
        wide.move(17)
        need_again.wait()
        for b in range(images):
            scatter.ready(b)

            def step(s, b=b):
                tok[b, s, :] = (late[b, s, :] + scatter.total(b, s)).astype(LOW)

            each_slab(own, step)
            scatter.finish(b)
        store.later(tok, layer_out)
        for k in range(18, count + pairs - 1):
            wide.move(k)
        trip(5)
        store.later(gacc, gain_out)
        wide.drain()
        for halves in (halves_feed, halves_cross, halves_late, halves_mid, halves_words):
            halves.leave()
        store.close()

    V, DS = pltpu.VMEM, pltpu.SemaphoreType.DMA
    gsem = DS((2, images, 3))
    scratch = scatter_scratch(images, own, width)
    scratch += [V((rows, width), LOW), V((rows, width), LOW), V((word_rows, width), LOW)] + [gsem] * 4
    scratch += [
        V((rows, ff), LOW), V((rows, inner), LOW), V((2, width, inner), LOW), V((2, inner, width), LOW),
        V((rows, inner), LOW), V((word_rows, inner), LOW), V((word_rows, inner), LOW),
        V((rows, inner), LOW), V((rows, inner), LOW), V((rows, inner), LOW),
        V((images, own, width), LOW), V((images, own, width), F32), V((images, own, width), F32),
        V((images, own, width), LOW), V((images, own, width), LOW), V((word_rows, states), LOW),
        DS((48,)), DS((8,)), DS((2, count)), DS((2, 5, pairs + 1)), V((8, width), F32), V((5, 8, width), F32), DS((2, 5)), DS((2, 5 + pairs)), DS((2, 2)),
    ]
    scratch += [
        V((HELD, pairs, blk, inner), LOW),
        V((RING, pairs - 1, blk, inner), LOW), V((RING, pairs - 1, blk, inner), LOW), V((2, blk, inner), LOW),
        V((2, 2, pairs, rows, blk), LOW), V((2, 2, rows, inner), LOW),
        DS((2, count, pairs - 1)), DS((2, count, pairs - 1)),
        DS((2, 2, pairs)), DS((2, 2)), DS((2,)),
        pltpu.SemaphoreType.REGULAR, pltpu.SemaphoreType.REGULAR,
        V((2, pairs, word_rows, blk), LOW), V((2, word_rows, inner), LOW), DS((2, pairs)), DS((2,)),
    ]
    sds = jax.ShapeDtypeStruct
    result = pl.pallas_call(
        kernel,
        out_shape=[
            sds((count, blk, inner), LOW), sds((word_rows, states), LOW), sds((images, own, width), LOW),
            sds((images, own, width), LOW), sds((8, width), F32), sds((count, rows, inner), LOW), sds((rows, half), LOW),
            sds((rows, half), LOW), sds((rows, half), LOW), sds((rows, half), LOW), sds((word_rows, half), LOW),
            sds((2, 2, word_rows, inner), LOW), sds((2, word_rows, half), LOW),
        ],
        in_specs=[HB] * len(vars_in) + [VM] * 4,
        out_specs=[HB] * 13,
        scratch_shapes=scratch,
        compiler_params=params(number, 62),
        name="backward_all",
    )(*vars_in.values(), t.marks, *t.gains)
    return result[:5]


def spread(blocks, places, shapes, whole, gains):
    count, blk, inner = blocks.shape
    more = len(whole)

    def kernel(*refs):
        blocks_ref, whole_in, gains_ref, refs = refs[0], refs[1 : 1 + more], refs[1 + more], refs[2 + more :]
        outs, whole_out, refs = refs[: len(shapes)], refs[len(shapes) : len(shapes) + more], refs[len(shapes) + more :]
        gains_out, refs = refs[:3], refs[3:]
        for j, row in enumerate(gains_out):
            row[...] = gains_ref[j, :]
        held, flat_stage, turned_stage, isem, osem, wsem, *kept = refs
        ins = [pltpu.make_async_copy(blocks_ref.at[i], held.at[i], isem.at[i]) for i in range(count)]
        for copy in ins:
            copy.start()
        done, plain, turns = [], 0, 0
        came = [pltpu.make_async_copy(whole_in[j], kept[j], wsem.at[0, j]) for j in range(more)]
        for copy in came:
            copy.start()
        for i, (which, row, col, turned) in enumerate(places):
            ins[i].wait()
            if turned:
                stage = turned_stage.at[turns]
                turns += 1
                for j in range(0, inner, 128):
                    stage[pl.ds(j, 128), :] = held[i, :, pl.ds(j, 128)].astype(F32).T
                place = outs[which].at[pl.ds(row, inner), pl.ds(col, blk)]
            else:
                stage = flat_stage.at[plain]
                plain += 1
                stage[...] = held[i].astype(F32)
                place = outs[which].at[pl.ds(row, blk), pl.ds(col, inner)]
            done.append(pltpu.make_async_copy(stage, place, osem.at[i]))
            done[-1].start()
        for j in range(more):
            came[j].wait()
            done.append(pltpu.make_async_copy(kept[j], whole_out[j], wsem.at[1, j]))
            done[-1].start()
        for copy in done:
            copy.wait()

    turns = sum(1 for place in places if place[3])
    V, DS = pltpu.VMEM, pltpu.SemaphoreType.DMA
    return pl.pallas_call(
        kernel,
        out_shape=[jax.ShapeDtypeStruct(shape, F32) for shape in shapes]
        + [jax.ShapeDtypeStruct(array.shape, array.dtype) for array in whole]
        + [jax.ShapeDtypeStruct(gains.shape[1:], F32)] * 3,
        in_specs=[HB] * (1 + more) + [VM],
        out_specs=[HB] * (len(shapes) + more) + [VM] * 3,
        scratch_shapes=[
            V((count, blk, inner), LOW), V((count - turns, blk, inner), F32), V((turns, inner, blk), F32),
            DS((count,)), DS((count,)), DS((2, more)),
        ] + [V(array.shape, array.dtype) for array in whole],
        compiler_params=pltpu.CompilerParams(vmem_limit_bytes=62 * 1024 * 1024),
        name="spread",
    )(blocks, *whole, gains)


def by_kernels(
    tokens, caption, token_mask, cotangent, gain_self, gain_cross, gain_feed, text_proj,
    query_self, key_self, value_self, out_self, query_cross, key_cross, value_cross, out_cross, up_proj, down_proj,
):
    given = types.SimpleNamespace(
        tokens=tokens, caption=caption, cotangent=cotangent, text_proj=text_proj,
        query_self=query_self, key_self=key_self, value_self=value_self, out_self=out_self,
        query_cross=query_cross, key_cross=key_cross, value_cross=value_cross, out_cross=out_cross,
        up_proj=up_proj, down_proj=down_proj, marks=token_mask[:, :, None].astype(F32),
        gains=[gain_self, gain_cross, gain_feed],
    )
    pairs = lax.axis_size(WIDE) // 2
    kept = forward_all(pairs, 1, given)
    grads, d_words, d_tokens, layer_out, gains = backward_all(pairs, 2, given, kept)
    inner = query_self.shape[1]
    blk = query_self.shape[0] // (2 * pairs)
    ff, text = up_proj.shape[1] // inner, caption.shape[2] // inner
    places = [(10, c * inner, 0, True) for c in range(ff)]
    places += [(9, 0, c * inner, False) for c in range(ff)]
    places += [(8, 0, 0, True), (6, 0, 0, False), (7, 0, 0, False), (5, 0, 0, False)]
    places += [(0, c * inner, 0, True) for c in range(text)]
    places += [(4, 0, 0, True), (1, 0, 0, False), (2, 0, 0, False), (3, 0, 0, False)]
    shapes = [(text * inner, blk)] + [(blk, inner)] * 3 + [(inner, blk)] + [(blk, inner)] * 3 + [(inner, blk)]
    shapes += [(blk, ff * inner), (ff * inner, blk)]
    out = spread(grads, places, shapes, [layer_out, d_tokens, d_words], gains)
    sums, (layer_out, d_tokens, d_words, *gains) = out[: len(shapes)], out[len(shapes) :]
    return (layer_out, d_tokens, d_words.reshape(caption.shape), *gains, *sums)


def local(
    tokens,
    caption,
    token_mask,
    cotangent,
    gain_self,
    gain_cross,
    gain_feed,
    text_proj,
    query_self,
    key_self,
    value_self,
    out_self,
    query_cross,
    key_cross,
    value_cross,
    out_cross,
    up_proj,
    down_proj,
):
    given = (tokens, caption, token_mask, cotangent, gain_self, gain_cross, gain_feed, text_proj, query_self, key_self, value_self, out_self, query_cross, key_cross, value_cross, out_cross, up_proj, down_proj)
    if lax.axis_size(WIDE) != 8 or lax.axis_size(NARROW) != 4:
        return by_collectives(*given)
    return by_kernels(*given)


def solution(mesh):
    in_specs = (
        P(WIDE, NARROW, None),
        P(WIDE, None, NARROW),
        P(WIDE, NARROW),
        P(WIDE, NARROW, None),
        P(),
        P(),
        P(),
        P(NARROW, None),
        P(None, NARROW),
        P(None, NARROW),
        P(None, NARROW),
        P(NARROW, None),
        P(None, NARROW),
        P(None, NARROW),
        P(None, NARROW),
        P(NARROW, None),
        P(None, NARROW),
        P(NARROW, None),
    )
    out_specs = (
        P(WIDE, NARROW, None),
        P(WIDE, NARROW, None),
        P(WIDE, None, NARROW),
        P(),
        P(),
        P(),
        P(NARROW, WIDE),
        P(WIDE, NARROW),
        P(WIDE, NARROW),
        P(WIDE, NARROW),
        P(NARROW, WIDE),
        P(WIDE, NARROW),
        P(WIDE, NARROW),
        P(WIDE, NARROW),
        P(NARROW, WIDE),
        P(WIDE, NARROW),
        P(NARROW, WIDE),
    )
    return jax.shard_map(local, mesh=mesh, in_specs=in_specs, out_specs=out_specs, check_vma=False)
```

```python
import math
import types

import jax
import jax.numpy as jnp
from jax import lax
from jax.experimental import pallas as pl
from jax.experimental.pallas import tpu as pltpu
from jax.sharding import PartitionSpec as P

HEAD = 128
MESH = pl.DeviceIdType.MESH
WIDE, NARROW = "wide", "narrow"
LOW, F32 = jnp.bfloat16, jnp.float32
LAST, FIRST = (((1,), (1,)), ((), ())), (((0,), (0,)), ((), ()))

def normalize(rows):
    centre = jnp.mean(rows, axis=-1, keepdims=True)
    centred = rows - centre
    variance = jnp.mean(centred * centred, axis=-1, keepdims=True)
    inv_std = lax.rsqrt(variance + 1e-05)
    return (centred * inv_std, inv_std)


def norm_back(d_normed, normed, inv_std):
    inner = d_normed - jnp.mean(d_normed, axis=-1, keepdims=True)
    inner = inner - normed * jnp.mean(d_normed * normed, axis=-1, keepdims=True)
    return inv_std * inner


def times_weight(left, right):
    return jnp.dot(left, right, preferred_element_type=jnp.float32)


def split_heads(matrix):
    return matrix.reshape(matrix.shape[0], matrix.shape[1], matrix.shape[2] // HEAD, HEAD)


def join_heads(heads):
    return heads.reshape(heads.shape[0], heads.shape[1], heads.shape[2] * HEAD)


def head_scores(query, keys):
    scores = jnp.einsum(
        "bqhe,bkhe->bhqk", split_heads(query), split_heads(keys), preferred_element_type=jnp.float32
    )
    return scores * (1.0 / math.sqrt(HEAD))


def attend(query, keys, values):
    scores = head_scores(query, keys)
    peak = jnp.max(scores, axis=-1, keepdims=True)
    powers = jnp.exp(scores - peak)
    summed = jnp.sum(powers, axis=-1, keepdims=True)
    low_probs = (powers / summed).astype(jnp.bfloat16)
    attended = jnp.einsum(
        "bhqk,bkhe->bqhe", low_probs, split_heads(values), preferred_element_type=jnp.float32
    )
    return join_heads(attended).astype(jnp.bfloat16), peak + jnp.log(summed)


def attend_back(query, keys, values, log_total, d_attended):
    probs = jnp.exp(head_scores(query, keys) - log_total)
    low_probs = probs.astype(jnp.bfloat16)
    d_heads = split_heads(d_attended)
    d_probs = jnp.einsum(
        "bqhe,bkhe->bhqk", d_heads, split_heads(values), preferred_element_type=jnp.float32
    )
    d_values = jnp.einsum("bhqk,bqhe->bkhe", low_probs, d_heads, preferred_element_type=jnp.float32)
    weighted = jnp.sum(probs * d_probs, axis=-1, keepdims=True)
    d_scores = (probs * (d_probs - weighted)).astype(jnp.bfloat16)
    scale = 1.0 / math.sqrt(HEAD)
    d_query = (
        jnp.einsum("bhqk,bkhe->bqhe", d_scores, split_heads(keys), preferred_element_type=jnp.float32)
        * scale
    )
    d_keys = (
        jnp.einsum("bhqk,bqhe->bkhe", d_scores, split_heads(query), preferred_element_type=jnp.float32)
        * scale
    )
    return tuple(join_heads(d).astype(jnp.bfloat16) for d in (d_query, d_keys, d_values))


def contract(left, right):
    return lax.dot_general(
        left, right, (((0, 1), (0, 1)), ((), ())), preferred_element_type=jnp.float32
    ).astype(jnp.bfloat16)


def against(left, right):
    return lax.dot_general(
        left, right, (((2,), (1,)), ((), ())), preferred_element_type=jnp.float32
    )


def group_rows(piece):
    return lax.all_gather(piece, NARROW, axis=1, tiled=True)


def own_rows(partial):
    return lax.psum_scatter(partial, NARROW, scatter_dimension=1, tiled=True)


def feed_back(partial):
    return own_rows(partial.astype(jnp.bfloat16)).astype(jnp.float32)


def text_total(partial):
    return lax.psum(partial, NARROW)


def by_collectives(
    tokens,
    caption,
    token_mask,
    cotangent,
    gain_self,
    gain_cross,
    gain_feed,
    text_proj,
    query_self,
    key_self,
    value_self,
    out_self,
    query_cross,
    key_cross,
    value_cross,
    out_cross,
    up_proj,
    down_proj,
):
    gain_one = gain_self.astype(jnp.float32)
    gain_two = gain_cross.astype(jnp.float32)
    gain_three = gain_feed.astype(jnp.float32)
    low = jnp.bfloat16

    resid_in = tokens.astype(jnp.float32)
    normed_self, inv_self = normalize(resid_in)
    image_self = group_rows((normed_self * gain_one).astype(low))
    query_sa = times_weight(image_self, query_self).astype(low)
    keys_sa = times_weight(image_self, key_self).astype(low)
    values_sa = times_weight(image_self, value_self).astype(low)
    attended_sa, total_sa = attend(query_sa, keys_sa, values_sa)
    resid_mid = resid_in + own_rows(times_weight(attended_sa, out_self))
    context = text_total(times_weight(caption, text_proj)).astype(low)
    keys_ca = times_weight(context, key_cross).astype(low)
    values_ca = times_weight(context, value_cross).astype(low)
    normed_cross, inv_cross = normalize(resid_mid)
    image_cross = group_rows((normed_cross * gain_two).astype(low))
    query_ca = times_weight(image_cross, query_cross).astype(low)
    attended_ca, total_ca = attend(query_ca, keys_ca, values_ca)
    resid_late = resid_mid + own_rows(times_weight(attended_ca, out_cross))
    normed_feed, inv_feed = normalize(resid_late)
    d_result = cotangent.astype(jnp.float32) * token_mask[:, :, None].astype(jnp.float32)
    d_image = group_rows(d_result.astype(low))
    image_feed = group_rows((normed_feed * gain_three).astype(low))
    pre_act = times_weight(image_feed, up_proj)
    gelu_out, gelu_pull = jax.vjp(jax.nn.gelu, pre_act)
    activ = gelu_out.astype(low)
    resid_out = resid_late + feed_back(times_weight(activ, down_proj))
    d_pre = gelu_pull(against(d_image, down_proj))[0].astype(low)
    part_down = contract(activ, d_image)
    part_up = contract(image_feed, d_pre)
    d_hidden_feed = feed_back(against(d_pre, up_proj))
    part_gain_feed = jnp.sum(d_hidden_feed * normed_feed, axis=(0, 1))
    d_late = d_result + norm_back(d_hidden_feed * gain_three, normed_feed, inv_feed)
    d_image_cross = group_rows(d_late.astype(low))
    part_out_cross = contract(attended_ca, d_image_cross)
    d_attended_ca = against(d_image_cross, out_cross).astype(low)
    d_query_ca, d_keys_ca, d_values_ca = attend_back(
        query_ca, keys_ca, values_ca, total_ca, d_attended_ca
    )
    part_query_cross = contract(image_cross, d_query_ca)
    part_key_cross = contract(context, d_keys_ca)
    part_value_cross = contract(context, d_values_ca)
    d_hidden_cross = own_rows(against(d_query_ca, query_cross))
    d_context = text_total(against(d_keys_ca, key_cross) + against(d_values_ca, value_cross))
    d_context = d_context.astype(low)
    part_text = contract(caption, d_context)
    d_words = against(d_context, text_proj).astype(low)
    part_gain_cross = jnp.sum(d_hidden_cross * normed_cross, axis=(0, 1))
    d_mid = d_late + norm_back(d_hidden_cross * gain_two, normed_cross, inv_cross)
    d_image_self = group_rows(d_mid.astype(low))
    part_out_self = contract(attended_sa, d_image_self)
    d_attended_sa = against(d_image_self, out_self).astype(low)
    d_query_sa, d_keys_sa, d_values_sa = attend_back(
        query_sa, keys_sa, values_sa, total_sa, d_attended_sa
    )
    part_query_self = contract(image_self, d_query_sa)
    part_key_self = contract(image_self, d_keys_sa)
    part_value_self = contract(image_self, d_values_sa)
    d_hidden_self = own_rows(
        against(d_query_sa, query_self)
        + against(d_keys_sa, key_self)
        + against(d_values_sa, value_self)
    )
    part_gain_self = jnp.sum(d_hidden_self * normed_self, axis=(0, 1))
    d_input = d_mid + norm_back(d_hidden_self * gain_one, normed_self, inv_self)
    parts = (
        part_text,
        part_query_self,
        part_key_self,
        part_value_self,
        part_out_self,
        part_query_cross,
        part_key_cross,
        part_value_cross,
        part_out_cross,
        part_up,
        part_down,
    )
    dims = (1, 0, 0, 0, 1, 0, 0, 0, 1, 0, 1)
    summed = [
        lax.psum_scatter(part, WIDE, scatter_dimension=dim, tiled=True)
        for part, dim in zip(parts, dims)
    ]
    gains = lax.psum((part_gain_self, part_gain_cross, part_gain_feed), (WIDE, NARROW))
    return (
        resid_out.astype(low),
        d_input.astype(low),
        d_words,
        *gains,
        *[part.astype(jnp.float32) for part in summed],
    )


RING = 6
HELD = 8


def send(src, dst, sems, index, peer):
    return pltpu.make_async_remote_copy(
        src_ref=src,
        dst_ref=dst,
        send_sem=sems.at[(0,) + index],
        recv_sem=sems.at[(1,) + index],
        device_id=peer,
        device_id_type=MESH,
    )


def greet(barrier, peer):
    pl.semaphore_signal(barrier, inc=1, device_id=peer, device_id_type=MESH)


def each_slab(count, step, slab=16):
    def body(i, carry):
        step(pl.ds(pl.multiple_of(i * slab, slab), slab))
        return carry

    lax.fori_loop(0, count // slab, body, 0)


class Wide:
    def __init__(self, pairs, units, refs):
        (self.mine, self.right, self.left, self.stage, self.aslot, self.bslot, self.rsem, self.lsem, self.asem,
         self.bsem, self.osem, self.rfree, self.lfree, self.fara, self.farb, self.fasem, self.fbsem) = refs
        self.pairs, self.units = pairs, units
        self.asked, self.gone = set(), set()
        me = lax.axis_index(WIDE)
        self.z, self.y = me // 2, me % 2
        self.has_right, self.has_left = self.z < pairs - 1, self.z > 0
        self.peer = {WIDE: self.z * 2 + 1 - self.y}
        self.end = (self.z == 0) | (self.z == pairs - 1)
        self.inner = (self.z > 0) & (self.z < pairs - 1)
        self.beside = {WIDE: (self.z + 1 - 2 * (self.z % 2)) * 2 + self.y}
        self.next = {WIDE: jnp.minimum(self.z + 1, pairs - 1) * 2 + self.y}
        self.last = {WIDE: jnp.maximum(self.z - 1, 0) * 2 + self.y}
        group = -1
        for i, unit in enumerate(units):
            if i == 0 or unit.rows is not units[i - 1].rows:
                group += 1
            unit.group = group
        self.blk, self.cols = self.mine.shape[2], self.mine.shape[3]

    def meet(self, barrier):
        greet(barrier, self.peer)

        @pl.when(self.has_right)
        def _():
            greet(barrier, self.next)

        @pl.when(self.has_left)
        def _():
            greet(barrier, self.last)

        return 1 + self.has_right.astype(jnp.int32) + self.has_left.astype(jnp.int32)

    def trade(self, i):
        unit = self.units[i]
        return send(unit.columns, unit.nb_columns, unit.sems, (i,), self.peer)

    def loads(self, i):
        unit = self.units[i]
        s, rows = unit.group % 2, unit.count
        copies = []
        if i == 0 or self.units[i - 1].group != unit.group:
            for k in range(self.pairs):
                at = pl.multiple_of((k * 2 + self.y) * self.blk, self.blk)
                sources = (unit.rows.at[:, pl.ds(at, self.blk)], unit.nb_rows.at[:, pl.ds(k * self.blk, self.blk)])
                for part, src in enumerate(sources):
                    copies.append(
                        pltpu.make_async_copy(
                            src, self.aslot.at[s, part, k, pl.ds(0, rows)], self.asem.at[s, part, k]
                        )
                    )
        q = i % 2
        for part, src in enumerate((unit.columns, unit.nb_columns)):
            copies.append(
                pltpu.make_async_copy(src, self.bslot.at[q, part, pl.ds(0, rows)], self.bsem.at[q, part])
            )
        return copies

    def load(self, i):
        unit = self.units[i]
        if not unit.early:
            self.trade(i).wait_recv()
        if unit.halves is not None and (i == 0 or self.units[i - 1].group != unit.group):
            unit.halves.arrive()
        for copy in self.loads(i):
            copy.start()

    def compute(self, i):
        unit = self.units[i]
        s, q, g, rows = unit.group % 2, i % 2, i % HELD, unit.count
        for copy in self.loads(i):
            copy.wait()
        if i >= HELD:
            self.sent(i - HELD)

        def body(k, carry):
            total = None
            for part in (0, 1):
                term = lax.dot_general(
                    self.aslot[s, part, k, :rows], self.bslot[q, part, :rows], FIRST, preferred_element_type=F32
                )
                total = term if total is None else total + term
            self.mine[g, k] = total.astype(LOW)
            return carry

        lax.fori_loop(0, self.pairs, body, 0)

    def add(self, dst, src):
        def step(s):
            dst[s, :] = dst[s, :] + src[s, :]

        each_slab(self.blk, step, 64)

    def r_copy(self, i, t):
        d = jnp.clip(self.pairs - t + self.z, 0, self.pairs - 1)
        return send(self.mine.at[i % HELD, d], self.right.at[i % RING, t - 1], self.rsem, (i, t - 1), self.next)

    def l_copy(self, i, t):
        d = jnp.clip(t - self.pairs + self.z, 0, self.pairs - 1)
        return send(self.mine.at[i % HELD, d], self.left.at[i % RING, t - 1], self.lsem, (i, t - 1), self.last)

    def sends_right(self, t):
        return self.has_right & (t >= self.z + 1)

    def sends_left(self, t):
        return self.has_left & (t >= self.pairs - self.z)

    def credit(self, i, free, when):
        if i >= RING:

            @pl.when(when)
            def _():
                pl.semaphore_wait(free, 1)

    def release(self, i):
        helped = self.units[i].help is not None

        @pl.when(self.z == 0)
        def _():
            if i >= RING:
                pl.semaphore_wait(self.rfree, 1)
            if not helped:
                for t in range(1, self.pairs):
                    self.r_copy(i, t).start()

        @pl.when(self.z == self.pairs - 1)
        def _():
            if i >= RING:
                pl.semaphore_wait(self.lfree, 1)
            if not helped:
                for t in range(1, self.pairs):
                    self.l_copy(i, t).start()

        if helped:

            @pl.when(self.end)
            def _():
                for ship in self.units[i].help.ships:
                    ship.start()

    def assist(self, i):
        unit = self.units[i]
        g, rows = i % HELD, unit.count
        away = jnp.where(self.z == 1, 0, self.pairs - 1)

        @pl.when(self.inner)
        def _():
            for ship in unit.help.ships:
                ship.wait_recv()
            unit.help.arrive()
            copies = []
            for part in (0, 1):
                for k in range(self.pairs):
                    src = unit.help.rows[part].at[:, pl.ds(k * self.blk, self.blk)]
                    copies.append(pltpu.make_async_copy(src, self.fara.at[part, k], self.fasem.at[part, k]))
                copies.append(
                    pltpu.make_async_copy(unit.help.columns[part], self.farb.at[part], self.fbsem.at[part])
                )
            for copy in copies:
                copy.start()
            for copy in copies:
                copy.wait()

            def body(k, carry):
                @pl.when(k != away)
                def _():
                    total = self.mine[g, k].astype(F32)
                    for part in (0, 1):
                        total = total + lax.dot_general(
                            self.fara[part, k], self.farb[part], FIRST, preferred_element_type=F32
                        )
                    self.mine[g, k] = total.astype(LOW)

                return carry

            lax.fori_loop(0, self.pairs, body, 0)

    def step(self, i, t):
        g, r = i % HELD, i % RING
        first_right, first_left = t == self.z + 1, t == self.pairs - self.z
        helped = self.units[i].help is not None

        @pl.when(self.sends_right(t) & self.has_left)
        def _():
            self.credit(i, self.rfree, first_right)

            @pl.when(self.z > 1 if helped else self.z > 0)
            def _():
                self.r_copy(i, t - 1).wait_recv()
                d = jnp.clip(self.pairs - t + self.z, 0, self.pairs - 1)
                self.add(self.mine.at[g, d], self.right.at[r, t - 2])

            self.r_copy(i, t).start()

        @pl.when(self.sends_left(t) & self.has_right)
        def _():
            self.credit(i, self.lfree, first_left)

            @pl.when(self.z < self.pairs - 2 if helped else self.z < self.pairs - 1)
            def _():
                self.l_copy(i, t - 1).wait_recv()
                d = jnp.clip(t - self.pairs + self.z, 0, self.pairs - 1)
                self.add(self.mine.at[g, d], self.left.at[r, t - 2])

            self.l_copy(i, t).start()

    def out_copy(self, i):
        return pltpu.make_async_copy(self.stage.at[i % 2], self.units[i].out, self.osem.at[i % 2])

    def final(self, i):
        g, r, t = i % HELD, i % RING, self.pairs - 1
        helped = self.units[i].help is not None

        @pl.when(self.z > 1 if helped else self.z > 0)
        def _():
            self.r_copy(i, t).wait_recv()
            self.add(self.mine.at[g, self.z], self.right.at[r, t - 1])

        @pl.when(self.z < self.pairs - 2 if helped else self.z < self.pairs - 1)
        def _():
            self.l_copy(i, t).wait_recv()
            self.add(self.mine.at[g, self.z], self.left.at[r, t - 1])

        if i + RING < len(self.units):

            @pl.when(self.has_left)
            def _():
                pl.semaphore_signal(self.rfree, inc=1, device_id=self.last, device_id_type=MESH)

            @pl.when(self.has_right)
            def _():
                pl.semaphore_signal(self.lfree, inc=1, device_id=self.next, device_id_type=MESH)

        if i >= 2:
            self.out_copy(i - 2).wait()

        def step(s):
            self.stage[i % 2, s, :] = self.mine[g, self.z, s, :]

        each_slab(self.blk, step, 64)
        self.out_copy(i).start()

    def sent(self, i):
        helped = self.units[i].help is not None
        for t in range(1, self.pairs):

            @pl.when(self.sends_right(t) & self.has_left if helped else self.sends_right(t))
            def _():
                self.r_copy(i, t).wait_send()

            @pl.when(self.sends_left(t) & self.has_right if helped else self.sends_left(t))
            def _():
                self.l_copy(i, t).wait_send()

    def ask(self, i):
        if i < len(self.units) and not self.units[i].early and i not in self.asked:
            self.asked.add(i)
            self.trade(i).start()

    def move(self, k):
        count, pairs = len(self.units), self.pairs
        for t in range(pairs - 1, 2, -1):
            if 0 <= k - (t - 1) < count:
                self.step(k - (t - 1), t)
        if 0 <= k - (pairs - 1) < count:
            self.final(k - (pairs - 1))
        if 0 <= k - 1 < count:
            if self.units[k - 1].help is not None:
                self.assist(k - 1)
            self.step(k - 1, 2)

    def leave(self, i):
        if not self.units[i].early and i not in self.gone:
            self.gone.add(i)
            self.trade(i).wait_send()

    def multiply(self, i, loaded=False):
        if not loaded:
            self.load(i)
        self.compute(i)
        self.release(i)

    def drain(self):
        count = len(self.units)
        for i in range(max(0, count - 2), count):
            self.out_copy(i).wait()
        for i in range(max(0, count - HELD), count):
            self.sent(i)
        for i in range(count):
            self.leave(i)
            if self.units[i].help is not None:

                @pl.when(self.end)
                def _():
                    for ship in self.units[i].help.ships:
                        ship.wait_send()

                @pl.when(self.inner)
                def _():
                    self.units[i].help.leave()


VM = pl.BlockSpec(memory_space=pltpu.VMEM)
HB = pl.BlockSpec(memory_space=pl.ANY)


def norm_rows(rows):
    centre = jnp.mean(rows, axis=-1, keepdims=True)
    centred = rows - centre
    variance = jnp.mean(centred * centred, axis=-1, keepdims=True)
    inv_std = lax.rsqrt(variance + 1e-05)
    return centred * inv_std, inv_std


class Narrow:
    def __init__(self):
        self.me = lax.axis_index(NARROW)
        x, c = self.me // 2, self.me % 2
        self.core_at = x * 2 + 1 - c
        self.chip_at = (1 - x) * 2 + c
        self.far_at = (1 - x) * 2 + 1 - c
        self.core = {NARROW: self.core_at}
        self.chip = {NARROW: self.chip_at}

    def meet(self, barrier):
        greet(barrier, self.core)
        greet(barrier, self.chip)
        return 2


class Gather:
    def __init__(self, net, full, own, sems):
        self.net, self.full, self.own, self.sems = net, full, own, sems

    def place(self, b, who):
        at = (b * 4 + who) * self.own
        return self.full.at[pl.ds(pl.multiple_of(at, self.own), self.own), :]

    def mine(self, b):
        return self.place(b, self.net.me)

    def to_core(self, b):
        return send(self.mine(b), self.mine(b), self.sems, (b, 0), self.net.core)

    def to_chip(self, b):
        return send(self.mine(b), self.mine(b), self.sems, (b, 1), self.net.chip)

    def onward(self, b):
        block = self.place(b, self.net.chip_at)
        return send(block, block, self.sems, (b, 2), self.net.core)

    def start(self, b):
        self.to_chip(b).start()
        self.to_core(b).start()

    def forward(self, b):
        self.to_chip(b).wait_recv()
        self.onward(b).start()

    def finish(self, b):
        self.to_core(b).wait_recv()
        self.onward(b).wait_recv()
        self.to_core(b).wait_send()
        self.to_chip(b).wait_send()
        self.onward(b).wait_send()


class Scatter:
    def __init__(self, net, part, landed, outgoing, arrived, sems):
        self.net, self.part, self.landed = net, part, landed
        self.outgoing, self.arrived, self.sems = outgoing, arrived, sems
        self.own = part.shape[1] // 4

    def rows(self, b, who):
        return self.part.at[b, pl.ds(pl.multiple_of(who * self.own, self.own), self.own), :]

    def core_copy(self, b, k):
        who = self.net.far_at if k == 0 else self.net.core_at
        return send(self.rows(b, who), self.landed.at[b, k], self.sems, (b, k), self.net.core)

    def chip_copy(self, b):
        return send(self.outgoing.at[b], self.arrived.at[b], self.sems, (b, 2), self.net.chip)

    def start(self, b):
        self.core_copy(b, 0).start()
        self.core_copy(b, 1).start()

    def cross(self, b):
        self.core_copy(b, 0).wait_recv()
        mine = self.rows(b, self.net.chip_at)

        def step(s):
            total = mine[s, :] + self.landed[b, 0, s, :]
            self.outgoing[b, s, :] = total.astype(self.outgoing.dtype)

        each_slab(self.own, step)
        self.chip_copy(b).start()

    def ready(self, b):
        self.core_copy(b, 1).wait_recv()
        self.chip_copy(b).wait_recv()

    def total(self, b, s):
        near = self.rows(b, self.net.me)[s, :] + self.landed[b, 1, s, :]
        return near + self.arrived[b, s, :].astype(F32)

    def finish(self, b):
        self.core_copy(b, 0).wait_send()
        self.core_copy(b, 1).wait_send()
        self.chip_copy(b).wait_send()


class Halves:
    def __init__(self, net, full, there, pairs, sems, index):
        me = lax.axis_index(WIDE)
        y, rows = me % 2, full.shape[0] // 2
        blk = full.shape[1] // (2 * pairs)
        span = pl.ds(pl.multiple_of(net.me % 2 * rows, rows), rows)
        self.copies = [
            send(
                full.at[span, pl.ds(pl.multiple_of((2 * k + 1 - y) * blk, blk), blk)],
                there.at[span, pl.ds(k * blk, blk)], sems, (index, k), {WIDE: me + 1 - 2 * y},
            )
            for k in range(pairs)
        ]
        self.onward = send(there.at[span], there.at[span], sems, (index, pairs), net.core)

    def start(self):
        for copy in self.copies:
            copy.start()

    def forward(self):
        for copy in self.copies:
            copy.wait_recv()
        self.onward.start()

    def arrive(self):
        self.onward.wait_recv()

    def leave(self):
        for copy in self.copies:
            copy.wait_send()
        self.onward.wait_send()


class Help:
    def __init__(self, ships, rows, columns, onward=()):
        self.ships, self.rows, self.columns, self.onward = ships, rows, columns, onward

    def arrive(self):
        for copy in self.onward:
            copy.start()
        for copy in self.onward:
            copy.wait_recv()

    def leave(self):
        for copy in self.onward:
            copy.wait_send()


def scatter_scratch(images, own, width, hop=LOW):
    return [
        pltpu.VMEM((images, 4 * own, width), F32),
        pltpu.VMEM((images, 2, own, width), F32),
        pltpu.VMEM((images, own, width), hop),
        pltpu.VMEM((images, own, width), hop),
        pltpu.SemaphoreType.DMA((2, images, 3)),
    ]


def params(number, limit):
    return pltpu.CompilerParams(
        collective_id=number, has_side_effects=True, vmem_limit_bytes=limit * 1024 * 1024
    )


class Copies:
    def __init__(self, sems):
        self.sems, self.used, self.open = sems, 0, []

    def start(self, src, dst):
        copy = pltpu.make_async_copy(src, dst, self.sems.at[self.used])
        self.used += 1
        copy.start()
        return copy

    def later(self, src, dst):
        self.open.append(self.start(src, dst))

    def close(self):
        for copy in self.open:
            copy.wait()


def columns_of(width, step, tile=512):
    def body(j, carry):
        step(pl.ds(pl.multiple_of(j * tile, tile), tile))
        return carry

    lax.fori_loop(0, width // tile, body, 0)


def dot(left, right, dims=(((1,), (0,)), ((), ()))):
    return lax.dot_general(left, right, dims, preferred_element_type=F32)


def softmax_parts(q, k):
    scores = dot(q, k, LAST) * (1.0 / math.sqrt(HEAD))
    powers = jnp.exp(scores - jnp.max(scores, axis=-1, keepdims=True))
    return powers / jnp.sum(powers, axis=-1, keepdims=True)


def head_columns(j):
    return pl.ds(pl.multiple_of(j * HEAD, HEAD), HEAD)


def heads_forward(b, images, query, keys, values, out):
    many, some = query.shape[0] // images, keys.shape[0] // images
    asked, told = pl.ds(b * many, many), pl.ds(b * some, some)

    def body(j, carry):
        cols = head_columns(j)
        probs = softmax_parts(query[asked, cols], keys[told, cols])
        out[asked, cols] = dot(probs.astype(LOW), values[told, cols]).astype(LOW)
        return carry

    lax.fori_loop(0, query.shape[1] // HEAD, body, 0)


def heads_back(images, query, keys, values, d_att):
    heads = query.shape[1] // HEAD
    many, some = query.shape[0] // images, keys.shape[0] // images
    scale = 1.0 / math.sqrt(HEAD)

    def body(j, carry):
        b = j // heads
        cols = head_columns(j % heads)
        asked = pl.ds(pl.multiple_of(b * many, many), many)
        told = pl.ds(pl.multiple_of(b * some, some), some)
        q, k, v, d = query[asked, cols], keys[told, cols], values[told, cols], d_att[asked, cols]
        probs = softmax_parts(q, k)
        d_probs = dot(d, v, LAST)
        weighted = jnp.sum(probs * d_probs, axis=-1, keepdims=True)
        d_scores = (probs * (d_probs - weighted)).astype(LOW)
        values[told, cols] = dot(probs.astype(LOW), d, FIRST).astype(LOW)
        keys[told, cols] = (dot(d_scores, q, FIRST) * scale).astype(LOW)
        query[asked, cols] = (dot(d_scores, k) * scale).astype(LOW)
        return carry

    lax.fori_loop(0, images * heads, body, 0)


def gelu(u):
    turn = jnp.tanh(math.sqrt(2.0 / math.pi) * (u + 0.044715 * (u * u * u)))
    return 0.5 * u * (1.0 + turn)


def gelu_slope(u):
    c = math.sqrt(2.0 / math.pi)
    turn = jnp.tanh(c * (u + 0.044715 * (u * u * u)))
    return 0.5 * (1.0 + turn) + 0.5 * u * (1.0 - turn * turn) * (c * (1.0 + 0.134145 * (u * u)))


def flat(array):
    return array.reshape(array.shape[0] * array.shape[1], array.shape[2])


def forward_all(pairs, number, given):
    t = given
    images, own, width = t.tokens.shape
    length, words = 4 * own, t.caption.shape[1]
    inner, ff, states = t.query_self.shape[1], t.up_proj.shape[1], t.caption.shape[2]
    rows, word_rows, word_own = images * length, images * words, words // 4
    chunks, text_chunks = ff // inner, states // inner
    half = width // 2
    vars_in = dict(
        tokens=t.tokens, caption=flat(t.caption), cotangent=t.cotangent, text_proj=t.text_proj,
        query_self=t.query_self, key_self=t.key_self, value_self=t.value_self, out_self=t.out_self,
        query_cross=t.query_cross, key_cross=t.key_cross, value_cross=t.value_cross,
        out_cross=t.out_cross, up_proj=t.up_proj,
    )
    sds = jax.ShapeDtypeStruct
    outs = dict(
        image_self=sds((rows, width), LOW), image_cross=sds((rows, width), LOW),
        image_feed=sds((rows, width), LOW), d_image=sds((rows, width), LOW),
        context=sds((word_rows, width), LOW),
        query_sa=sds((rows, inner), LOW), keys_sa=sds((rows, inner), LOW), values_sa=sds((rows, inner), LOW),
        query_ca=sds((rows, inner), LOW), keys_ca=sds((word_rows, inner), LOW), values_ca=sds((word_rows, inner), LOW),
        attended_sa=sds((rows, inner), LOW), attended_ca=sds((rows, inner), LOW),
        resid_mid=sds((images, own, width), F32), resid_late=sds((images, own, width), F32),
        activ=sds((rows, ff), LOW), pre_act=sds((images, length, ff), F32),
        nb_self=sds((rows, half), LOW), nb_low=sds((rows, half), LOW),
        nb_context=sds((word_rows, half), LOW), nb_first=sds((rows, inner), LOW), nb_caption=sds((word_rows, states), LOW),
        far_caption=sds((2, word_rows, states), LOW), far_context=sds((2, word_rows, half), LOW),
        nb_att_sa=sds((rows, inner), LOW), nb_att_ca=sds((rows, inner), LOW),
    )

    def kernel(*refs):
        h = types.SimpleNamespace(**dict(zip(vars_in, refs)))
        refs = refs[len(vars_in):]
        marks, gain_self, gain_cross, gain_feed = refs[:4]
        refs = refs[4:]
        o = types.SimpleNamespace(**dict(zip(outs, refs)))
        refs = refs[len(outs):]
        scatter_refs, text_refs = refs[:5], refs[5:10]
        (full_s, full_c, full_f, full_d, full_x, gsem_s, gsem_c, gsem_f, gsem_d, gsem_x,
         wn, wt, tok, cot, cap, sq, sk, sv, xq, xk, xv, att_s, att_c, mid, late, act,
         fsem, osem, hsem, asem, zsem) = refs[10:]
        net = Narrow()
        fetch, store = Copies(fsem), Copies(osem)
        barrier = pltpu.get_barrier_semaphore()
        me = lax.axis_index(WIDE)
        pair = {WIDE: me + 1 - 2 * (me % 2)}
        greet(barrier, pair)
        z, y = me // 2, me % 2
        beside = {WIDE: (z + 1 - 2 * (z % 2)) * 2 + y}
        greet(barrier, beside)
        others = net.meet(barrier) + 2
        end = (z == 0) | (z == pairs - 1)
        blk = width // (2 * pairs)
        ships = [
            send(cap, o.far_caption.at[0], zsem, (0,), beside),
            send(o.nb_caption, o.far_caption.at[1], zsem, (1,), beside),
            send(o.nb_context, o.far_context.at[1], zsem, (2,), beside),
        ] + [
            send(
                full_x.at[:, pl.ds(pl.multiple_of((2 * k + y) * blk, blk), blk)],
                o.far_context.at[0, :, pl.ds(k * blk, blk)], zsem, (3 + k,), beside,
            )
            for k in range(pairs)
        ]

        def whole(j, ref):
            return fetch.start(ref, wn.at[j])

        def band(j, ref, c):
            return fetch.start(ref.at[pl.ds(c * inner, inner)], wt.at[j])

        need_tok = fetch.start(h.tokens, tok)
        need_cap = fetch.start(h.caption, cap)
        need_proj = [band(c, h.text_proj, c) for c in range(text_chunks)]
        need_cot = fetch.start(h.cotangent, cot)
        need_qkv = [whole(j, ref) for j, ref in enumerate((h.query_self, h.key_self, h.value_self))]
        need_out_self = fetch.start(h.out_self, wt.at[2])
        need_kv = [whole(4, h.key_cross), whole(5, h.value_cross)]
        need_query_cross = whole(3, h.query_cross)
        need_out_cross = fetch.start(h.out_cross, wt.at[3])
        need_up = {3: fetch.start(h.up_proj.at[:, pl.ds(3 * inner, inner)], wn.at[6])}
        gather_s = Gather(net, full_s, own, gsem_s)
        gather_c = Gather(net, full_c, own, gsem_c)
        gather_f = Gather(net, full_f, own, gsem_f)
        gather_d = Gather(net, full_d, own, gsem_d)
        gather_x = Gather(net, full_x, word_own, gsem_x)
        scatter, text = Scatter(net, *scatter_refs), Scatter(net, *text_refs)
        part = scatter.part

        def of(b, n=length):
            return pl.ds(b * n, n)

        need_tok.wait()
        pl.semaphore_wait(barrier, others)
        for b in range(images):
            mine = gather_s.mine(b)

            def step(s, b=b, mine=mine):
                normed, _ = norm_rows(tok[b, s, :].astype(F32))
                mine[s, :] = (normed * gain_self[...].astype(F32)[None]).astype(LOW)

            each_slab(own, step)
            gather_s.start(b)
        need_cap.wait()
        first = [send(cap, o.nb_caption, asem, (images,), pair)]
        first[0].start()

        @pl.when(end)
        def _():
            ships[0].start()

        for need in need_proj:
            need.wait()
        for b in range(images):

            def step(cols, b=b):
                total = None
                for c in range(text_chunks):
                    term = dot(cap[of(b, words), pl.ds(c * inner, inner)], wt[c, :, cols])
                    total = term if total is None else total + term
                text.part[b, :, cols] = total

            columns_of(width, step)
            text.start(b)
        need_cot.wait()
        for b in range(images):
            mine = gather_d.mine(b)

            def step(s, b=b, mine=mine):
                mine[s, :] = (cot[b, s, :].astype(F32) * marks[b, s, :]).astype(LOW)

            each_slab(own, step)

        def project(b, source, weights, targets, n=length):
            for j, target in zip(weights, targets):
                target[of(b, n), :] = dot(source[of(b, n), :], wn[j]).astype(LOW)

        def back_out(b, attended, j):
            def step(cols):
                part[b, :, cols] = dot(attended[of(b), :], wt[j, :, cols])

            columns_of(width, step)
            scatter.start(b)

        gather_s.forward(0)
        text.cross(0)
        text.cross(1)
        gather_d.start(0)
        for b in range(images):
            gather_s.finish(b)
            if b == 0:
                for need in need_qkv:
                    need.wait()
            project(b, full_s, (0, 1, 2), (sq, sk, sv))
            if b + 1 < images:
                gather_s.forward(b + 1)
            heads_forward(b, images, sq, sk, sv, att_s)
            if b == 0:
                need_out_self.wait()
            back_out(b, att_s, 2)
            if b == 0:
                scatter.cross(b)
        store.later(full_s, o.image_self)
        for ref, out in ((sq, o.query_sa), (sk, o.keys_sa), (sv, o.values_sa), (att_s, o.attended_sa)):
            store.later(ref, out)
        for c in range(3):
            need_up[c] = fetch.start(h.up_proj.at[:, pl.ds(c * inner, inner)], wn.at[c])
        for b in range(images):
            text.ready(b)
            mine = gather_x.mine(b)

            def step(s, b=b, mine=mine):
                mine[s, :] = text.total(b, s).astype(LOW)

            each_slab(word_own, step)
        scatter.cross(1)
        for b in range(images):
            gather_x.start(b)
        halves_self = Halves(net, full_s, o.nb_self, pairs, hsem, 0)
        halves_self.start()
        first.append(send(att_s, o.nb_att_sa, asem, (images + 1,), pair))
        first[-1].start()

        def rows_out(b, source, target, gain, gather):
            scatter.ready(b)
            mine = gather.mine(b)

            def step(s):
                kept = source[b, s, :].astype(F32) + scatter.total(b, s)
                target[b, s, :] = kept
                normed, _ = norm_rows(kept)
                mine[s, :] = (normed * gain[...].astype(F32)[None]).astype(LOW)

            each_slab(own, step)
            gather.start(b)

        rows_out(0, tok, mid, gain_cross, gather_c)
        gather_d.start(1)
        for b in range(images):
            gather_x.forward(b)
        rows_out(1, tok, mid, gain_cross, gather_c)
        store.later(mid, o.resid_mid)
        for need in need_kv:
            need.wait()
        for b in range(images):
            gather_x.finish(b)
            project(b, full_x, (4, 5), (xk, xv), words)
            text.finish(b)
        halves_context = Halves(net, full_x, o.nb_context, pairs, hsem, 1)
        halves_context.start()
        first[0].wait_recv()

        @pl.when(end)
        def _():
            for ship in ships[3:]:
                ship.start()
            ships[1].start()

        store.later(full_x, o.context)
        store.later(xk, o.keys_ca)
        store.later(xv, o.values_ca)
        need_query_cross.wait()
        gather_c.forward(0)
        for b in range(images):
            gather_c.finish(b)
            project(b, full_c, (3,), (xq,))
            if b + 1 < images:
                gather_c.forward(b + 1)
            heads_forward(b, images, xq, xk, xv, att_c)
            scatter.finish(b)
            if b == 0:
                need_out_cross.wait()
            back_out(b, att_c, 3)
            if b == 0:
                for j in range(images):
                    gather_d.forward(j)
                scatter.cross(b)
                for j in range(images):
                    gather_d.finish(j)
                halves_low = Halves(net, full_d, o.nb_low, pairs, hsem, 2)
                halves_low.start()
                store.later(full_d, o.d_image)
        first.append(send(att_c, o.nb_att_ca, asem, (images + 2,), pair))
        first[-1].start()
        store.later(full_c, o.image_cross)
        store.later(xq, o.query_ca)
        store.later(att_c, o.attended_ca)
        scatter.cross(1)
        halves_self.forward()
        halves_context.forward()
        rows_out(0, mid, late, gain_feed, gather_f)
        rows_out(1, mid, late, gain_feed, gather_f)
        store.later(late, o.resid_late)
        halves_low.forward()
        halves_context.arrive()

        @pl.when(end)
        def _():
            ships[2].start()

        first += [
            send(act.at[of(b), pl.ds(0, inner)], o.nb_first.at[of(b)], asem, (b,), pair) for b in range(images)
        ]
        gather_f.forward(0)
        for b in range(images):
            gather_f.finish(b)
            scatter.finish(b)
            for c in range(chunks):
                if b == 0:
                    need_up[c].wait()
                cols = pl.ds(c * inner, inner)
                part[b, :, cols] = dot(full_f[of(b), :], wn[6 if c == 3 else c])
                if b == 0 and c == 1:
                    gather_f.forward(1)

                def step(s, b=b, cols=cols):
                    act[pl.ds(pl.multiple_of(b * length + s.start, 16), 16), cols] = gelu(part[b, s, cols]).astype(LOW)

                each_slab(length, step)
                if c == 0:
                    first[3 + b].start()
        store.later(act, o.activ)
        store.later(part, o.pre_act)
        store.later(full_f, o.image_feed)
        for halves in (halves_self, halves_context, halves_low):
            if halves is not halves_context:
                halves.arrive()
            halves.leave()
        first[0].wait_send()
        for copy in first[1:]:
            copy.wait()

        @pl.when(end)
        def _():
            for ship in ships:
                ship.wait_send()

        @pl.when(jnp.logical_not(end))
        def _():
            for ship in ships:
                ship.wait_recv()

        store.close()

    V, DS = pltpu.VMEM, pltpu.SemaphoreType.DMA
    gsem = DS((2, images, 3))
    scratch = scatter_scratch(images, own, width) + scatter_scratch(images, word_own, width, F32)
    scratch += [V((rows, width), LOW)] * 4 + [V((word_rows, width), LOW)] + [gsem] * 5
    scratch += [
        V((7, width, inner), LOW), V((4, inner, width), LOW),
        V((images, own, width), LOW), V((images, own, width), LOW), V((word_rows, states), LOW),
        V((rows, inner), LOW), V((rows, inner), LOW), V((rows, inner), LOW),
        V((rows, inner), LOW), V((word_rows, inner), LOW), V((word_rows, inner), LOW),
        V((rows, inner), LOW), V((rows, inner), LOW),
        V((images, own, width), F32), V((images, own, width), F32), V((rows, ff), LOW),
        DS((40,)), DS((40,)), DS((2, 3, pairs + 1)), DS((2, images + 3)), DS((2, pairs + 3)),
    ]
    result = pl.pallas_call(
        kernel,
        out_shape=list(outs.values()),
        in_specs=[HB] * len(vars_in) + [VM] * 4,
        out_specs=[HB] * len(outs),
        scratch_shapes=scratch,
        compiler_params=params(number, 62),
        name="forward_all",
    )(*vars_in.values(), t.marks, *t.gains)
    return types.SimpleNamespace(**dict(zip(outs, result)))


def backward_all(pairs, number, given, kept):
    t = given
    images, own, width = t.tokens.shape
    length, words = 4 * own, t.caption.shape[1]
    inner, ff, states = t.query_self.shape[1], t.up_proj.shape[1], t.caption.shape[2]
    rows, word_rows, word_own = images * length, images * words, words // 4
    chunks, text_chunks = ff // inner, states // inner
    half, blk = width // 2, width // (2 * pairs)
    count = 2 * chunks + text_chunks + 8
    vars_in = dict(
        vars(kept),
        tokens=t.tokens, caption=flat(t.caption), cotangent=t.cotangent, text_proj=t.text_proj,
        query_self=t.query_self, key_self=t.key_self, value_self=t.value_self, out_self=t.out_self,
        query_cross=t.query_cross, key_cross=t.key_cross, value_cross=t.value_cross,
        out_cross=t.out_cross, up_proj=t.up_proj, down_proj=t.down_proj,
    )

    def kernel(*refs):
        h = types.SimpleNamespace(**dict(zip(vars_in, refs)))
        refs = refs[len(vars_in):]
        marks, gain_self, gain_cross, gain_feed = refs[:4]
        grads_out, words_out, tokens_out, layer_out, gain_out, nb_cols, nb_feed, nb_cross, nb_late, nb_mid, nb_words, far_cols, far_words = refs[4:17]
        refs = refs[17:]
        scatter_refs = refs[:5]
        (full_c, full_s, full_x, gsem_c, gsem_s, gsem_x, text_sem,
         big, d_att, wa, wb, xq, xk, xv, sq, sk, sv, cot, late, mid, tok, low_rows, word_grad,
         fsem, osem, nbsem, hsem, gacc, gland, gsems, zsem, wordsem) = refs[5:37]
        net = Narrow()
        units = []

        def unit(rows_ref, nb_rows, columns, size, halves=None, early=None, help=None):
            i = len(units)
            there = nb_cols.at[i, pl.ds(0, size)] if early is None else early
            units.append(types.SimpleNamespace(
                rows=rows_ref, nb_rows=nb_rows, columns=columns, count=size, halves=halves,
                nb_columns=there, sems=nbsem, out=grads_out.at[i], early=early is not None, help=help,
            ))

        def chunk(ref, c):
            return ref.at[:, pl.ds(c * inner, inner)]

        halves_feed = Halves(net, h.image_feed, nb_feed, pairs, hsem, 0)
        halves_cross = Halves(net, h.image_cross, nb_cross, pairs, hsem, 1)
        halves_late = Halves(net, full_c, nb_late, pairs, hsem, 2)
        halves_mid = Halves(net, full_s, nb_mid, pairs, hsem, 3)
        halves_words = Halves(net, full_x, nb_words, pairs, hsem, 4)
        for c in range(chunks):
            unit(h.d_image, h.nb_low, chunk(h.activ, c), rows, None, h.nb_first if c == 0 else None)
        for c in range(chunks):
            unit(h.image_feed, nb_feed, chunk(big, c), rows, halves_feed)
        unit(full_c, nb_late, h.attended_ca, rows, halves_late, h.nb_att_ca)
        me = lax.axis_index(WIDE)
        z, y = me // 2, me % 2
        beside = {WIDE: (z + 1 - 2 * (z % 2)) * 2 + y}
        far_rows = (h.far_context.at[0], h.far_context.at[1])
        for j, column in enumerate((xk, xv)):
            theirs = nb_cols.at[len(units), pl.ds(0, word_rows)]
            ships = [
                send(src, far_cols.at[j, part], zsem, (2 * j + part,), beside) for part, src in enumerate((column, theirs))
            ]
            help = Help(ships, far_rows, (far_cols.at[j, 0], far_cols.at[j, 1]))
            unit(h.context, h.nb_context, column, word_rows, None, None, help)
        unit(h.image_cross, nb_cross, xq, rows, halves_cross)
        part_rows = word_rows // 2
        span = pl.ds(pl.multiple_of(net.me % 2 * part_rows, part_rows), part_rows)
        ships = [send(nb_words.at[span], far_words.at[1, span], zsem, (4,), beside)] + [
            send(
                full_x.at[span, pl.ds(pl.multiple_of((2 * k + y) * blk, blk), blk)],
                far_words.at[0, span, pl.ds(k * blk, blk)], zsem, (5 + k,), beside,
            )
            for k in range(pairs)
        ]
        onward = [send(far_words.at[j, span], far_words.at[j, span], wordsem, (j,), net.core) for j in range(2)]
        for c in range(text_chunks):
            help = Help(
                ships if c == 0 else [], (far_words.at[0], far_words.at[1]),
                (chunk(h.far_caption.at[0], c), chunk(h.far_caption.at[1], c)), onward if c == 0 else [],
            )
            unit(full_x, nb_words, chunk(h.caption, c), word_rows, halves_words, chunk(h.nb_caption, c), help)
        unit(full_s, nb_mid, h.attended_sa, rows, halves_mid, h.nb_att_sa)
        for column in (sq, sk, sv):
            unit(h.image_self, h.nb_self, column, rows)
        wide = Wide(pairs, units, refs[37:])
        fetch, store = Copies(fsem), Copies(osem)

        def of(b, n=length):
            return pl.ds(b * n, n)

        barrier = pltpu.get_barrier_semaphore()
        far = {WIDE: (wide.z + 2) % pairs * 2 + wide.y}
        near = {WIDE: (wide.z + 1 - 2 * (wide.z % 2)) * 2 + wide.y}
        greet(barrier, far)
        others = wide.meet(barrier) + net.meet(barrier) + 1

        def up_chunk(c):
            return fetch.start(chunk(h.up_proj, c), wa.at[c % 2])

        wide.load(0)
        need_image = fetch.start(h.d_image, full_s)

        def down_chunk(c):
            return fetch.start(h.down_proj.at[pl.ds(c * inner, inner)], wb.at[c % 2])

        need_down = {c: down_chunk(c) for c in range(2)}
        need_pre = fetch.start(h.pre_act, scatter_refs[0])
        need_up = {c: up_chunk(c) for c in range(2)}
        need_cot = fetch.start(h.cotangent, cot)
        need_late = fetch.start(h.resid_late, late)
        need_ca = [fetch.start(a, b) for a, b in ((h.query_ca, xq), (h.keys_ca, xk), (h.values_ca, xv))]
        need_mid = fetch.start(h.resid_mid, mid)
        need_sa = [fetch.start(a, b) for a, b in ((h.query_sa, sq), (h.keys_sa, sk), (h.values_sa, sv))]
        need_tok = fetch.start(h.tokens, tok)
        wide.compute(0)
        pl.semaphore_wait(barrier, others)
        wide.release(0)
        wide.ask(1)
        wide.ask(2)
        scatter = Scatter(net, *scatter_refs)
        part = scatter.part
        gather_c, gather_s = Gather(net, full_c, own, gsem_c), Gather(net, full_s, own, gsem_s)
        gather_x = Gather(net, full_x, word_own, gsem_x)

        need_image.wait()
        need_pre.wait()
        for c in range(chunks):
            need_down[c].wait()
            cols = pl.ds(c * inner, inner)
            for b in range(images):
                slope = dot(full_s[of(b), :], wb[c % 2], LAST)
                big[of(b), cols] = (gelu_slope(part[b, :, cols]) * slope).astype(LOW)
            if c + 2 < chunks:
                need_down[c + 2] = down_chunk(c + 2)
            if c == 1:
                wide.ask(3)
                halves_feed.start()
        need_out = fetch.start(h.out_cross, wb.at[0])
        need_out_self = fetch.start(h.out_self, wb.at[1])
        wide.multiply(1)
        wide.ask(4)
        wide.move(1)
        for c in range(chunks):
            need_up[c].wait()
            for b in range(images):

                def step(cols, b=b, c=c):
                    term = dot(big[of(b), pl.ds(c * inner, inner)], wa[c % 2, cols, :], LAST)
                    part[b, :, cols] = term if c == 0 else part[b, :, cols] + term

                columns_of(width, step)
                if c == chunks - 1:
                    scatter.start(b)
            if c + 2 < chunks:
                need_up[c + 2] = up_chunk(c + 2)
        need_query = fetch.start(h.query_cross, wa.at[0])
        need_key = fetch.start(h.key_cross, wa.at[1])
        gacc[...] = jnp.zeros_like(gacc)

        def back_rows(b, above, mask, source, gain, slot, keep, mine):
            scatter.ready(b)

            def step(s):
                d_hidden = scatter.total(b, s)
                normed, inv_std = norm_rows(source[b, s, :].astype(F32))
                gacc[slot : slot + 1, :] += jnp.sum(d_hidden * normed, axis=0, keepdims=True)
                top = above[b, s, :].astype(F32)
                if mask is not None:
                    top = top * mask[b, s, :]
                scaled = d_hidden * gain[...].astype(F32)[None]
                inside = scaled - jnp.mean(scaled, axis=-1, keepdims=True)
                inside = inside - normed * jnp.mean(scaled * normed, axis=-1, keepdims=True)
                d_rows = top + inv_std * inside
                if keep is not None:
                    keep[b, s, :] = d_rows
                mine[s, :] = d_rows.astype(LOW)

            each_slab(own, step)

        def multiply(b, target, lefts, rights, n=length):
            def step(cols):
                total = None
                for left, j in zip(lefts, rights):
                    term = dot(left[of(b, n), :], wa[j, cols, :], LAST)
                    total = term if total is None else total + term
                target[b, :, cols] = total

            columns_of(width, step)

        def out_back(b, full, j):
            d_att[of(b), :] = dot(full[of(b), :], wb[j], LAST).astype(LOW)

        wide.multiply(2)
        wide.ask(5)
        wide.move(2)
        for b in range(images):
            scatter.cross(b)
        wide.multiply(3)
        wide.ask(6)
        need_cot.wait()
        need_late.wait()
        for b in range(images):
            back_rows(b, cot, marks, late, gain_feed, 2, late, gather_c.mine(b))
            gather_c.start(b)
        wide.move(3)
        halves_feed.forward()
        for b in range(images):
            gather_c.forward(b)
        wide.multiply(4)
        wide.ask(7)
        need_out.wait()
        for b in range(images):
            scatter.finish(b)
            gather_c.finish(b)
            out_back(b, full_c, 0)
        halves_late.start()
        need_text = fetch.start(h.text_proj.at[pl.ds(0, inner)], wb.at[0])
        wide.move(4)
        wide.multiply(5)
        for need in need_ca:
            need.wait()
        heads_back(images, xq, xk, xv, d_att)
        wide.ask(9)
        wide.ask(10)
        halves_cross.start()
        need_query.wait()
        for b in range(images):
            multiply(b, part, [xq], [0])
            scatter.start(b)
        need_value = fetch.start(h.value_cross, wa.at[0])
        wide.multiply(6)
        wide.ask(11)
        for b in range(images):
            scatter.cross(b)
        wide.move(5)
        need_mid.wait()
        for b in range(images):
            back_rows(b, late, None, mid, gain_cross, 1, mid, gather_s.mine(b))
            gather_s.start(b)
        need_again = fetch.start(h.resid_late, late)
        wide.multiply(7)
        halves_late.forward()
        wide.move(6)
        for b in range(images):
            gather_s.forward(b)
        wide.multiply(8)
        for b in range(images):
            scatter.finish(b)
            gather_s.finish(b)
        halves_mid.start()
        text = Scatter(
            net, part.at[:, pl.ds(0, words)], scatter.landed.at[:, :, pl.ds(0, word_own)],
            scatter.outgoing.at[:, pl.ds(0, word_own)], scatter.arrived.at[:, pl.ds(0, word_own)], text_sem,
        )
        need_key.wait()
        need_value.wait()
        for b in range(images):
            multiply(b, text.part, [xk, xv], [1, 0], words)
            text.start(b)
        need_qkv = [fetch.start(h.query_self, wa.at[0]), fetch.start(h.key_self, wa.at[1])]
        need_out_self.wait()
        for b in range(images):
            out_back(b, full_s, 1)
        need_second = fetch.start(h.text_proj.at[pl.ds(inner, inner)], wb.at[1])
        wide.move(7)
        for b in range(images):
            text.cross(b)
        wide.multiply(9)
        for need in need_sa:
            need.wait()
        heads_back(images, sq, sk, sv, d_att)
        for b in range(images):
            text.ready(b)
            mine = gather_x.mine(b)

            def step(s, b=b, mine=mine):
                mine[s, :] = text.total(b, s).astype(LOW)

            each_slab(word_own, step)
            gather_x.start(b)
        wide.multiply(10)
        halves_cross.forward()
        wide.move(8)
        for b in range(images):
            gather_x.forward(b)
        for b in range(images):
            text.finish(b)
            gather_x.finish(b)
        halves_words.start()
        for c, need in enumerate((need_text, need_second)):
            need.wait()
            word_grad[:, pl.ds(c * inner, inner)] = dot(full_x[...], wb[c], LAST).astype(LOW)
        store.later(word_grad, words_out)
        need_down = {c: down_chunk(c) for c in range(2)}
        for need in need_qkv:
            need.wait()
        for b in range(images):
            multiply(b, part, [sq, sk], [0, 1])
        need_value = fetch.start(h.value_self, wa.at[0])
        wide.multiply(11)
        for c in range(chunks):
            wide.leave(chunks + c)
        need_act = fetch.start(h.activ, big)
        wide.move(9)
        need_value.wait()
        for b in range(images):

            def step(cols, b=b):
                part[b, :, cols] += dot(sv[of(b), :], wa[0, cols, :], LAST)

            columns_of(width, step)
            scatter.start(b)
        halves_words.forward()
        wide.multiply(12)
        for b in range(images):
            scatter.cross(b)
        wide.move(10)
        need_tok.wait()
        for b in range(images):
            back_rows(b, mid, None, tok, gain_self, 0, None, low_rows.at[b])
        store.later(low_rows, tokens_out)
        for b in range(images):
            scatter.finish(b)
        wide.ask(15)
        halves_mid.forward()
        wide.multiply(13)
        wide.move(11)
        trips = [
            send(gacc, gland.at[j], gsems, (j,), peer)
            for j, peer in enumerate((net.core, net.chip, wide.peer, near, far))
        ]

        def trip(j):
            if j > 0:
                trips[j - 1].wait()
                gacc[...] = gacc[...] + gland[j - 1]
            if j < len(trips):
                trips[j].start()

        def forward_chunk(c):
            need_down[c].wait()
            for b in range(images):

                def step(cols, b=b):
                    term = dot(big[of(b), pl.ds(c * inner, inner)], wb[c % 2, :, cols])
                    part[b, :, cols] = term if c == 0 else part[b, :, cols] + term

                columns_of(width, step)
            if c + 2 < chunks:
                need_down[c + 2] = down_chunk(c + 2)

        trip(0)
        wide.multiply(14)
        wide.ask(16)
        trip(1)
        wide.move(12)
        trip(2)
        wide.multiply(15)
        wide.ask(17)
        trip(3)
        wide.move(13)
        wide.multiply(16)
        need_act.wait()
        forward_chunk(0)
        wide.move(14)
        forward_chunk(1)
        wide.multiply(17)
        wide.move(15)
        for c in range(2, chunks):
            forward_chunk(c)
        for b in range(images):
            scatter.start(b)
        wide.move(16)
        for b in range(images):
            scatter.cross(b)
        trip(4)
        wide.move(17)
        need_again.wait()
        for b in range(images):
            scatter.ready(b)

            def step(s, b=b):
                tok[b, s, :] = (late[b, s, :] + scatter.total(b, s)).astype(LOW)

            each_slab(own, step)
            scatter.finish(b)
        store.later(tok, layer_out)
        for k in range(18, count + pairs - 1):
            wide.move(k)
        trip(5)
        store.later(gacc, gain_out)
        wide.drain()
        for halves in (halves_feed, halves_cross, halves_late, halves_mid, halves_words):
            halves.leave()
        store.close()

    V, DS = pltpu.VMEM, pltpu.SemaphoreType.DMA
    gsem = DS((2, images, 3))
    scratch = scatter_scratch(images, own, width)
    scratch += [V((rows, width), LOW), V((rows, width), LOW), V((word_rows, width), LOW)] + [gsem] * 4
    scratch += [
        V((rows, ff), LOW), V((rows, inner), LOW), V((2, width, inner), LOW), V((2, inner, width), LOW),
        V((rows, inner), LOW), V((word_rows, inner), LOW), V((word_rows, inner), LOW),
        V((rows, inner), LOW), V((rows, inner), LOW), V((rows, inner), LOW),
        V((images, own, width), LOW), V((images, own, width), F32), V((images, own, width), F32),
        V((images, own, width), LOW), V((images, own, width), LOW), V((word_rows, states), LOW),
        DS((48,)), DS((8,)), DS((2, count)), DS((2, 5, pairs + 1)), V((8, width), F32), V((5, 8, width), F32), DS((2, 5)), DS((2, 5 + pairs)), DS((2, 2)),
    ]
    scratch += [
        V((HELD, pairs, blk, inner), LOW),
        V((RING, pairs - 1, blk, inner), LOW), V((RING, pairs - 1, blk, inner), LOW), V((2, blk, inner), LOW),
        V((2, 2, pairs, rows, blk), LOW), V((2, 2, rows, inner), LOW),
        DS((2, count, pairs - 1)), DS((2, count, pairs - 1)),
        DS((2, 2, pairs)), DS((2, 2)), DS((2,)),
        pltpu.SemaphoreType.REGULAR, pltpu.SemaphoreType.REGULAR,
        V((2, pairs, word_rows, blk), LOW), V((2, word_rows, inner), LOW), DS((2, pairs)), DS((2,)),
    ]
    sds = jax.ShapeDtypeStruct
    result = pl.pallas_call(
        kernel,
        out_shape=[
            sds((count, blk, inner), LOW), sds((word_rows, states), LOW), sds((images, own, width), LOW),
            sds((images, own, width), LOW), sds((8, width), F32), sds((count, rows, inner), LOW), sds((rows, half), LOW),
            sds((rows, half), LOW), sds((rows, half), LOW), sds((rows, half), LOW), sds((word_rows, half), LOW),
            sds((2, 2, word_rows, inner), LOW), sds((2, word_rows, half), LOW),
        ],
        in_specs=[HB] * len(vars_in) + [VM] * 4,
        out_specs=[HB] * 13,
        scratch_shapes=scratch,
        compiler_params=params(number, 62),
        name="backward_all",
    )(*vars_in.values(), t.marks, *t.gains)
    return result[:5]


def spread(blocks, places, shapes, whole, gains):
    count, blk, inner = blocks.shape
    more = len(whole)

    def kernel(*refs):
        blocks_ref, whole_in, gains_ref, refs = refs[0], refs[1 : 1 + more], refs[1 + more], refs[2 + more :]
        outs, whole_out, refs = refs[: len(shapes)], refs[len(shapes) : len(shapes) + more], refs[len(shapes) + more :]
        gains_out, refs = refs[:3], refs[3:]
        for j, row in enumerate(gains_out):
            row[...] = gains_ref[j, :]
        held, flat_stage, turned_stage, isem, osem, wsem, *kept = refs
        ins = [pltpu.make_async_copy(blocks_ref.at[i], held.at[i], isem.at[i]) for i in range(count)]
        for copy in ins:
            copy.start()
        done, plain, turns = [], 0, 0
        came = [pltpu.make_async_copy(whole_in[j], kept[j], wsem.at[0, j]) for j in range(more)]
        for copy in came:
            copy.start()
        for i, (which, row, col, turned) in enumerate(places):
            ins[i].wait()
            if turned:
                stage = turned_stage.at[turns]
                turns += 1
                for j in range(0, inner, 128):
                    stage[pl.ds(j, 128), :] = held[i, :, pl.ds(j, 128)].astype(F32).T
                place = outs[which].at[pl.ds(row, inner), pl.ds(col, blk)]
            else:
                stage = flat_stage.at[plain]
                plain += 1
                stage[...] = held[i].astype(F32)
                place = outs[which].at[pl.ds(row, blk), pl.ds(col, inner)]
            done.append(pltpu.make_async_copy(stage, place, osem.at[i]))
            done[-1].start()
        for j in range(more):
            came[j].wait()
            done.append(pltpu.make_async_copy(kept[j], whole_out[j], wsem.at[1, j]))
            done[-1].start()
        for copy in done:
            copy.wait()

    turns = sum(1 for place in places if place[3])
    V, DS = pltpu.VMEM, pltpu.SemaphoreType.DMA
    return pl.pallas_call(
        kernel,
        out_shape=[jax.ShapeDtypeStruct(shape, F32) for shape in shapes]
        + [jax.ShapeDtypeStruct(array.shape, array.dtype) for array in whole]
        + [jax.ShapeDtypeStruct(gains.shape[1:], F32)] * 3,
        in_specs=[HB] * (1 + more) + [VM],
        out_specs=[HB] * (len(shapes) + more) + [VM] * 3,
        scratch_shapes=[
            V((count, blk, inner), LOW), V((count - turns, blk, inner), F32), V((turns, inner, blk), F32),
            DS((count,)), DS((count,)), DS((2, more)),
        ] + [V(array.shape, array.dtype) for array in whole],
        compiler_params=pltpu.CompilerParams(vmem_limit_bytes=62 * 1024 * 1024),
        name="spread",
    )(blocks, *whole, gains)


def by_kernels(
    tokens, caption, token_mask, cotangent, gain_self, gain_cross, gain_feed, text_proj,
    query_self, key_self, value_self, out_self, query_cross, key_cross, value_cross, out_cross, up_proj, down_proj,
):
    given = types.SimpleNamespace(
        tokens=tokens, caption=caption, cotangent=cotangent, text_proj=text_proj,
        query_self=query_self, key_self=key_self, value_self=value_self, out_self=out_self,
        query_cross=query_cross, key_cross=key_cross, value_cross=value_cross, out_cross=out_cross,
        up_proj=up_proj, down_proj=down_proj, marks=token_mask[:, :, None].astype(F32),
        gains=[gain_self, gain_cross, gain_feed],
    )
    pairs = lax.axis_size(WIDE) // 2
    kept = forward_all(pairs, 1, given)
    grads, d_words, d_tokens, layer_out, gains = backward_all(pairs, 2, given, kept)
    inner = query_self.shape[1]
    blk = query_self.shape[0] // (2 * pairs)
    ff, text = up_proj.shape[1] // inner, caption.shape[2] // inner
    places = [(10, c * inner, 0, True) for c in range(ff)]
    places += [(9, 0, c * inner, False) for c in range(ff)]
    places += [(8, 0, 0, True), (6, 0, 0, False), (7, 0, 0, False), (5, 0, 0, False)]
    places += [(0, c * inner, 0, True) for c in range(text)]
    places += [(4, 0, 0, True), (1, 0, 0, False), (2, 0, 0, False), (3, 0, 0, False)]
    shapes = [(text * inner, blk)] + [(blk, inner)] * 3 + [(inner, blk)] + [(blk, inner)] * 3 + [(inner, blk)]
    shapes += [(blk, ff * inner), (ff * inner, blk)]
    out = spread(grads, places, shapes, [layer_out, d_tokens, d_words], gains)
    sums, (layer_out, d_tokens, d_words, *gains) = out[: len(shapes)], out[len(shapes) :]
    return (layer_out, d_tokens, d_words.reshape(caption.shape), *gains, *sums)


def local(
    tokens,
    caption,
    token_mask,
    cotangent,
    gain_self,
    gain_cross,
    gain_feed,
    text_proj,
    query_self,
    key_self,
    value_self,
    out_self,
    query_cross,
    key_cross,
    value_cross,
    out_cross,
    up_proj,
    down_proj,
):
    given = (tokens, caption, token_mask, cotangent, gain_self, gain_cross, gain_feed, text_proj, query_self, key_self, value_self, out_self, query_cross, key_cross, value_cross, out_cross, up_proj, down_proj)
    if lax.axis_size(WIDE) != 8 or lax.axis_size(NARROW) != 4:
        return by_collectives(*given)
    return by_kernels(*given)


def solution(mesh):
    in_specs = (
        P(WIDE, NARROW, None),
        P(WIDE, None, NARROW),
        P(WIDE, NARROW),
        P(WIDE, NARROW, None),
        P(),
        P(),
        P(),
        P(NARROW, None),
        P(None, NARROW),
        P(None, NARROW),
        P(None, NARROW),
        P(NARROW, None),
        P(None, NARROW),
        P(None, NARROW),
        P(None, NARROW),
        P(NARROW, None),
        P(None, NARROW),
        P(NARROW, None),
    )
    out_specs = (
        P(WIDE, NARROW, None),
        P(WIDE, NARROW, None),
        P(WIDE, None, NARROW),
        P(),
        P(),
        P(),
        P(NARROW, WIDE),
        P(WIDE, NARROW),
        P(WIDE, NARROW),
        P(WIDE, NARROW),
        P(NARROW, WIDE),
        P(WIDE, NARROW),
        P(WIDE, NARROW),
        P(WIDE, NARROW),
        P(NARROW, WIDE),
        P(WIDE, NARROW),
        P(NARROW, WIDE),
    )
    return jax.shard_map(local, mesh=mesh, in_specs=in_specs, out_specs=out_specs, check_vma=False)
```
